32 devices in a mesh: ctx: 4 (over z), row: 2 (over x), col: 4 (over y, core).
Axes of the slice: x: 2, y: 2, z: 4, core: 2. Of those that a mesh axis runs over, the one named last changes fastest.
Arguments:
- tokens: bfloat16 [1024, 8192], P('ctx', 'row'), may hold values from -6 to 6
- proj_x: bfloat16 [8192, 8192], P('row', 'col'), may hold values from -0.09375 to 0.09375
- proj_z: bfloat16 [8192, 8192], P('row', 'col'), may hold values from -0.0625 to 0.0625
- proj_bc: bfloat16 [8192, 256], P('row'), may hold values from -0.015625 to 0.015625
- proj_dt: bfloat16 [8192, 128], P('row', 'col'), may hold values from -0.0625 to 0.0625
- dt_bias: float32 [128], P('col'), may hold values from -1.5 to 0.5
- decay_rate: float32 [128], P('col'), may hold values from 0.00048828125 to 0.2
- skip_gain: float32 [128], P('col'), may hold values from 0.5 to 1.5
- conv_x: float32 [8192, 4], P('col'), may hold values from -3 to 3
- conv_bc: float32 [256, 4], replicated, may hold values from -3 to 3
- norm_gain: float32 [8192], P('col'), may hold values from 0.1 to 1.9
- proj_out: bfloat16 [8192, 8192], P('col', 'row'), may hold values from -0.09375 to 0.09375
Outputs:
- layer_out: bfloat16 [1024, 8192], P('ctx', ('row', 'col'))
The draws below stay inside these ranges and needn't reach their ends.
All inputs are finite; a program needn't handle non-finite values.
Results may differ from the reference program's by a relative error of at most 0.03.
Values may be sent and summed in bfloat16 or wider, within the bound.
No kernel may reach another device: no remote copies, remote signals or barrier semaphores. Data moves between devices by JAX's collectives and lax.ppermute only.
A program may use at most 128 MiB of HBM per device.

```python
import math
import jax
import jax.numpy as jnp
from jax import lax

D = 8192
H = 128
P_SIZE = 64
N = 128
Q = 256
K = 4
INNER = 8192
TOKENS = 1024
N_ROW = 2


def raised(entries, key, source, target, parts, factor):
    owner, partner = [(jnp.arange(entries.shape[dim]) // (entries.shape[dim] // parts)).reshape([-1 if axis == dim else 1 for axis in range(entries.ndim)]) for dim in (source, target)]
    chosen = jax.random.permutation(key, parts)[partner]
    strong = (owner == chosen) | (owner == (partner + parts // 2) % parts)
    return jnp.where(strong, factor * entries, entries)


def level_of(key, dims, pieces, least, largest):
    gain, own = 1.0, jax.random.fold_in(key, 6)
    for position, blocks in pieces:
        steps = jnp.exp(jax.random.uniform(jax.random.fold_in(own, position), (blocks,), jnp.float32, least / len(pieces), largest / len(pieces)))
        gain = gain * jnp.repeat(steps, dims[position] // blocks).reshape([-1 if axis == position else 1 for axis in range(len(dims))])
    return gain


def scatter_about(own_key, dims, scale, reach, cuts=(), kind=jnp.bfloat16):
    loudness = level_of(own_key, dims, cuts, -0.22, 0.18) if cuts else 1.0
    result = jax.random.normal(own_key, dims, jnp.float32) * scale * loudness
    return jnp.minimum(jnp.maximum(result, -reach), reach).astype(kind)


def bell_draw_with(key, dims, spread, limit, cuts, heavy, dtype=jnp.bfloat16):
    values = spread * jax.random.normal(key, dims, jnp.float32)
    if cuts:
        values = values * level_of(key, dims, cuts, -0.22, 0.18)
    return jnp.clip(raised(values, jax.random.fold_in(key, 3), *heavy), -limit, limit).astype(dtype)


def setup_inputs(seed: int = 0) -> dict:
    key_of = jax.random.split(jax.random.key(seed), 13)
    return {
        "tokens": scatter_about(key_of[0], (TOKENS, D), 1.0, 6.0, ((0, 4), (1, 2))),
        "proj_x": bell_draw_with(key_of[1], (D, INNER), D ** -0.5, 0.09375, ((0, 2), (1, 4)), (0, 1, 4, 2.0)),
        "proj_z": scatter_about(key_of[2], (D, INNER), D ** -0.5, 0.0625, ((0, 2), (1, 4))),
        "proj_bc": scatter_about(key_of[3], (D, 2 * N), (0.25 * D ** -0.5), 0.015625, ((0, 2),)),
        "proj_dt": scatter_about(key_of[4], (D, H), D ** -0.5, 0.0625, ((0, 2), (1, 4))),
        "dt_bias": jnp.clip(-1.5 + 2.0 * jax.random.uniform(key_of[5], (H,), jnp.float32) ** level_of(key_of[5], (H,), ((0, 4),), -0.2, 0.2), -1.5, 0.5),
        "decay_rate": jnp.clip(jnp.exp(math.log(0.2) - 6.015181 * jax.random.uniform(key_of[6], (H,), jnp.float32) ** level_of(key_of[6], (H,), ((0, 4),), -0.2, 0.2)), 0.00048828125, 0.2),
        "skip_gain": jnp.clip(0.5 + 1.0 * jax.random.uniform(key_of[7], (H,), jnp.float32) ** level_of(key_of[7], (H,), ((0, 4),), -0.2, 0.2), 0.5, 1.5),
        "conv_x": scatter_about(key_of[8], (INNER, K), K ** -0.5, 3.0, ((0, 4),), jnp.float32),
        "conv_bc": scatter_about(key_of[9], (2 * N, K), K ** -0.5, 3.0, (), jnp.float32),
        "norm_gain": jnp.clip(1.0 + 0.18 * jax.random.normal(key_of[10], (INNER,), jnp.float32), 0.1, 1.9),
        "proj_out": bell_draw_with(key_of[11], (INNER, D), INNER ** -0.5, 0.09375, ((0, 4), (1, 2)), (0, 1, 4, 2.0)),
    }


highest_mode = lax.Precision.HIGHEST

def blocked_product(tokens, weight):
    block_width = tokens.shape[1] // N_ROW
    running = jnp.zeros((tokens.shape[0], weight.shape[1]), jnp.float32)
    for block_index in range(N_ROW):
        low_edge = block_index * block_width
        block_sum = jnp.dot(tokens[:, low_edge:low_edge + block_width], weight[low_edge:low_edge + block_width], preferred_element_type=jnp.float32)
        rounded = lax.optimization_barrier(block_sum.astype(jnp.bfloat16))
        running = running + rounded.astype(jnp.float32)
    return running.astype(jnp.bfloat16)

def causal_conv(values, kernel):
    tap_count = kernel.shape[1]
    padded = jnp.pad(values.astype(jnp.float32), ((tap_count - 1, 0), (0, 0)))
    running = jnp.zeros(values.shape, jnp.float32)
    for tap_index in range(tap_count):
        running = running + kernel[:, tap_index] * padded[tap_index:tap_index + values.shape[0]]
    return jax.nn.silu(running)

def head_scan(inputs_now, b_full, c_full):
    x_head, dt_head, decay_now, skip_now = inputs_now
    seq_len = x_head.shape[0]
    group_count = seq_len // Q
    log_decay = (-decay_now * dt_head).reshape(group_count, Q)
    cum_decay = jnp.cumsum(log_decay, axis=1)
    x_scaled = (x_head * dt_head[:, None]).reshape(group_count, Q, -1)
    b_blocks = b_full.reshape(group_count, Q, -1)
    c_blocks = c_full.reshape(group_count, Q, -1)
    scores = jnp.einsum('cin,cjn->cij', c_blocks, b_blocks, precision=highest_mode)
    lower_mask = jnp.arange(Q)[:, None] >= jnp.arange(Q)[None, :]
    log_gap = cum_decay[:, :, None] - cum_decay[:, None, :]
    weights = jnp.where(lower_mask, jnp.exp(jnp.where(lower_mask, log_gap, 0.0)), 0.0)
    inner_out = jnp.einsum('cij,cjp->cip', scores * weights, x_scaled, precision=highest_mode)
    tail_weight = jnp.exp(cum_decay[:, -1:] - cum_decay)
    group_states = jnp.einsum('cj,cjp,cjn->cpn', tail_weight, x_scaled, b_blocks, precision=highest_mode)

    def group_step(carried, step_inputs):
        group_log, group_state = step_inputs
        return (jnp.exp(group_log) * carried + group_state, carried)
    start_state = jnp.zeros(group_states.shape[1:], jnp.float32)
    final_state, entering = lax.scan(group_step, start_state, (cum_decay[:, -1], group_states))
    outer_out = jnp.exp(cum_decay)[:, :, None] * jnp.einsum('cin,cpn->cip', c_blocks, entering, precision=highest_mode)
    return (inner_out + outer_out).reshape(seq_len, -1) + skip_now * x_head

def reference(tokens, proj_x, proj_z, proj_bc, proj_dt, dt_bias, decay_rate, skip_gain, conv_x, conv_bc, norm_gain, proj_out):
    x_in = blocked_product(tokens, proj_x)
    z_in = blocked_product(tokens, proj_z)
    bc_in = blocked_product(tokens, proj_bc)
    dt_in = blocked_product(tokens, proj_dt)
    x_conv = causal_conv(x_in, conv_x)
    bc_conv = causal_conv(bc_in, conv_bc)
    b_full = bc_conv[:, :N]
    c_full = bc_conv[:, N:]
    dt_full = jax.nn.softplus(dt_in.astype(jnp.float32) + dt_bias)
    seq_len = tokens.shape[0]
    x_heads = x_conv.reshape(seq_len, H, P_SIZE).transpose(1, 0, 2)
    ssm_heads = lax.map(lambda inputs_now: head_scan(inputs_now, b_full, c_full), (x_heads, dt_full.T, decay_rate, skip_gain))
    ssm_out = ssm_heads.transpose(1, 0, 2)
    gated = ssm_out * jax.nn.silu(z_in.astype(jnp.float32)).reshape(seq_len, H, P_SIZE)
    inv_rms = lax.rsqrt(lax.optimization_barrier(jnp.mean(gated * gated, axis=2, keepdims=True)) + 1e-05)
    normed = (gated * inv_rms * norm_gain.reshape(H, P_SIZE)).reshape(seq_len, H * P_SIZE).astype(jnp.bfloat16)
    return jnp.dot(normed, proj_out, preferred_element_type=jnp.float32).astype(jnp.bfloat16)
```

```python
import functools

import jax
import jax.numpy as jnp
from jax import lax
from jax.experimental import pallas as pl
from jax.experimental.pallas import tpu as pltpu
from jax.sharding import PartitionSpec as P

Q = 256
EPS = 1e-05
HALO = 16
VMEM_LIMIT = 48 * 1024 * 1024
f32 = jnp.float32
bf16 = jnp.bfloat16
highest_mode = lax.Precision.HIGHEST


def mm(a, b):
    return jnp.dot(a, b, preferred_element_type=f32)


def mm_tn(a, b):
    return lax.dot_general(a, b, (((0,), (0,)), ((), ())), preferred_element_type=f32)


def mm_nt(a, b):
    return lax.dot_general(a, b, (((1,), (1,)), ((), ())), preferred_element_type=f32)


def silu(v):
    return v / (1.0 + jnp.exp(-v))


def softplus(v):
    return jnp.maximum(v, 0.0) + jnp.log(1.0 + jnp.exp(-jnp.abs(v)))


def total(mine, theirs):
    return (mine.astype(f32) + theirs.astype(f32)).astype(bf16).astype(f32)


def spread(per_head, head_dim):
    heads = per_head.shape[0]
    high = per_head.astype(bf16)
    low = (per_head - high.astype(f32)).astype(bf16)
    parts = jnp.concatenate([high.astype(f32), low.astype(f32)], axis=0).astype(bf16)
    shape = (2 * heads, heads * head_dim)
    row = lax.broadcasted_iota(jnp.int32, shape, 0) % heads
    col = lax.broadcasted_iota(jnp.int32, shape, 1) // head_dim
    return mm_tn(parts, jnp.where(row == col, 1.0, 0.0).astype(bf16))


def pick(row_vector, first, count):
    shape = (count, row_vector.shape[1])
    lane = lax.broadcasted_iota(jnp.int32, shape, 1)
    sub = lax.broadcasted_iota(jnp.int32, shape, 0)
    return jnp.sum(jnp.where(lane == sub + first, row_vector, 0.0), axis=1, keepdims=True)


def conv(ext_ref, taps, toks):
    count = taps.shape[0]
    running = None
    for tap in range(count):
        term = taps[tap : tap + 1, :] * ext_ref[pl.ds(HALO - count + 1 + tap, toks), :]
        running = term if running is None else running + term
    return running


def prefix(messages, here, state_dim):
    def parts(message):
        return message[:state_dim].astype(f32), message[state_dim : state_dim + 1].astype(f32)

    state, decay = parts(messages[0])
    enter = jnp.zeros_like(state)
    reach = jnp.ones_like(decay)
    for step, message in enumerate(messages[1:]):
        their_state, their_decay = parts(message)
        later = ((here >> step) & 1) == 1
        enter = jnp.where(later, enter + reach * their_state, enter)
        reach = jnp.where(later, reach * their_decay, reach)
        state = jnp.where(later, decay * their_state + state, their_decay * state + their_state)
        decay = decay * their_decay
    return enter, state, decay


def first_kernel(where, tok, w_x, w_bc, w_dt, msg, acc_x, acc_bc, acc_dt):
    step = pl.program_id(0)
    toks, lanes = acc_bc.shape

    @pl.when(step == 0)
    def _():
        acc_x[...] = jnp.zeros_like(acc_x)
        acc_bc[...] = jnp.zeros_like(acc_bc)
        acc_dt[...] = jnp.zeros_like(acc_dt)

    now = tok[...]
    acc_x[...] += mm(now, w_x[...])
    acc_bc[...] += mm(now, w_bc[...])
    acc_dt[...] += mm_nt(w_dt[...], now)

    @pl.when(step == pl.num_programs(0) - 1)
    def _():
        heads = acc_dt.shape[0]
        msg[:toks, :] = acc_bc[...].astype(bf16)
        msg[toks : toks + heads, :] = acc_dt[...].astype(bf16)
        for j in range(acc_x.shape[1] // lanes):
            low = toks + heads + j * toks
            msg[low : low + toks, :] = acc_x[:, j * lanes : (j + 1) * lanes].astype(bf16)


def product_kernel(where, tok, weight, *refs, edges):
    step = pl.program_id(0)
    out, acc = refs[edges or 0], refs[-1]
    toks = tok.shape[0]
    lanes = out.shape[1]

    @pl.when(step == 0)
    def _():
        acc[...] = jnp.zeros_like(acc)

    acc[...] += mm(tok[...], weight[...])

    @pl.when(step == pl.num_programs(0) - 1)
    def _():
        for j in range(acc.shape[1] // lanes):
            out[j * toks : (j + 1) * toks, :] = acc[:, j * lanes : (j + 1) * lanes].astype(bf16)
        if edges is not None:
            edge = refs[edges + 1]
            for j in range(edges):
                edge[j * HALO : (j + 1) * HALO, :] = refs[j][...]
            for j in range(acc.shape[1] // lanes):
                low = (edges + j) * HALO
                edge[low : low + HALO, :] = acc[
                    toks - HALO :, j * lanes : (j + 1) * lanes
                ].astype(bf16)


def state_kernel(
    where, *refs, first, chunk, chunks, head_dim, state_dim, toks, lanes
):
    refs = list(refs)
    if first:
        bc_mine, bc_theirs = refs.pop(0), refs.pop(0)
    else:
        bc_in = refs.pop(0)
    dt_mine, dt_theirs, x_mine, x_theirs, edge_a, edge_b, taps_x, taps_bc, bias, decay = refs[:10]
    refs = refs[10:]
    if first:
        bc_out, scores = refs.pop(0), refs.pop(0)
    msg, scaled, conv_out, cum_out, cum_t_out, ext = refs
    row, here = where[0], where[2]
    blocks = x_mine.shape[0] // toks
    heads = blocks * lanes // head_dim
    local_heads = heads * chunks
    inside = jnp.where(here > 0, 1.0, 0.0)

    def halo(block):
        low = block * HALO
        return total(edge_a[low : low + HALO, :], edge_b[low : low + HALO, :]) * inside

    if first:
        ext[:HALO, :] = halo(0)
        ext[HALO:, :] = total(bc_mine[...], bc_theirs[...])
        bc_now = silu(conv(ext, taps_bc[...], toks)).astype(bf16)
        bc_out[...] = bc_now
        b_now = bc_now[:, :state_dim]
        products = mm_nt(bc_now[:, state_dim:], b_now)
        shape = (toks, toks)
        lower = lax.broadcasted_iota(jnp.int32, shape, 0) >= lax.broadcasted_iota(jnp.int32, shape, 1)
        scores[...] = jnp.where(lower, products, 0.0)
    else:
        b_now = bc_in[:, :state_dim]

    low = pl.multiple_of(row * local_heads, local_heads)
    dt_sum = total(dt_mine[pl.ds(low, local_heads), :], dt_theirs[pl.ds(low, local_heads), :])
    dt_sum = dt_sum[chunk * heads : (chunk + 1) * heads]
    first_head = row * local_heads + chunk * heads
    dt_now = softplus(dt_sum + pick(bias[...], first_head, heads))
    log_decay = -pick(decay[...], first_head, heads) * dt_now
    shape = (toks, toks)
    upper = lax.broadcasted_iota(jnp.int32, shape, 0) <= lax.broadcasted_iota(jnp.int32, shape, 1)
    cum = lax.dot_general(
        log_decay,
        jnp.where(upper, 1.0, 0.0),
        (((1,), (0,)), ((), ())),
        precision=highest_mode,
        preferred_element_type=f32,
    )
    last = cum[:, toks - 1 : toks]
    cum_out[...] = cum
    cum_t_out[...] = cum.T
    dt_wide = spread(dt_now, head_dim)
    tail_wide = spread(dt_now * jnp.exp(last - cum), head_dim)
    through = spread(jnp.exp(jnp.broadcast_to(last, (heads, HALO))), head_dim)
    rows = state_dim + HALO
    for j in range(blocks):
        ext[:HALO, :] = halo(1 + chunk * blocks + j)
        ext[HALO:, :] = total(
            x_mine[j * toks : (j + 1) * toks, :], x_theirs[j * toks : (j + 1) * toks, :]
        )
        cols = slice(j * lanes, (j + 1) * lanes)
        x_now = silu(conv(ext, taps_x[:, cols], toks))
        conv_out[:, cols] = x_now.astype(bf16)
        scaled[:, cols] = (x_now * dt_wide[:, cols]).astype(bf16)
        state = mm_tn(b_now, (x_now * tail_wide[:, cols]).astype(bf16))
        msg[j * rows : j * rows + state_dim, :] = state.astype(bf16)
        msg[j * rows + state_dim : (j + 1) * rows, :] = through[:, cols].astype(bf16)


def combine_kernel(where, *refs, state_dim, lanes):
    *messages, out = refs
    rows = state_dim + HALO
    for j in range(out.shape[0] // rows):
        now = [m[j * rows : (j + 1) * rows, :] for m in messages]
        _, state, decay = prefix(now, where[2], state_dim)
        out[j * rows : j * rows + state_dim, :] = state.astype(bf16)
        out[j * rows + state_dim : (j + 1) * rows, :] = jnp.broadcast_to(decay, (HALO, lanes)).astype(bf16)


def inner_kernel(where, scores, scaled, conv_out, cum, cum_t, skip, out, *, head_dim, first_of, local_heads):
    toks, channels = scaled.shape
    pair = 2 * head_dim
    half = toks // 2
    heads = channels // head_dim
    skip_now = pick(skip[...], where[0] * local_heads + first_of, heads)
    skip_wide = spread(jnp.broadcast_to(skip_now, (heads, HALO)), head_dim)[:1, :]
    left = lax.broadcasted_iota(jnp.int32, (toks, pair), 1) < head_dim
    zero = jnp.zeros((toks, pair), bf16)
    for p in range(heads // 2):
        cols = slice(p * pair, (p + 1) * pair)
        x_pair = scaled[:, cols]
        top = None
        for side in range(2):
            h = 2 * p + side
            x_now = jnp.where(left, x_pair, zero) if side == 0 else jnp.where(left, zero, x_pair)
            gap_top = jnp.minimum(cum_t[:half, h : h + 1] - cum[h : h + 1, :half], 0.0)
            gap_low = jnp.minimum(cum_t[half:, h : h + 1] - cum[h : h + 1, :], 0.0)
            w_top = (jnp.exp(gap_top) * scores[:half, :half]).astype(bf16)
            w_low = (jnp.exp(gap_low) * scores[half:, :]).astype(bf16)
            part_top = mm(w_top, x_now[:half])
            part_low = mm(w_low, x_now)
            top = part_top if top is None else top + part_top
            low = part_low if side == 0 else low + part_low
        skips = skip_wide[:, cols]
        out[:half, cols] = top + skips * conv_out[:half, cols].astype(f32)
        out[half:, cols] = low + skips * conv_out[half:, cols].astype(f32)


def gate_kernel(where, inner, bc, cum, z_mine, z_theirs, gain, *refs, head_dim, state_dim, lanes):
    *messages, out = refs
    toks = inner.shape[0]
    rows = state_dim + HALO
    grown = spread(jnp.exp(cum[...]), head_dim)
    c_now = bc[:, state_dim:]
    wide = 2 * head_dim
    shape = (wide, wide)
    same = (lax.broadcasted_iota(jnp.int32, shape, 0) // head_dim) == (
        lax.broadcasted_iota(jnp.int32, shape, 1) // head_dim
    )
    mean_of = jnp.where(same, 1.0 / head_dim, 0.0).astype(bf16)
    for j in range(inner.shape[1] // lanes):
        now = [m[j * rows : (j + 1) * rows, :] for m in messages]
        enter, _, _ = prefix(now, where[2], state_dim)
        cols = slice(j * lanes, (j + 1) * lanes)
        scanned = inner[:, cols] + grown[:, cols] * mm(c_now, enter.astype(bf16))
        z_now = total(z_mine[j * toks : (j + 1) * toks, :], z_theirs[j * toks : (j + 1) * toks, :])
        gated = scanned * silu(z_now)
        square = gated * gated
        for i in range(lanes // wide):
            part = square[:, i * wide : (i + 1) * wide]
            high = part.astype(bf16)
            rest = (part - high.astype(f32)).astype(bf16)
            mean = mm(high, mean_of) + mm(rest, mean_of)
            low = j * lanes + i * wide
            out[j * toks : (j + 1) * toks, i * wide : (i + 1) * wide] = (
                gated[:, i * wide : (i + 1) * wide]
                * lax.rsqrt(mean + EPS)
                * gain[:, low : low + wide]
            ).astype(bf16)


def out_kernel(where, weight, *refs, half):
    *normed, send, keep = refs
    step = pl.program_id(0)
    lanes = normed[0].shape[1]
    toks = send.shape[0]
    width = weight.shape[1]
    per_send = send.shape[1] // width
    acc = None
    for side in range(2):
        low = jnp.where(side == 0, where[0], 1 - where[0]) * half
        at = 0
        for chunk in normed[side * (len(normed) // 2) : (side + 1) * (len(normed) // 2)]:
            for j in range(chunk.shape[0] // toks):
                rows = pl.ds(pl.multiple_of(low + at, lanes), lanes)
                part = mm(chunk[j * toks : (j + 1) * toks, :], weight[rows, :])
                acc = part if acc is None else acc + part
                at += lanes
    done = acc.astype(bf16)

    @pl.when(step < per_send)
    def _():
        send[:, pl.ds(pl.multiple_of(step * width, width), width)] = done

    @pl.when(step >= per_send)
    def _():
        keep[:, pl.ds(pl.multiple_of((step - per_send) * width, width), width)] = done


def add_kernel(a, b, out):
    out[...] = (a[...].astype(f32) + b[...].astype(f32)).astype(bf16)


def sds(*shape, dtype=bf16):
    return jax.ShapeDtypeStruct(shape, dtype)


def cost(flops, size):
    return pl.CostEstimate(flops=int(flops), bytes_accessed=int(size), transcendentals=0)


def call(kernel, where, args, specs, outs, out_specs, scratch=(), grid=(1,), flops=0, size=0, name=None):
    return pl.pallas_call(
        kernel,
        grid_spec=pltpu.PrefetchScalarGridSpec(
            num_scalar_prefetch=1,
            grid=grid,
            in_specs=specs,
            out_specs=out_specs,
            scratch_shapes=list(scratch),
        ),
        out_shape=outs,
        compiler_params=pltpu.CompilerParams(
            dimension_semantics=("arbitrary",) * len(grid), vmem_limit_bytes=VMEM_LIMIT
        ),
        cost_estimate=cost(flops, size),
        name=name,
    )(where, *args)


def whole(shape):
    return pl.BlockSpec(shape, lambda i, w: (0,) * len(shape))


def at(shape, index):
    return pl.BlockSpec(shape, index)


def swapped(shard, axis, by):
    devices = lax.axis_size(axis)
    return lax.ppermute(shard, axis, [(i, i ^ by) for i in range(devices)])


def fast(
    tokens, proj_x, proj_z, proj_bc, proj_dt, dt_bias, decay_rate, skip_gain,
    conv_x, conv_bc, norm_gain, proj_out,
):
    toks, depth = tokens.shape
    heads = proj_dt.shape[1]
    head_dim = proj_x.shape[1] // heads
    lanes = proj_bc.shape[1]
    state_dim = lanes // 2
    taps = conv_bc.shape[1]
    local_heads = heads // 2
    half = local_heads * head_dim
    chunks = 2
    width = half // chunks
    blocks = width // lanes
    chunk_heads = local_heads // chunks
    out_cols = proj_out.shape[1]
    ctx_size = lax.axis_size("ctx")
    row, col, ctx = lax.axis_index("row"), lax.axis_index("col"), lax.axis_index("ctx")
    where = jnp.stack([row, col, ctx]).astype(jnp.int32)
    conv_x_t, conv_bc_t, proj_dt_t = conv_x.T, conv_bc.T, proj_dt.T
    bias, decay, skip, gain = (v[None] for v in (dt_bias, decay_rate, skip_gain, norm_gain))

    kb = depth // 8
    tok_spec = at((toks, kb), lambda k, w: (0, k))
    msg_rows = toks + heads + blocks * toks
    msg_first = call(
        first_kernel,
        where,
        (tokens, proj_x, proj_bc, proj_dt_t),
        [
            tok_spec,
            at((kb, width), lambda k, w: (k, (1 - w[0]) * chunks)),
            at((kb, lanes), lambda k, w: (k, 0)),
            at((heads, kb), lambda k, w: (0, k)),
        ],
        sds(msg_rows, lanes),
        whole((msg_rows, lanes)),
        [pltpu.VMEM((toks, width), f32), pltpu.VMEM((toks, lanes), f32), pltpu.VMEM((heads, toks), f32)],
        grid=(depth // kb,),
        flops=2 * toks * depth * (width + lanes + heads),
        size=2 * depth * (toks + width + lanes + heads),
        name="first",
    )
    first_got = swapped(msg_first, "row", 1)

    def product(weight, n_cols, col_of, edge_blocks, name):
        edge_args = [msg_first] * len(edge_blocks)
        edge_specs = [at((HALO, lanes), lambda k, w, e=e: (e, 0)) for e in edge_blocks]
        out_rows = n_cols // lanes * toks
        outs, out_specs = [sds(out_rows, lanes)], [whole((out_rows, lanes))]
        edges = None
        if edge_blocks:
            edges = len(edge_blocks)
            edge_rows = (edges + n_cols // lanes) * HALO
            outs.append(sds(edge_rows, lanes))
            out_specs.append(whole((edge_rows, lanes)))
        return call(
            functools.partial(product_kernel, edges=edges),
            where,
            (tokens, weight, *edge_args),
            [tok_spec, at((kb, n_cols), lambda k, w: (k, col_of(w))), *edge_specs],
            outs,
            out_specs,
            [pltpu.VMEM((toks, n_cols), f32)],
            grid=(depth // kb,),
            flops=2 * toks * depth * n_cols,
            size=2 * depth * (toks + n_cols),
            name=name,
        )

    def last_rows(low):
        return (low + toks) // HALO - 1

    bc_edge = last_rows(0)
    x_edges = [last_rows(toks + heads + j * toks) for j in range(blocks)]
    msg_second, edge_other = product(
        proj_x, width, lambda w: (1 - w[0]) * chunks + 1, [bc_edge, *x_edges], "x_other"
    )
    second_got = swapped(msg_second, "row", 1)
    down = [(i, (i + 1) % ctx_size) for i in range(ctx_size)]
    edge_a = lax.ppermute(
        edge_other, ("ctx", "row"), [(2 * i + s, 2 * j + 1 - s) for i, j in down for s in range(2)]
    )
    x_mine, edge_own = product(proj_x, half, lambda w: w[0], [bc_edge], "x_own")
    edge_b = lax.ppermute(edge_own, "ctx", down)
    z_send = [
        product(proj_z, width, lambda w, c=c: (1 - w[0]) * chunks + c, [], "z_other")[0]
        for c in range(chunks)
    ]
    z_got = [swapped(z, "row", 1) for z in z_send]
    z_mine = product(proj_z, half, lambda w: w[0], [], "z_own")[0]

    edge_shape = edge_a.shape
    rows = state_dim + HALO
    kernel_sizes = dict(head_dim=head_dim, state_dim=state_dim, lanes=lanes)
    states, scans = [], []
    bc_now = scores = None
    for c in range(chunks):
        dt_at = at((heads, lanes), lambda k, w: (toks // heads, 0))
        args, specs = [], []
        outs, out_specs = [], []
        if c == 0:
            args += [msg_first, first_got]
            specs += [at((toks, lanes), lambda k, w: (0, 0))] * 2
            outs += [sds(toks, lanes), sds(toks, toks, dtype=f32)]
            out_specs += [whole((toks, lanes)), whole((toks, toks))]
        else:
            args += [bc_now]
            specs += [whole((toks, lanes))]
        x_theirs = first_got[toks + heads :] if c == 0 else second_got
        args += [msg_first, first_got, x_mine, x_theirs, edge_a, edge_b, conv_x_t, conv_bc_t, bias, decay]
        specs += [
            dt_at,
            dt_at,
            at((blocks * toks, lanes), lambda k, w, c=c: (c, 0)),
            whole((blocks * toks, lanes)),
            whole(edge_shape),
            whole(edge_shape),
            at((taps, width), lambda k, w, c=c: (0, w[0] * chunks + c)),
            whole((taps, lanes)),
            whole((1, heads)),
            whole((1, heads)),
        ]
        outs += [
            sds(blocks * rows, lanes),
            sds(toks, width),
            sds(toks, width),
            sds(chunk_heads, toks, dtype=f32),
            sds(toks, chunk_heads, dtype=f32),
        ]
        out_specs += [whole(o.shape) for o in outs[len(out_specs) :]]
        got = call(
            functools.partial(
                state_kernel, first=c == 0, chunk=c, chunks=chunks, toks=toks, **kernel_sizes
            ),
            where, args, specs, outs, out_specs,
            [pltpu.VMEM((HALO + toks, lanes), f32)],
            flops=2 * toks * width * (state_dim + 64), size=2 * toks * width * 6, name="state",
        )
        if c == 0:
            bc_now, scores = got[:2]
            got = got[2:]
        states.append(got[0])
        scans.append(got[1:])

    messages = []
    for c in range(chunks):
        heard = [states[c]]
        send = states[c]
        by = 1
        while by < ctx_size:
            if by > 1:
                send = call(
                    functools.partial(combine_kernel, state_dim=state_dim, lanes=lanes),
                    where, heard, [whole(send.shape)] * len(heard), sds(*send.shape), whole(send.shape),
                    flops=send.size * 6, size=send.size * 6, name="combine",
                )
            heard.append(swapped(send, "ctx", by))
            by *= 2
        messages.append(heard)

    inners = []
    for c in range(chunks):
        scaled, conv_out, cum, cum_t = scans[c]
        args = (scores, scaled, conv_out, cum, cum_t, skip)
        inners.append(
            call(
                functools.partial(
                    inner_kernel, head_dim=head_dim, first_of=c * chunk_heads, local_heads=local_heads
                ),
                where, args, [whole(a.shape) for a in args], sds(toks, width, dtype=f32),
                whole((toks, width)), flops=chunk_heads * 2 * toks * toks * 2 * head_dim,
                size=2 * toks * width * 5, name="inner",
            )
        )

    normed, normed_got = [], []
    for c in range(chunks):
        cum = scans[c][2]
        args = (inners[c], bc_now, cum, z_mine, z_got[c], gain, *messages[c])
        now = call(
            functools.partial(gate_kernel, **kernel_sizes),
            where,
            args,
            [
                whole((toks, width)),
                whole((toks, lanes)),
                whole(cum.shape),
                at((blocks * toks, lanes), lambda k, w, c=c: (c, 0)),
                whole((blocks * toks, lanes)),
                at((1, width), lambda k, w, c=c: (0, w[0] * chunks + c)),
                *[whole(m.shape) for m in messages[c]],
            ],
            sds(blocks * toks, lanes),
            whole((blocks * toks, lanes)),
            flops=2 * toks * width * (state_dim + 4 * head_dim), size=2 * toks * width * 6, name="gate",
        )
        normed.append(now)
        normed_got.append(swapped(now, "row", 1))

    piece = out_cols // lax.axis_size("col")
    tile = piece // 2
    per = piece // tile

    def out_half(pair_of, name):
        def weight_at(n, w):
            core = jnp.where(n < per, 1 - w[1] % 2, w[1] % 2)
            return (0, (pair_of(w) * 2 + core) * per + n % per)

        args = (proj_out, *normed, *normed_got)
        return call(
            functools.partial(out_kernel, half=half),
            where,
            args,
            [at((proj_out.shape[0], tile), weight_at), *[whole(a.shape) for a in args[1:]]],
            [sds(toks, piece)] * 2,
            [whole((toks, piece))] * 2,
            grid=(2 * per,),
            flops=2 * toks * proj_out.shape[0] * 2 * piece,
            size=2 * proj_out.shape[0] * 2 * piece,
            name=name,
        )

    def added(a, b):
        return (a.astype(f32) + b.astype(f32)).astype(bf16)

    far_send, far_keep = out_half(lambda w: 1 - w[1] // 2, "out_far")
    far = added(far_keep, swapped(far_send, "col", 1))
    far_got = swapped(far, "col", 2)
    near_send, near_keep = out_half(lambda w: w[1] // 2, "out_near")
    near = near_keep.astype(f32) + swapped(near_send, "col", 1).astype(f32)
    return (near + far_got.astype(f32)).astype(bf16)


def shifted(shard, axis, by):
    devices = lax.axis_size(axis)
    pairs = [(i, i + by) for i in range(devices) if 0 <= i + by < devices]
    return lax.ppermute(shard, axis, pairs)


def general(
    tokens,
    proj_x,
    proj_z,
    proj_bc,
    proj_dt,
    dt_bias,
    decay_rate,
    skip_gain,
    conv_x,
    conv_bc,
    norm_gain,
    proj_out,
):
    tok_count = tokens.shape[0]
    col_heads = proj_dt.shape[1]
    head_dim = proj_x.shape[1] // col_heads
    state_dim = proj_bc.shape[1] // 2
    tap_count = conv_bc.shape[1]
    group_count = tok_count // Q
    bc_term = jnp.einsum("dc,td->ct", proj_bc, tokens, preferred_element_type=jnp.float32)
    local_heads = col_heads // lax.axis_size("row")
    first_head = lax.axis_index("row") * local_heads
    x_part = jnp.einsum("dc,td->ct", proj_x, tokens, preferred_element_type=jnp.float32).reshape(
        local_heads * lax.axis_size("row"), head_dim, tok_count
    )
    z_part = jnp.einsum("dc,td->ct", proj_z, tokens, preferred_element_type=jnp.float32).reshape(
        local_heads * lax.axis_size("row"), head_dim, tok_count
    )
    dt_part = jnp.einsum("dc,td->ct", proj_dt, tokens, preferred_element_type=jnp.float32).reshape(
        local_heads * lax.axis_size("row"), 1, tok_count
    )
    head_sum = lax.psum_scatter(
        jnp.concatenate([x_part, z_part, dt_part], axis=1).astype(jnp.bfloat16),
        "row",
        scatter_dimension=0,
        tiled=True,
    )
    bc_sum = lax.psum(bc_term.astype(jnp.bfloat16), "row")
    channels = local_heads * head_dim
    z_in = head_sum[:, head_dim : 2 * head_dim]
    dt_in = head_sum[:, 2 * head_dim]
    flat_in = jnp.concatenate([head_sum[:, :head_dim].reshape(channels, tok_count), bc_sum], axis=0)
    prior = shifted(flat_in[:, tok_count - tap_count + 1 :], "ctx", 1)
    padded = jnp.concatenate([prior, flat_in], axis=1).astype(jnp.float32)
    kernel = jnp.concatenate(
        [lax.dynamic_slice_in_dim(conv_x, first_head * head_dim, channels, 0), conv_bc], axis=0
    )
    running = jnp.zeros(flat_in.shape, jnp.float32)
    for tap_index in range(tap_count):
        running = (
            running
            + kernel[:, tap_index : tap_index + 1] * padded[:, tap_index : tap_index + tok_count]
        )
    conv_out = jax.nn.silu(running)
    x_conv = conv_out[:channels].reshape(local_heads, head_dim, tok_count)
    b_blocks = conv_out[channels : channels + state_dim].reshape(state_dim, group_count, Q)
    c_blocks = conv_out[channels + state_dim :].reshape(state_dim, group_count, Q)
    bias_now = lax.dynamic_slice_in_dim(dt_bias, first_head, local_heads, 0)
    decay_now = lax.dynamic_slice_in_dim(decay_rate, first_head, local_heads, 0)
    skip_now = lax.dynamic_slice_in_dim(skip_gain, first_head, local_heads, 0)
    gain_now = lax.dynamic_slice_in_dim(norm_gain, first_head * head_dim, channels, 0).reshape(
        local_heads, head_dim, 1
    )
    dt_full = jax.nn.softplus(dt_in.astype(jnp.float32) + bias_now[:, None])
    log_decay = -decay_now[:, None] * dt_full
    x_scaled = x_conv * dt_full[:, None, :]
    cum_decay = jnp.cumsum(log_decay.reshape(local_heads, group_count, Q), axis=2)
    x_blocks = x_scaled.reshape(local_heads, head_dim, group_count, Q)
    scores = jnp.einsum("nci,ncj->cij", c_blocks, b_blocks, precision=highest_mode)
    lower_mask = jnp.arange(Q)[:, None] >= jnp.arange(Q)[None, :]
    log_gap = cum_decay[:, :, :, None] - cum_decay[:, :, None, :]
    weights = jnp.where(lower_mask, jnp.exp(jnp.where(lower_mask, log_gap, 0.0)), 0.0)
    inner_out = jnp.einsum(
        "hcij,hpcj->hpci", scores[None] * weights, x_blocks, precision=highest_mode
    )
    tail_weight = jnp.exp(cum_decay[:, :, -1:] - cum_decay)
    group_states = jnp.einsum(
        "hcj,hpcj,ncj->chpn", tail_weight, x_blocks, b_blocks, precision=highest_mode
    )
    group_logs = cum_decay[:, :, -1].T

    def group_step(carried, step_inputs):
        group_log, group_state = step_inputs
        return (jnp.exp(group_log)[:, None, None] * carried + group_state, carried)

    start_state = jnp.zeros((local_heads, head_dim, state_dim), jnp.float32)
    final_state, local_enter = lax.scan(group_step, start_state, (group_logs, group_states))
    device_log = jnp.sum(group_logs, axis=0)
    before_logs = jnp.cumsum(group_logs, axis=0) - group_logs
    log_all, state_all = (
        lax.all_gather(device_log[None].astype(jnp.bfloat16), "ctx", axis=0, tiled=True).astype(
            jnp.float32
        ),
        lax.all_gather(final_state[None].astype(jnp.bfloat16), "ctx", axis=0, tiled=True).astype(
            jnp.float32
        ),
    )
    my_index = lax.axis_index("ctx")
    earlier_mask = (jnp.arange(log_all.shape[0], dtype=jnp.int32) < my_index)[:, None]
    log_prefix = jnp.cumsum(log_all, axis=0)
    up_to_me = jnp.sum(jnp.where(earlier_mask, log_all, 0.0), axis=0)
    reach_weight = jnp.where(
        earlier_mask, jnp.exp(jnp.where(earlier_mask, up_to_me - log_prefix, 0.0)), 0.0
    )
    device_state = jnp.einsum("jh,jhpn->hpn", reach_weight, state_all, precision=highest_mode)
    enter_state = jnp.exp(before_logs)[:, :, None, None] * device_state[None] + local_enter
    outer_out = jnp.exp(cum_decay)[:, None] * jnp.einsum(
        "nci,chpn->hpci", c_blocks, enter_state, precision=highest_mode
    )
    ssm_out = (inner_out + outer_out).reshape(local_heads, head_dim, tok_count) + skip_now[
        :, None, None
    ] * x_conv
    gated = ssm_out * jax.nn.silu(z_in.astype(jnp.float32))
    inv_rms = lax.rsqrt(jnp.mean(gated * gated, axis=1, keepdims=True) + 1e-05)
    normed = (gated * inv_rms * gain_now).astype(jnp.bfloat16)
    out_cols = proj_out.shape[1]
    piece = lax.all_gather(normed, "row", axis=0, tiled=True)
    piece_heads = piece.shape[0]
    rows_now = proj_out.reshape(piece_heads, head_dim, out_cols)
    col_partial = jnp.einsum("hpt,hpd->td", piece, rows_now, preferred_element_type=jnp.float32)
    return lax.psum_scatter(
        col_partial.astype(jnp.bfloat16), "col", scatter_dimension=1, tiled=True
    )


def local(*args):
    tokens, proj_x, _, proj_bc, proj_dt = args[:5]
    toks, heads, lanes = tokens.shape[0], proj_dt.shape[1], proj_bc.shape[1]
    ctx_size = lax.axis_size("ctx")
    fits = (
        lax.axis_size("row") == 2
        and lax.axis_size("col") == 4
        and ctx_size & (ctx_size - 1) == 0
        and toks == Q
        and lanes == toks
        and heads % 32 == 0
        and toks % heads == 0
        and proj_x.shape[1] % (4 * lanes) == 0
        and lanes % (2 * proj_x.shape[1] // heads) == 0
    )
    return fast(*args) if fits else general(*args)


def solution(mesh):
    in_specs = (
        P("ctx", "row"),
        P("row", "col"),
        P("row", "col"),
        P("row", None),
        P("row", "col"),
        P("col"),
        P("col"),
        P("col"),
        P("col", None),
        P(),
        P("col"),
        P("col", "row"),
    )
    out_specs = P("ctx", ("row", "col"))
    return jax.shard_map(local, mesh=mesh, in_specs=in_specs, out_specs=out_specs, check_vma=False)
```

```python
import functools

import jax
import jax.numpy as jnp
from jax import lax
from jax.experimental import pallas as pl
from jax.experimental.pallas import tpu as pltpu
from jax.sharding import PartitionSpec as P

Q = 256
EPS = 1e-05
HALO = 16
MIB = 1024 * 1024
f32 = jnp.float32
bf16 = jnp.bfloat16
highest_mode = lax.Precision.HIGHEST


def mm(a, b):
    return jnp.dot(a, b, preferred_element_type=f32)


def mm_tn(a, b):
    return lax.dot_general(a, b, (((0,), (0,)), ((), ())), preferred_element_type=f32)


def mm_nt(a, b):
    return lax.dot_general(a, b, (((1,), (1,)), ((), ())), preferred_element_type=f32)


def silu(v):
    return v / (1.0 + jnp.exp(-v))


def softplus(v):
    return jnp.maximum(v, 0.0) + jnp.log(1.0 + jnp.exp(-jnp.abs(v)))


def total(mine, theirs):
    return (mine.astype(f32) + theirs.astype(f32)).astype(bf16).astype(f32)


def spread(per_head, head_dim):
    heads = per_head.shape[0]
    high = per_head.astype(bf16)
    low = (per_head - high.astype(f32)).astype(bf16)
    parts = jnp.concatenate([high.astype(f32), low.astype(f32)], axis=0).astype(bf16)
    shape = (2 * heads, heads * head_dim)
    row = lax.broadcasted_iota(jnp.int32, shape, 0) % heads
    col = lax.broadcasted_iota(jnp.int32, shape, 1) // head_dim
    return mm_tn(parts, jnp.where(row == col, 1.0, 0.0).astype(bf16))


def pick(row_vector, first, count):
    shape = (count, row_vector.shape[1])
    lane = lax.broadcasted_iota(jnp.int32, shape, 1)
    sub = lax.broadcasted_iota(jnp.int32, shape, 0)
    return jnp.sum(jnp.where(lane == sub + first, row_vector, 0.0), axis=1, keepdims=True)


def conv(ext_ref, taps, toks):
    count = taps.shape[0]
    running = None
    for tap in range(count):
        term = taps[tap : tap + 1, :] * ext_ref[pl.ds(HALO - count + 1 + tap, toks), :]
        running = term if running is None else running + term
    return running


def prefix(messages, here, state_dim):
    def parts(message):
        return message[:state_dim].astype(f32), message[state_dim : state_dim + 1].astype(f32)

    state, decay = parts(messages[0])
    enter = jnp.zeros_like(state)
    reach = jnp.ones_like(decay)
    for step, message in enumerate(messages[1:]):
        their_state, their_decay = parts(message)
        later = ((here >> step) & 1) == 1
        enter = jnp.where(later, enter + reach * their_state, enter)
        reach = jnp.where(later, reach * their_decay, reach)
        state = jnp.where(later, decay * their_state + state, their_decay * state + their_state)
        decay = decay * their_decay
    return enter, state, decay


def copies(pairs, sems):
    started = []
    for i, (source, target) in enumerate(pairs):
        now = pltpu.make_async_copy(source, target, sems.at[i])
        now.start()
        started.append(now)
    return started


def product(tok, held, waits, acc, kb):
    for i in range(tok.shape[1] // kb):
        for wait in waits[i]:
            wait.wait()
        deep = slice(i * kb, (i + 1) * kb)
        for low in range(0, acc.shape[1], 256):
            cols = slice(low, min(low + 256, acc.shape[1]))
            part = mm(tok[:, deep], held[deep, cols])
            if i == 0:
                acc[:, cols] = part
            else:
                acc[:, cols] += part


def place():
    return lax.axis_index("row"), lax.axis_index("col"), lax.axis_index("ctx")


def first_kernel(tok, w_x, w_bc, w_dt, msg, edge, held_tok, held_x, held_bc, held_dt, acc_x, acc_bc, acc_dt, sems, *, chunks, kb):
    toks, lanes = acc_bc.shape
    width = acc_x.shape[1]
    low = pl.multiple_of((1 - place()[0]) * chunks * width, width)
    parts = tok.shape[1] // kb
    pairs = []
    for i in range(parts):
        deep = pl.ds(i * kb, kb)
        pairs += [
            (tok.at[:, deep], held_tok.at[:, deep]),
            (w_x.at[deep, pl.ds(low, width)], held_x.at[deep, :]),
            (w_bc.at[deep, :], held_bc.at[deep, :]),
            (w_dt.at[:, deep], held_dt.at[:, deep]),
        ]
    started = copies(pairs, sems)
    for i in range(parts):
        for wait in started[4 * i : 4 * i + 4]:
            wait.wait()
        deep = slice(i * kb, (i + 1) * kb)
        now = held_tok[:, deep]
        for acc, part in (
            (acc_x, mm(now, held_x[deep, :])),
            (acc_bc, mm(now, held_bc[deep, :])),
            (acc_dt, mm_nt(held_dt[:, deep], now)),
        ):
            if i == 0:
                acc[...] = part
            else:
                acc[...] += part
    heads = acc_dt.shape[0]
    msg[:toks, :] = acc_bc[...].astype(bf16)
    msg[toks : toks + heads, :] = acc_dt[...].astype(bf16)
    edge[:HALO, :] = acc_bc[toks - HALO :, :].astype(bf16)
    for j in range(width // lanes):
        low = toks + heads + j * toks
        cols = slice(j * lanes, (j + 1) * lanes)
        msg[low : low + toks, :] = acc_x[:, cols].astype(bf16)
        edge[(1 + j) * HALO : (2 + j) * HALO, :] = acc_x[toks - HALO :, cols].astype(bf16)


def second_kernel(tok, w_x, edge_in, msg, mine, edge_other, edge_own, held_tok, held, acc, sems, *, chunks, kb):
    toks, width = acc.shape
    lanes = msg.shape[1]
    row = place()[0]
    half = chunks * (msg.shape[0] // toks) * lanes
    first = width - half
    low_other = pl.multiple_of((2 - row) * half - first, lanes)
    low_own = pl.multiple_of(row * half, lanes)
    parts = tok.shape[1] // kb
    pairs = []
    for i in range(parts):
        deep = pl.ds(i * kb, kb)
        pairs += [
            (tok.at[:, deep], held_tok.at[:, deep]),
            (w_x.at[deep, pl.ds(low_other, first)], held.at[deep, pl.ds(0, first)]),
            (w_x.at[deep, pl.ds(low_own, half)], held.at[deep, pl.ds(first, half)]),
        ]
    started = copies(pairs, sems)
    product(held_tok, held, [started[3 * i : 3 * i + 3] for i in range(parts)], acc, kb)
    per = msg.shape[0] // toks
    base = edge_in.shape[0]
    edge_other[:base, :] = edge_in[...]
    edge_own[:HALO, :] = edge_in[:HALO, :]
    for j in range(width // lanes):
        now = acc[:, j * lanes : (j + 1) * lanes].astype(bf16)
        if j < per:
            msg[j * toks : (j + 1) * toks, :] = now
            edge_other[base + j * HALO : base + (j + 1) * HALO, :] = now[toks - HALO :, :]
        else:
            i = j - per
            mine[i * toks : (i + 1) * toks, :] = now
            edge_own[(i + 1) * HALO : (i + 2) * HALO, :] = now[toks - HALO :, :]


def gate_product_kernel(tok, weight, *refs, kb):
    *outs, tok_out, held, acc, sems = refs
    toks, width = acc.shape
    lanes = outs[0].shape[1]
    low = pl.multiple_of((1 - place()[0]) * width, width)
    parts = tok.shape[1] // kb
    pairs = []
    for i in range(parts):
        deep = pl.ds(i * kb, kb)
        pairs += [
            (tok.at[:, deep], tok_out.at[:, deep]),
            (weight.at[deep, pl.ds(low, width)], held.at[deep, :]),
        ]
    started = copies(pairs, sems)
    product(tok_out, held, [started[2 * i : 2 * i + 2] for i in range(parts)], acc, kb)
    per = width // lanes // len(outs)
    for j in range(width // lanes):
        at_row = j % per * toks
        outs[j // per][at_row : at_row + toks, :] = acc[:, j * lanes : (j + 1) * lanes].astype(bf16)


def middle_kernel(tok, weight, w_out, scores, skip, *refs, chunks, kb, head_dim):
    scans, refs = [refs[4 * c : 4 * c + 4] for c in range(chunks)], refs[4 * chunks :]
    inners, refs = refs[:chunks], refs[chunks:]
    mine, w_own, held, acc, sems = refs
    toks, width = acc.shape
    lanes = mine.shape[1]
    where = place()
    low = pl.multiple_of(where[0] * width, width)
    parts = tok.shape[1] // kb
    pairs = [
        (weight.at[pl.ds(i * kb, kb), pl.ds(low, width)], held.at[pl.ds(i * kb, kb), :])
        for i in range(parts)
    ]
    pairs += [
        (w_out.at[pl.ds(low + i * lanes, lanes), :], w_own.at[pl.ds(i * lanes, lanes), :])
        for i in range(width // lanes)
    ]
    started = copies(pairs, sems)
    heads = width // head_dim
    for c in range(chunks):
        within(
            where, scores, *scans[c], skip, inners[c], head_dim=head_dim,
            first_of=c * heads // chunks, local_heads=heads,
        )
    product(tok, held, [[now] for now in started[:parts]], acc, kb)
    for j in range(width // lanes):
        mine[j * toks : (j + 1) * toks, :] = acc[:, j * lanes : (j + 1) * lanes].astype(bf16)
    for now in started[parts:]:
        now.wait()


def state_kernel(
    *refs, first, chunk, chunks, head_dim, state_dim, toks, lanes
):
    refs = list(refs)
    if not first:
        bc_in = refs.pop(0)
    mine, theirs, x_mine, x_theirs, edge_a, edge_b, taps_x, taps_bc, bias, decay = refs[:10]
    refs = refs[10:]
    if first:
        bc_out, scores = refs.pop(0), refs.pop(0)
    msg, scaled, conv_out, cum_out, cum_t_out, ext = refs
    row, _, here = place()
    blocks = x_mine.shape[0] // toks // chunks
    heads = blocks * lanes // head_dim
    local_heads = heads * chunks
    inside = jnp.where(here > 0, 1.0, 0.0)

    def halo(block):
        low = block * HALO
        return total(edge_a[low : low + HALO, :], edge_b[low : low + HALO, :]) * inside

    if first:
        ext[:HALO, :] = halo(0)
        ext[HALO:, :] = total(mine[:toks, :], theirs[:toks, :])
        bc_now = silu(conv(ext, taps_bc[...], toks)).astype(bf16)
        bc_out[...] = bc_now
        b_now = bc_now[:, :state_dim]
        products = mm_nt(bc_now[:, state_dim:], b_now)
        shape = (toks, toks)
        lower = lax.broadcasted_iota(jnp.int32, shape, 0) >= lax.broadcasted_iota(jnp.int32, shape, 1)
        scores[...] = jnp.where(lower, products, 0.0)
    else:
        b_now = bc_in[:, :state_dim]

    low = pl.multiple_of(toks + row * local_heads, local_heads)
    dt_sum = total(mine[pl.ds(low, local_heads), :], theirs[pl.ds(low, local_heads), :])
    dt_sum = dt_sum[chunk * heads : (chunk + 1) * heads]
    first_head = row * local_heads + chunk * heads
    dt_now = softplus(dt_sum + pick(bias[...], first_head, heads))
    log_decay = -pick(decay[...], first_head, heads) * dt_now
    shape = (toks, toks)
    upper = lax.broadcasted_iota(jnp.int32, shape, 0) <= lax.broadcasted_iota(jnp.int32, shape, 1)
    cum = lax.dot_general(
        log_decay,
        jnp.where(upper, 1.0, 0.0),
        (((1,), (0,)), ((), ())),
        precision=highest_mode,
        preferred_element_type=f32,
    )
    last = cum[:, toks - 1 : toks]
    cum_out[...] = cum
    cum_t_out[...] = cum.T
    dt_wide = spread(dt_now, head_dim)
    tail_wide = spread(dt_now * jnp.exp(last - cum), head_dim)
    through = spread(jnp.exp(jnp.broadcast_to(last, (heads, HALO))), head_dim)
    rows = state_dim + HALO
    x_low = x_theirs.shape[0] - blocks * toks
    taps_low = (row * chunks + chunk) * blocks * lanes
    for j in range(blocks):
        ext[:HALO, :] = halo(1 + chunk * blocks + j)
        ext[HALO:, :] = total(
            x_mine[(chunk * blocks + j) * toks : (chunk * blocks + j + 1) * toks, :],
            x_theirs[x_low + j * toks : x_low + (j + 1) * toks, :],
        )
        cols = slice(j * lanes, (j + 1) * lanes)
        x_now = silu(conv(ext, taps_x[:, pl.ds(pl.multiple_of(taps_low + j * lanes, lanes), lanes)], toks))
        conv_out[:, cols] = x_now.astype(bf16)
        scaled[:, cols] = (x_now * dt_wide[:, cols]).astype(bf16)
        state = mm_tn(b_now, (x_now * tail_wide[:, cols]).astype(bf16))
        msg[j * rows : j * rows + state_dim, :] = state.astype(bf16)
        msg[j * rows + state_dim : (j + 1) * rows, :] = through[:, cols].astype(bf16)


def combine_kernel(*refs, state_dim, lanes):
    *messages, out = refs
    rows = state_dim + HALO
    for j in range(out.shape[0] // rows):
        now = [m[j * rows : (j + 1) * rows, :] for m in messages]
        _, state, decay = prefix(now, place()[2], state_dim)
        out[j * rows : j * rows + state_dim, :] = state.astype(bf16)
        out[j * rows + state_dim : (j + 1) * rows, :] = jnp.broadcast_to(decay, (HALO, lanes)).astype(bf16)


def within(where, scores, scaled, conv_out, cum, cum_t, skip, out, *, head_dim, first_of, local_heads):
    toks, channels = scaled.shape
    pair = 2 * head_dim
    half = toks // 2
    heads = channels // head_dim
    skip_now = pick(skip[...], where[0] * local_heads + first_of, heads)
    skip_wide = spread(jnp.broadcast_to(skip_now, (heads, HALO)), head_dim)[:1, :]
    left = lax.broadcasted_iota(jnp.int32, (toks, pair), 1) < head_dim
    zero = jnp.zeros((toks, pair), bf16)
    for p in range(heads // 2):
        cols = slice(p * pair, (p + 1) * pair)
        x_pair = scaled[:, cols]
        top = None
        for side in range(2):
            h = 2 * p + side
            x_now = jnp.where(left, x_pair, zero) if side == 0 else jnp.where(left, zero, x_pair)
            gap_top = jnp.minimum(cum_t[:half, h : h + 1] - cum[h : h + 1, :half], 0.0)
            gap_low = jnp.minimum(cum_t[half:, h : h + 1] - cum[h : h + 1, :], 0.0)
            w_top = (jnp.exp(gap_top) * scores[:half, :half]).astype(bf16)
            w_low = (jnp.exp(gap_low) * scores[half:, :]).astype(bf16)
            part_top = mm(w_top, x_now[:half])
            part_low = mm(w_low, x_now)
            top = part_top if top is None else top + part_top
            low = part_low if side == 0 else low + part_low
        skips = skip_wide[:, cols]
        out[:half, cols] = top + skips * conv_out[:half, cols].astype(f32)
        out[half:, cols] = low + skips * conv_out[half:, cols].astype(f32)


def gate_kernel(inner, bc, cum, z_mine, z_theirs, gain, *refs, messages, chunk, chunks, head_dim, state_dim, lanes):
    messages, outs = refs[:messages], refs[messages:]
    toks = inner.shape[0]
    part_toks = toks // len(outs)
    row, _, here = place()
    gain_low = (row * chunks + chunk) * inner.shape[1]
    rows = state_dim + HALO
    grown = spread(jnp.exp(cum[...]), head_dim)
    c_now = bc[:, state_dim:]
    wide = 2 * head_dim
    shape = (wide, wide)
    same = (lax.broadcasted_iota(jnp.int32, shape, 0) // head_dim) == (
        lax.broadcasted_iota(jnp.int32, shape, 1) // head_dim
    )
    mean_of = jnp.where(same, 1.0 / head_dim, 0.0).astype(bf16)
    for j in range(inner.shape[1] // lanes):
        now = [m[j * rows : (j + 1) * rows, :] for m in messages]
        enter, _, _ = prefix(now, here, state_dim)
        cols = slice(j * lanes, (j + 1) * lanes)
        scanned = inner[:, cols] + grown[:, cols] * mm(c_now, enter.astype(bf16))
        z_low = (chunk * inner.shape[1] // lanes + j) * toks
        z_now = total(z_mine[z_low : z_low + toks, :], z_theirs[j * toks : (j + 1) * toks, :])
        gated = scanned * silu(z_now)
        square = gated * gated
        for i in range(lanes // wide):
            part = square[:, i * wide : (i + 1) * wide]
            high = part.astype(bf16)
            rest = (part - high.astype(f32)).astype(bf16)
            mean = mm(high, mean_of) + mm(rest, mean_of)
            low = j * lanes + i * wide
            done = (
                gated[:, i * wide : (i + 1) * wide]
                * lax.rsqrt(mean + EPS)
                * gain[:, pl.ds(pl.multiple_of(gain_low + low, wide), wide)]
            ).astype(bf16)
            for t, out in enumerate(outs):
                out[j * part_toks : (j + 1) * part_toks, i * wide : (i + 1) * wide] = done[
                    t * part_toks : (t + 1) * part_toks
                ]


def own_kernel(weight, w_own, *refs, groups):
    *normed, partial, rest, whole, sems = refs
    toks, width = partial.shape
    lanes = normed[0].shape[1]
    half = rest.shape[0]
    other = pl.multiple_of((1 - place()[0]) * half, half)
    started = copies(
        [
            (weight.at[pl.ds(other + i * lanes, lanes), :], rest.at[pl.ds(i * lanes, lanes), :])
            for i in range(half // lanes)
        ],
        sems,
    )
    low = 0
    for parts in groups:
        chunk = [normed.pop(0) for _ in range(parts)]
        part_toks = toks // parts
        for j in range(chunk[0].shape[0] // part_toks):
            for t, part in enumerate(chunk):
                whole[t * part_toks : (t + 1) * part_toks, low : low + lanes] = part[
                    j * part_toks : (j + 1) * part_toks, :
                ]
            low += lanes
    for low in range(0, width, 512):
        cols = slice(low, min(low + 512, width))
        partial[:, cols] = mm(whole[...], w_own[:, cols])
    for now in started:
        now.wait()


def rest_kernel(partial, rest, *refs, part, parts, pair_of, groups):
    *normed, send, keep = refs
    part_toks, piece = send.shape
    lanes = normed[0].shape[1]
    toks = partial.shape[0]
    rows = slice(part * part_toks, (part + 1) * part_toks)
    step = min(512, piece)
    where = place()
    for target, core in ((send, 1 - where[1] % 2), (keep, where[1] % 2)):
        base = (pair_of(where) * 2 + core) * piece
        for low in range(0, piece, step):
            cols = pl.ds(pl.multiple_of(base + low, step), step)
            acc = partial[rows, cols]
            block = 0
            for chunk, pieces in zip(normed, groups):
                held_toks = toks // pieces
                first = part * part_toks if pieces == 1 else 0
                for j in range(chunk.shape[0] // held_toks):
                    now = chunk[j * held_toks + first : j * held_toks + first + part_toks, :]
                    acc = acc + mm(now, rest[block * lanes : (block + 1) * lanes, cols])
                    block += 1
            target[:, low : low + step] = acc.astype(bf16)


def sds(*shape, dtype=bf16):
    return jax.ShapeDtypeStruct(shape, dtype)


def cost(flops, size):
    return pl.CostEstimate(flops=int(flops), bytes_accessed=int(size), transcendentals=0)


def call(kernel, args, specs, outs, scratch=(), flops=0, size=0, name=None, mib=16):
    return pl.pallas_call(
        kernel,
        in_specs=specs or [IN_VMEM] * len(args),
        out_specs=[IN_VMEM] * len(outs),
        scratch_shapes=list(scratch),
        out_shape=outs,
        compiler_params=pltpu.CompilerParams(vmem_limit_bytes=mib * MIB),
        cost_estimate=cost(flops, size),
        name=name,
    )(*args)


IN_VMEM = pl.BlockSpec(memory_space=pltpu.VMEM)
IN_HBM = pl.BlockSpec(memory_space=pltpu.HBM)


def swapped(shard, axis, by):
    devices = lax.axis_size(axis)
    return lax.ppermute(shard, axis, [(i, i ^ by) for i in range(devices)])


def fast(
    tokens, proj_x, proj_z, proj_bc, proj_dt, dt_bias, decay_rate, skip_gain,
    conv_x, conv_bc, norm_gain, proj_out,
):
    toks, depth = tokens.shape
    heads = proj_dt.shape[1]
    head_dim = proj_x.shape[1] // heads
    lanes = proj_bc.shape[1]
    state_dim = lanes // 2
    taps = conv_bc.shape[1]
    local_heads = heads // 2
    half = local_heads * head_dim
    chunks = 2
    width = half // chunks
    blocks = width // lanes
    chunk_heads = local_heads // chunks
    out_cols = proj_out.shape[1]
    ctx_size = lax.axis_size("ctx")
    conv_x_t, conv_bc_t, proj_dt_t = conv_x.T, conv_bc.T, proj_dt.T
    bias, decay, skip, gain = (v[None] for v in (dt_bias, decay_rate, skip_gain, norm_gain))

    kb = depth // 8
    parts = depth // kb
    edge_rows = (1 + chunks * blocks) * HALO
    msg_first, edge_first = call(
        functools.partial(first_kernel, chunks=chunks, kb=kb),
        (tokens, proj_x, proj_bc, proj_dt_t),
        [IN_HBM] * 4,
        [sds(toks + heads + blocks * toks, lanes), sds((1 + blocks) * HALO, lanes)],
        [
            pltpu.VMEM((toks, depth), bf16),
            pltpu.VMEM((depth, width), bf16),
            pltpu.VMEM((depth, lanes), bf16),
            pltpu.VMEM((heads, depth), bf16),
            pltpu.VMEM((toks, width), f32),
            pltpu.VMEM((toks, lanes), f32),
            pltpu.VMEM((heads, toks), f32),
            pltpu.SemaphoreType.DMA((4 * parts,)),
        ],
        flops=2 * toks * depth * (width + lanes + heads),
        size=2 * depth * (toks + width + lanes + heads),
        name="first",
        mib=60,
    )
    first_got = swapped(msg_first, "row", 1)
    msg_second, x_mine, edge_other, edge_own = call(
        functools.partial(second_kernel, chunks=chunks, kb=kb),
        (tokens, proj_x, edge_first),
        [IN_HBM, IN_HBM, IN_VMEM],
        [sds(blocks * toks, lanes), sds(chunks * blocks * toks, lanes), *[sds(edge_rows, lanes)] * 2],
        [
            pltpu.VMEM((toks, depth), bf16),
            pltpu.VMEM((depth, width + half), bf16),
            pltpu.VMEM((toks, width + half), f32),
            pltpu.SemaphoreType.DMA((3 * parts,)),
        ],
        flops=2 * toks * depth * (width + half),
        size=2 * depth * (toks + width + half),
        name="second",
        mib=52,
    )
    second_got = swapped(msg_second, "row", 1)
    down = [(i, (i + 1) % ctx_size) for i in range(ctx_size)]
    edge_a = lax.ppermute(
        edge_other, ("ctx", "row"), [(2 * i + s, 2 * j + 1 - s) for i, j in down for s in range(2)]
    )
    edge_b = lax.ppermute(edge_own, "ctx", down)
    *z_send, tok_held = call(
        functools.partial(gate_product_kernel, kb=kb),
        (tokens, proj_z),
        [IN_HBM] * 2,
        [*[sds(blocks * toks, lanes)] * chunks, sds(toks, depth)],
        [
            pltpu.VMEM((depth, half), bf16),
            pltpu.VMEM((toks, half), f32),
            pltpu.SemaphoreType.DMA((2 * parts,)),
        ],
        flops=2 * toks * depth * half,
        size=2 * depth * (toks + half),
        name="z_other",
        mib=50,
    )
    z_got = [swapped(z, "row", 1) for z in z_send]

    rows = state_dim + HALO
    sizes = dict(head_dim=head_dim, state_dim=state_dim, lanes=lanes)
    states, scans = [], []
    bc_now = scores = None
    for c in range(chunks):
        args = [] if c == 0 else [bc_now]
        args += [
            msg_first, first_got, x_mine, first_got if c == 0 else second_got, edge_a, edge_b,
            conv_x_t, conv_bc_t, bias, decay,
        ]
        outs = [sds(toks, lanes), sds(toks, toks, dtype=f32)] if c == 0 else []
        outs += [
            sds(blocks * rows, lanes),
            sds(toks, width),
            sds(toks, width),
            sds(chunk_heads, toks, dtype=f32),
            sds(toks, chunk_heads, dtype=f32),
        ]
        got = call(
            functools.partial(
                state_kernel, first=c == 0, chunk=c, chunks=chunks, toks=toks, **sizes
            ),
            args,
            None,
            outs,
            [pltpu.VMEM((HALO + toks, lanes), f32)],
            flops=2 * toks * width * (state_dim + 64),
            size=2 * toks * width * 6,
            name="state",
        )
        if c == 0:
            bc_now, scores, *got = got
        states.append(got[0])
        scans.append(got[1:])

    messages = []
    for c in range(chunks):
        heard = [states[c]]
        send = states[c]
        by = 1
        while by < ctx_size:
            if by > 1:
                (send,) = call(
                    functools.partial(combine_kernel, state_dim=state_dim, lanes=lanes),
                    heard, None, [sds(*send.shape)],
                    flops=send.size * 6, size=send.size * 6, name="combine",
                )
            heard.append(swapped(send, "ctx", by))
            by *= 2
        messages.append(heard)

    args = (tok_held, proj_z, proj_out, scores, skip, *[a for scan in scans for a in scan])
    *inners, z_mine, w_own = call(
        functools.partial(middle_kernel, chunks=chunks, kb=kb, head_dim=head_dim),
        args,
        [IN_VMEM, IN_HBM, IN_HBM, *[IN_VMEM] * (len(args) - 3)],
        [*[sds(toks, width, dtype=f32)] * chunks, sds(chunks * blocks * toks, lanes), sds(half, out_cols)],
        [
            pltpu.VMEM((depth, half), bf16),
            pltpu.VMEM((toks, half), f32),
            pltpu.SemaphoreType.DMA((parts + half // lanes,)),
        ],
        flops=2 * toks * half * (depth + 2 * toks),
        size=2 * depth * half + 2 * half * out_cols,
        name="middle",
        mib=38,
    )

    normed, normed_got = [], []
    groups = [1] * (chunks - 1) + [2]
    for c in range(chunks):
        now = call(
            functools.partial(gate_kernel, messages=len(messages[c]), chunk=c, chunks=chunks, **sizes),
            (inners[c], bc_now, scans[c][2], z_mine, z_got[c], gain, *messages[c]),
            None,
            [sds(blocks * toks // groups[c], lanes)] * groups[c],
            flops=2 * toks * width * (state_dim + 4 * head_dim),
            size=2 * toks * width * 6,
            name="gate",
        )
        normed.append(now)
        normed_got.append([swapped(part, "row", 1) for part in now])

    piece = out_cols // lax.axis_size("col")
    args = (proj_out, w_own, *[part for now in normed for part in now])
    partial, rest = call(
        functools.partial(own_kernel, groups=groups),
        args,
        [IN_HBM, *[IN_VMEM] * (len(args) - 1)],
        [sds(toks, out_cols, dtype=f32), sds(half, out_cols)],
        [pltpu.VMEM((toks, half), bf16), pltpu.SemaphoreType.DMA((half // lanes,))],
        flops=2 * toks * half * out_cols,
        size=2 * half * out_cols,
        name="out_own",
        mib=26,
    )

    def out_rest(part, parts, pair_of, name):
        args = (partial, rest, *[now[part] if len(now) > 1 else now[0] for now in normed_got])
        return call(
            functools.partial(
                rest_kernel, part=part, parts=parts, pair_of=pair_of,
                groups=[len(now) if parts > 1 else 1 for now in normed_got],
            ),
            args,
            None,
            [sds(toks // parts, piece)] * 2,
            flops=2 * toks // parts * half * 2 * piece,
            size=half * 2 * piece,
            name=name,
        )

    def added(a, b):
        return (a.astype(f32) + b.astype(f32)).astype(bf16)

    parts = groups[-1]
    far = [out_rest(part, parts, lambda w: 1 - w[1] // 2, "out_far") for part in range(parts)]
    far = [added(keep, swapped(send, "col", 1)) for send, keep in far]
    far_got = [swapped(now, "col", 2) for now in far]
    near = [out_rest(part, parts, lambda w: w[1] // 2, "out_near") for part in range(parts)]
    near_keep, near_send = (jnp.concatenate([now[i] for now in near]) for i in (1, 0))
    total_near = near_keep.astype(f32) + swapped(near_send, "col", 1).astype(f32)
    return (total_near + jnp.concatenate(far_got).astype(f32)).astype(bf16)


def shifted(shard, axis, by):
    devices = lax.axis_size(axis)
    pairs = [(i, i + by) for i in range(devices) if 0 <= i + by < devices]
    return lax.ppermute(shard, axis, pairs)


def general(
    tokens,
    proj_x,
    proj_z,
    proj_bc,
    proj_dt,
    dt_bias,
    decay_rate,
    skip_gain,
    conv_x,
    conv_bc,
    norm_gain,
    proj_out,
):
    tok_count = tokens.shape[0]
    col_heads = proj_dt.shape[1]
    head_dim = proj_x.shape[1] // col_heads
    state_dim = proj_bc.shape[1] // 2
    tap_count = conv_bc.shape[1]
    group_count = tok_count // Q
    bc_term = jnp.einsum("dc,td->ct", proj_bc, tokens, preferred_element_type=jnp.float32)
    local_heads = col_heads // lax.axis_size("row")
    first_head = lax.axis_index("row") * local_heads
    x_part = jnp.einsum("dc,td->ct", proj_x, tokens, preferred_element_type=jnp.float32).reshape(
        local_heads * lax.axis_size("row"), head_dim, tok_count
    )
    z_part = jnp.einsum("dc,td->ct", proj_z, tokens, preferred_element_type=jnp.float32).reshape(
        local_heads * lax.axis_size("row"), head_dim, tok_count
    )
    dt_part = jnp.einsum("dc,td->ct", proj_dt, tokens, preferred_element_type=jnp.float32).reshape(
        local_heads * lax.axis_size("row"), 1, tok_count
    )
    head_sum = lax.psum_scatter(
        jnp.concatenate([x_part, z_part, dt_part], axis=1).astype(jnp.bfloat16),
        "row",
        scatter_dimension=0,
        tiled=True,
    )
    bc_sum = lax.psum(bc_term.astype(jnp.bfloat16), "row")
    channels = local_heads * head_dim
    z_in = head_sum[:, head_dim : 2 * head_dim]
    dt_in = head_sum[:, 2 * head_dim]
    flat_in = jnp.concatenate([head_sum[:, :head_dim].reshape(channels, tok_count), bc_sum], axis=0)
    prior = shifted(flat_in[:, tok_count - tap_count + 1 :], "ctx", 1)
    padded = jnp.concatenate([prior, flat_in], axis=1).astype(jnp.float32)
    kernel = jnp.concatenate(
        [lax.dynamic_slice_in_dim(conv_x, first_head * head_dim, channels, 0), conv_bc], axis=0
    )
    running = jnp.zeros(flat_in.shape, jnp.float32)
    for tap_index in range(tap_count):
        running = (
            running
            + kernel[:, tap_index : tap_index + 1] * padded[:, tap_index : tap_index + tok_count]
        )
    conv_out = jax.nn.silu(running)
    x_conv = conv_out[:channels].reshape(local_heads, head_dim, tok_count)
    b_blocks = conv_out[channels : channels + state_dim].reshape(state_dim, group_count, Q)
    c_blocks = conv_out[channels + state_dim :].reshape(state_dim, group_count, Q)
    bias_now = lax.dynamic_slice_in_dim(dt_bias, first_head, local_heads, 0)
    decay_now = lax.dynamic_slice_in_dim(decay_rate, first_head, local_heads, 0)
    skip_now = lax.dynamic_slice_in_dim(skip_gain, first_head, local_heads, 0)
    gain_now = lax.dynamic_slice_in_dim(norm_gain, first_head * head_dim, channels, 0).reshape(
        local_heads, head_dim, 1
    )
    dt_full = jax.nn.softplus(dt_in.astype(jnp.float32) + bias_now[:, None])
    log_decay = -decay_now[:, None] * dt_full
    x_scaled = x_conv * dt_full[:, None, :]
    cum_decay = jnp.cumsum(log_decay.reshape(local_heads, group_count, Q), axis=2)
    x_blocks = x_scaled.reshape(local_heads, head_dim, group_count, Q)
    scores = jnp.einsum("nci,ncj->cij", c_blocks, b_blocks, precision=highest_mode)
    lower_mask = jnp.arange(Q)[:, None] >= jnp.arange(Q)[None, :]
    log_gap = cum_decay[:, :, :, None] - cum_decay[:, :, None, :]
    weights = jnp.where(lower_mask, jnp.exp(jnp.where(lower_mask, log_gap, 0.0)), 0.0)
    inner_out = jnp.einsum(
        "hcij,hpcj->hpci", scores[None] * weights, x_blocks, precision=highest_mode
    )
    tail_weight = jnp.exp(cum_decay[:, :, -1:] - cum_decay)
    group_states = jnp.einsum(
        "hcj,hpcj,ncj->chpn", tail_weight, x_blocks, b_blocks, precision=highest_mode
    )
    group_logs = cum_decay[:, :, -1].T

    def group_step(carried, step_inputs):
        group_log, group_state = step_inputs
        return (jnp.exp(group_log)[:, None, None] * carried + group_state, carried)

    start_state = jnp.zeros((local_heads, head_dim, state_dim), jnp.float32)
    final_state, local_enter = lax.scan(group_step, start_state, (group_logs, group_states))
    device_log = jnp.sum(group_logs, axis=0)
    before_logs = jnp.cumsum(group_logs, axis=0) - group_logs
    log_all, state_all = (
        lax.all_gather(device_log[None].astype(jnp.bfloat16), "ctx", axis=0, tiled=True).astype(
            jnp.float32
        ),
        lax.all_gather(final_state[None].astype(jnp.bfloat16), "ctx", axis=0, tiled=True).astype(
            jnp.float32
        ),
    )
    my_index = lax.axis_index("ctx")
    earlier_mask = (jnp.arange(log_all.shape[0], dtype=jnp.int32) < my_index)[:, None]
    log_prefix = jnp.cumsum(log_all, axis=0)
    up_to_me = jnp.sum(jnp.where(earlier_mask, log_all, 0.0), axis=0)
    reach_weight = jnp.where(
        earlier_mask, jnp.exp(jnp.where(earlier_mask, up_to_me - log_prefix, 0.0)), 0.0
    )
    device_state = jnp.einsum("jh,jhpn->hpn", reach_weight, state_all, precision=highest_mode)
    enter_state = jnp.exp(before_logs)[:, :, None, None] * device_state[None] + local_enter
    outer_out = jnp.exp(cum_decay)[:, None] * jnp.einsum(
        "nci,chpn->hpci", c_blocks, enter_state, precision=highest_mode
    )
    ssm_out = (inner_out + outer_out).reshape(local_heads, head_dim, tok_count) + skip_now[
        :, None, None
    ] * x_conv
    gated = ssm_out * jax.nn.silu(z_in.astype(jnp.float32))
    inv_rms = lax.rsqrt(jnp.mean(gated * gated, axis=1, keepdims=True) + 1e-05)
    normed = (gated * inv_rms * gain_now).astype(jnp.bfloat16)
    out_cols = proj_out.shape[1]
    piece = lax.all_gather(normed, "row", axis=0, tiled=True)
    piece_heads = piece.shape[0]
    rows_now = proj_out.reshape(piece_heads, head_dim, out_cols)
    col_partial = jnp.einsum("hpt,hpd->td", piece, rows_now, preferred_element_type=jnp.float32)
    return lax.psum_scatter(
        col_partial.astype(jnp.bfloat16), "col", scatter_dimension=1, tiled=True
    )


def local(*args):
    tokens, proj_x, _, proj_bc, proj_dt = args[:5]
    toks, heads, lanes = tokens.shape[0], proj_dt.shape[1], proj_bc.shape[1]
    ctx_size = lax.axis_size("ctx")
    fits = (
        lax.axis_size("row") == 2
        and lax.axis_size("col") == 4
        and ctx_size & (ctx_size - 1) == 0
        and toks == Q
        and lanes == toks
        and heads % 32 == 0
        and toks % heads == 0
        and proj_x.shape[1] % (4 * lanes) == 0
        and lanes % (2 * proj_x.shape[1] // heads) == 0
    )
    return fast(*args) if fits else general(*args)


def solution(mesh):
    in_specs = (
        P("ctx", "row"),
        P("row", "col"),
        P("row", "col"),
        P("row", None),
        P("row", "col"),
        P("col"),
        P("col"),
        P("col"),
        P("col", None),
        P(),
        P("col"),
        P("col", "row"),
    )
    out_specs = P("ctx", ("row", "col"))
    return jax.shard_map(local, mesh=mesh, in_specs=in_specs, out_specs=out_specs, check_vma=False)
```

```python
import functools

import jax
import jax.numpy as jnp
from jax import lax
from jax.experimental import pallas as pl
from jax.experimental.pallas import tpu as pltpu
from jax.sharding import PartitionSpec as P

Q = 256
EPS = 1e-05
HALO = 16
MIB = 1024 * 1024
f32 = jnp.float32
bf16 = jnp.bfloat16
highest_mode = lax.Precision.HIGHEST


def mm(a, b):
    return jnp.dot(a, b, preferred_element_type=f32)


def mm_tn(a, b):
    return lax.dot_general(a, b, (((0,), (0,)), ((), ())), preferred_element_type=f32)


def mm_nt(a, b):
    return lax.dot_general(a, b, (((1,), (1,)), ((), ())), preferred_element_type=f32)


def silu(v):
    return v / (1.0 + jnp.exp(-v))


def softplus(v):
    return jnp.maximum(v, 0.0) + jnp.log(1.0 + jnp.exp(-jnp.abs(v)))


def total(mine, theirs):
    return (mine.astype(f32) + theirs.astype(f32)).astype(bf16).astype(f32)


def spread(per_head, head_dim):
    heads = per_head.shape[0]
    high = per_head.astype(bf16)
    low = (per_head - high.astype(f32)).astype(bf16)
    parts = jnp.concatenate([high.astype(f32), low.astype(f32)], axis=0).astype(bf16)
    shape = (2 * heads, heads * head_dim)
    row = lax.broadcasted_iota(jnp.int32, shape, 0) % heads
    col = lax.broadcasted_iota(jnp.int32, shape, 1) // head_dim
    return mm_tn(parts, jnp.where(row == col, 1.0, 0.0).astype(bf16))


def pick(row_vector, first, count):
    shape = (count, row_vector.shape[1])
    lane = lax.broadcasted_iota(jnp.int32, shape, 1)
    sub = lax.broadcasted_iota(jnp.int32, shape, 0)
    return jnp.sum(jnp.where(lane == sub + first, row_vector, 0.0), axis=1, keepdims=True)


def conv(ext_ref, taps, toks):
    count = taps.shape[0]
    running = None
    for tap in range(count):
        term = taps[tap : tap + 1, :] * ext_ref[pl.ds(HALO - count + 1 + tap, toks), :]
        running = term if running is None else running + term
    return running


def prefix(messages, here, state_dim):
    def parts(message):
        return message[:state_dim].astype(f32), message[state_dim : state_dim + 1].astype(f32)

    state, decay = parts(messages[0])
    enter = jnp.zeros_like(state)
    reach = jnp.ones_like(decay)
    for step, message in enumerate(messages[1:]):
        their_state, their_decay = parts(message)
        later = ((here >> step) & 1) == 1
        enter = jnp.where(later, enter + reach * their_state, enter)
        reach = jnp.where(later, reach * their_decay, reach)
        state = jnp.where(later, decay * their_state + state, their_decay * state + their_state)
        decay = decay * their_decay
    return enter, state, decay


def copies(pairs, sems):
    started = []
    for i, (source, target) in enumerate(pairs):
        now = pltpu.make_async_copy(source, target, sems.at[i])
        now.start()
        started.append(now)
    return started


def product(tok, held, waits, acc, kb):
    for i in range(tok.shape[1] // kb):
        for wait in waits[i]:
            wait.wait()
        deep = slice(i * kb, (i + 1) * kb)
        for low in range(0, acc.shape[1], 256):
            cols = slice(low, min(low + 256, acc.shape[1]))
            part = mm(tok[:, deep], held[deep, cols])
            if i == 0:
                acc[:, cols] = part
            else:
                acc[:, cols] += part


def place():
    return lax.axis_index("row"), lax.axis_index("col"), lax.axis_index("ctx")


def first_kernel(tok, w_x, w_bc, w_dt, msg, edge, held_tok, held_x, held_bc, held_dt, acc_x, acc_bc, acc_dt, sems, *, chunks, kb):
    toks, lanes = acc_bc.shape
    width = acc_x.shape[1]
    low = pl.multiple_of((1 - place()[0]) * chunks * width, width)
    parts = tok.shape[1] // kb
    pairs = []
    for i in range(parts):
        deep = pl.ds(i * kb, kb)
        pairs += [
            (tok.at[:, deep], held_tok.at[:, deep]),
            (w_x.at[deep, pl.ds(low, width)], held_x.at[deep, :]),
            (w_bc.at[deep, :], held_bc.at[deep, :]),
            (w_dt.at[:, deep], held_dt.at[:, deep]),
        ]
    started = copies(pairs, sems)
    for i in range(parts):
        for wait in started[4 * i : 4 * i + 4]:
            wait.wait()
        deep = slice(i * kb, (i + 1) * kb)
        now = held_tok[:, deep]
        for acc, part in (
            (acc_x, mm(now, held_x[deep, :])),
            (acc_bc, mm(now, held_bc[deep, :])),
            (acc_dt, mm_nt(held_dt[:, deep], now)),
        ):
            if i == 0:
                acc[...] = part
            else:
                acc[...] += part
    heads = acc_dt.shape[0]
    msg[:toks, :] = acc_bc[...].astype(bf16)
    msg[toks : toks + heads, :] = acc_dt[...].astype(bf16)
    edge[:HALO, :] = acc_bc[toks - HALO :, :].astype(bf16)
    for j in range(width // lanes):
        low = toks + heads + j * toks
        cols = slice(j * lanes, (j + 1) * lanes)
        msg[low : low + toks, :] = acc_x[:, cols].astype(bf16)
        edge[(1 + j) * HALO : (2 + j) * HALO, :] = acc_x[toks - HALO :, cols].astype(bf16)


def second_kernel(tok, w_x, edge_first, msg, mine, edge_other, edge_own, edge_in, held_tok, held, acc, sems, *, chunks, kb):
    toks, width = acc.shape
    lanes = msg.shape[1]
    row = place()[0]
    half = chunks * (msg.shape[0] // toks) * lanes
    first = width - half
    low_other = pl.multiple_of((2 - row) * half - first, lanes)
    low_own = pl.multiple_of(row * half, lanes)
    parts = tok.shape[1] // kb
    pairs = []
    for i in range(parts):
        deep = pl.ds(i * kb, kb)
        pairs += [
            (tok.at[:, deep], held_tok.at[:, deep]),
            (w_x.at[deep, pl.ds(low_other, first)], held.at[deep, pl.ds(0, first)]),
            (w_x.at[deep, pl.ds(low_own, half)], held.at[deep, pl.ds(first, half)]),
        ]
    started = copies([*pairs, (edge_first, edge_in)], sems)
    product(held_tok, held, [started[3 * i : 3 * i + 3] for i in range(parts)], acc, kb)
    started[-1].wait()
    per = msg.shape[0] // toks
    base = edge_in.shape[0]
    edge_other[:base, :] = edge_in[...]
    edge_own[:HALO, :] = edge_in[:HALO, :]
    for j in range(width // lanes):
        now = acc[:, j * lanes : (j + 1) * lanes].astype(bf16)
        if j < per:
            msg[j * toks : (j + 1) * toks, :] = now
            edge_other[base + j * HALO : base + (j + 1) * HALO, :] = now[toks - HALO :, :]
        else:
            i = j - per
            mine[i * toks : (i + 1) * toks, :] = now
            edge_own[(i + 1) * HALO : (i + 2) * HALO, :] = now[toks - HALO :, :]


def gate_product_kernel(tok, weight, *refs, kb):
    *outs, tok_out, held, acc, sems = refs
    toks, width = acc.shape
    lanes = outs[0].shape[1]
    low = pl.multiple_of((1 - place()[0]) * width, width)
    parts = tok.shape[1] // kb
    pairs = []
    for i in range(parts):
        deep = pl.ds(i * kb, kb)
        pairs += [
            (tok.at[:, deep], tok_out.at[:, deep]),
            (weight.at[deep, pl.ds(low, width)], held.at[deep, :]),
        ]
    started = copies(pairs, sems)
    product(tok_out, held, [started[2 * i : 2 * i + 2] for i in range(parts)], acc, kb)
    per = width // lanes // len(outs)
    for j in range(width // lanes):
        at_row = j % per * toks
        outs[j // per][at_row : at_row + toks, :] = acc[:, j * lanes : (j + 1) * lanes].astype(bf16)


def rows_of(weight, target, low, lanes):
    return [
        (weight.at[pl.ds(low + i * lanes, lanes), :], target.at[pl.ds(i * lanes, lanes), :])
        for i in range(target.shape[0] // lanes)
    ]


def rows_of(weight, target, low, lanes):
    return [
        (weight.at[pl.ds(low + i * lanes, lanes), :], target.at[pl.ds(i * lanes, lanes), :])
        for i in range(target.shape[0] // lanes)
    ]


def inner_kernel(scores, skip, w_out, *refs, chunks, head_dim, lanes):
    scans, refs = [refs[4 * c : 4 * c + 4] for c in range(chunks)], refs[4 * chunks :]
    *outs, w_own, sems = refs
    where = place()
    half = w_own.shape[0]
    started = copies(rows_of(w_out, w_own, pl.multiple_of(where[0] * half, half), lanes), sems)

    @pl.when(where[0] >= 0)
    def _():
        heads = half // head_dim
        for c in range(chunks):
            within(
                where, scores, *scans[c], skip, outs[c], head_dim=head_dim,
                first_of=c * heads // chunks, local_heads=heads,
            )

    for now in started:
        now.wait()


def own_gate_kernel(tok, weight, w_out, mine, w_early, held, acc, sems, *, kb):
    toks, width = acc.shape
    lanes = mine.shape[1]
    row = place()[0]
    low = pl.multiple_of(row * width, width)
    parts = tok.shape[1] // kb
    pairs = [
        (weight.at[pl.ds(i * kb, kb), pl.ds(low, width)], held.at[pl.ds(i * kb, kb), :])
        for i in range(parts)
    ]
    pairs += rows_of(w_out, w_early, pl.multiple_of((1 - row) * width, width), lanes)
    started = copies(pairs, sems)
    product(tok, held, [[now] for now in started[:parts]], acc, kb)
    for j in range(width // lanes):
        mine[j * toks : (j + 1) * toks, :] = acc[:, j * lanes : (j + 1) * lanes].astype(bf16)
    for now in started[parts:]:
        now.wait()


def state_kernel(
    *refs, first, chunk, chunks, head_dim, state_dim, toks, lanes
):
    refs = list(refs)
    if not first:
        bc_in = refs.pop(0)
    mine, theirs, x_mine, x_theirs, edge_a, edge_b, taps_x, taps_bc, bias, decay = refs[:10]
    refs = refs[10:]
    if first:
        bc_out, scores = refs.pop(0), refs.pop(0)
    msg, scaled, conv_out, cum_out, cum_t_out, ext = refs
    row, _, here = place()
    blocks = x_mine.shape[0] // toks // chunks
    heads = blocks * lanes // head_dim
    local_heads = heads * chunks
    inside = jnp.where(here > 0, 1.0, 0.0)

    def halo(block):
        low = block * HALO
        return total(edge_a[low : low + HALO, :], edge_b[low : low + HALO, :]) * inside

    if first:
        ext[:HALO, :] = halo(0)
        ext[HALO:, :] = total(mine[:toks, :], theirs[:toks, :])
        bc_now = silu(conv(ext, taps_bc[...], toks)).astype(bf16)
        bc_out[...] = bc_now
        b_now = bc_now[:, :state_dim]
        products = mm_nt(bc_now[:, state_dim:], b_now)
        shape = (toks, toks)
        lower = lax.broadcasted_iota(jnp.int32, shape, 0) >= lax.broadcasted_iota(jnp.int32, shape, 1)
        scores[...] = jnp.where(lower, products, 0.0)
    else:
        b_now = bc_in[:, :state_dim]

    low = pl.multiple_of(toks + row * local_heads, local_heads)
    dt_sum = total(mine[pl.ds(low, local_heads), :], theirs[pl.ds(low, local_heads), :])
    dt_sum = dt_sum[chunk * heads : (chunk + 1) * heads]
    first_head = row * local_heads + chunk * heads
    dt_now = softplus(dt_sum + pick(bias[...], first_head, heads))
    log_decay = -pick(decay[...], first_head, heads) * dt_now
    shape = (toks, toks)
    upper = lax.broadcasted_iota(jnp.int32, shape, 0) <= lax.broadcasted_iota(jnp.int32, shape, 1)
    cum = lax.dot_general(
        log_decay,
        jnp.where(upper, 1.0, 0.0),
        (((1,), (0,)), ((), ())),
        precision=highest_mode,
        preferred_element_type=f32,
    )
    last = cum[:, toks - 1 : toks]
    cum_out[...] = cum
    cum_t_out[...] = cum.T
    dt_wide = spread(dt_now, head_dim)
    tail_wide = spread(dt_now * jnp.exp(last - cum), head_dim)
    through = spread(jnp.exp(jnp.broadcast_to(last, (heads, HALO))), head_dim)
    rows = state_dim + HALO
    x_low = x_theirs.shape[0] - blocks * toks
    taps_low = (row * chunks + chunk) * blocks * lanes
    for j in range(blocks):
        ext[:HALO, :] = halo(1 + chunk * blocks + j)
        ext[HALO:, :] = total(
            x_mine[(chunk * blocks + j) * toks : (chunk * blocks + j + 1) * toks, :],
            x_theirs[x_low + j * toks : x_low + (j + 1) * toks, :],
        )
        cols = slice(j * lanes, (j + 1) * lanes)
        x_now = silu(conv(ext, taps_x[:, pl.ds(pl.multiple_of(taps_low + j * lanes, lanes), lanes)], toks))
        conv_out[:, cols] = x_now.astype(bf16)
        scaled[:, cols] = (x_now * dt_wide[:, cols]).astype(bf16)
        state = mm_tn(b_now, (x_now * tail_wide[:, cols]).astype(bf16))
        msg[j * rows : j * rows + state_dim, :] = state.astype(bf16)
        msg[j * rows + state_dim : (j + 1) * rows, :] = through[:, cols].astype(bf16)


def combine_kernel(*refs, state_dim, lanes):
    *messages, out = refs
    rows = state_dim + HALO
    for j in range(out.shape[0] // rows):
        now = [m[j * rows : (j + 1) * rows, :] for m in messages]
        _, state, decay = prefix(now, place()[2], state_dim)
        out[j * rows : j * rows + state_dim, :] = state.astype(bf16)
        out[j * rows + state_dim : (j + 1) * rows, :] = jnp.broadcast_to(decay, (HALO, lanes)).astype(bf16)


def within(where, scores, scaled, conv_out, cum, cum_t, skip, out, *, head_dim, first_of, local_heads):
    toks, channels = scaled.shape
    pair = 2 * head_dim
    half = toks // 2
    heads = channels // head_dim
    skip_now = pick(skip[...], where[0] * local_heads + first_of, heads)
    skip_wide = spread(jnp.broadcast_to(skip_now, (heads, HALO)), head_dim)[:1, :]
    left = lax.broadcasted_iota(jnp.int32, (toks, pair), 1) < head_dim
    zero = jnp.zeros((toks, pair), bf16)
    for p in range(heads // 2):
        cols = slice(p * pair, (p + 1) * pair)
        x_pair = scaled[:, cols]
        top = None
        for side in range(2):
            h = 2 * p + side
            x_now = jnp.where(left, x_pair, zero) if side == 0 else jnp.where(left, zero, x_pair)
            gap_top = jnp.minimum(cum_t[:half, h : h + 1] - cum[h : h + 1, :half], 0.0)
            gap_low = jnp.minimum(cum_t[half:, h : h + 1] - cum[h : h + 1, :], 0.0)
            w_top = (jnp.exp(gap_top) * scores[:half, :half]).astype(bf16)
            w_low = (jnp.exp(gap_low) * scores[half:, :]).astype(bf16)
            part_top = mm(w_top, x_now[:half])
            part_low = mm(w_low, x_now)
            top = part_top if top is None else top + part_top
            low = part_low if side == 0 else low + part_low
        skips = skip_wide[:, cols]
        out[:half, cols] = top + skips * conv_out[:half, cols].astype(f32)
        out[half:, cols] = low + skips * conv_out[half:, cols].astype(f32)


def gate_kernel(inner, bc, cum, z_mine, z_theirs, gain, *refs, messages, bounds, chunk, chunks, head_dim, state_dim, lanes):
    messages, outs = refs[:messages], refs[messages:]
    toks = inner.shape[0]
    row, _, here = place()
    gain_low = (row * chunks + chunk) * inner.shape[1]
    rows = state_dim + HALO
    grown = spread(jnp.exp(cum[...]), head_dim)
    c_now = bc[:, state_dim:]
    wide = 2 * head_dim
    shape = (wide, wide)
    same = (lax.broadcasted_iota(jnp.int32, shape, 0) // head_dim) == (
        lax.broadcasted_iota(jnp.int32, shape, 1) // head_dim
    )
    mean_of = jnp.where(same, 1.0 / head_dim, 0.0).astype(bf16)
    for j in range(inner.shape[1] // lanes):
        now = [m[j * rows : (j + 1) * rows, :] for m in messages]
        enter, _, _ = prefix(now, here, state_dim)
        cols = slice(j * lanes, (j + 1) * lanes)
        scanned = inner[:, cols] + grown[:, cols] * mm(c_now, enter.astype(bf16))
        z_low = (chunk * inner.shape[1] // lanes + j) * toks
        z_now = total(z_mine[z_low : z_low + toks, :], z_theirs[z_low : z_low + toks, :])
        gated = scanned * silu(z_now)
        square = gated * gated
        for i in range(lanes // wide):
            part = square[:, i * wide : (i + 1) * wide]
            high = part.astype(bf16)
            rest = (part - high.astype(f32)).astype(bf16)
            mean = mm(high, mean_of) + mm(rest, mean_of)
            low = j * lanes + i * wide
            done = (
                gated[:, i * wide : (i + 1) * wide]
                * lax.rsqrt(mean + EPS)
                * gain[:, pl.ds(pl.multiple_of(gain_low + low, wide), wide)]
            ).astype(bf16)
            for (start, end), out in zip(bounds, outs):
                size = end - start
                out[j * size : (j + 1) * size, i * wide : (i + 1) * wide] = done[start:end]


def own_kernel(weight, w_own, *refs, bounds):
    *normed, partial, w_late, whole, sems = refs
    lanes = normed[0].shape[1]
    row = place()[0]
    late = pl.multiple_of((2 - row) * w_own.shape[0] - w_late.shape[0], lanes)
    started = copies(rows_of(weight, w_late, late, lanes), sems)

    @pl.when(row >= 0)
    def _():
        own_product(w_own, normed, partial, whole, bounds)

    for now in started:
        now.wait()


def own_product(weight, normed, partial, whole, bounds):
    width = partial.shape[1]
    lanes = normed[0].shape[1]
    low = 0
    for chunk in zip(*[iter(normed)] * len(bounds)):
        blocks = chunk[0].shape[0] // (bounds[0][1] - bounds[0][0])
        for j in range(blocks):
            for (start, end), part in zip(bounds, chunk):
                size = end - start
                whole[start:end, low : low + lanes] = part[j * size : (j + 1) * size, :]
            low += lanes
    for low in range(0, width, 512):
        cols = slice(low, min(low + 512, width))
        partial[:, cols] = mm(whole[...], weight[:, cols])


def rest_kernel(partial, w_early, w_late, *refs, jobs):
    *normed, send, keep = refs
    lanes = normed[0].shape[1]
    piece = send.shape[1]
    step = min(512, piece)
    _, col, _ = place()
    at_row = 0
    for i, (start, end, far, crossed) in enumerate(jobs):
        size = end - start
        pair = 1 - col // 2 if far else col // 2
        kept = (col + crossed) % 2
        for target, core in ((send, 1 - kept), (keep, kept)):
            base = (pair * 2 + core) * piece
            for low in range(0, piece, step):
                cols = pl.ds(pl.multiple_of(base + low, step), step)
                acc = partial[start:end, cols]
                row = 0
                for chunk in normed[i :: len(jobs)]:
                    for j in range(chunk.shape[0] // size):
                        first = row < w_early.shape[0]
                        held = w_early if first else w_late
                        held_row = row - (0 if first else w_early.shape[0])
                        acc = acc + mm(
                            chunk[j * size : (j + 1) * size, :], held[held_row : held_row + lanes, cols]
                        )
                        row += lanes
                target[at_row : at_row + size, low : low + step] = acc.astype(bf16)
        at_row += size


def sds(*shape, dtype=bf16):
    return jax.ShapeDtypeStruct(shape, dtype)


def cost(flops, size):
    return pl.CostEstimate(flops=int(flops), bytes_accessed=int(size), transcendentals=0)


def call(kernel, args, specs, outs, scratch=(), flops=0, size=0, name=None, mib=16, after=()):
    used = len(args)

    def body(*refs):
        kernel(*refs[:used], *refs[used + len(after) :])

    return pl.pallas_call(
        body,
        in_specs=[*(specs or [IN_VMEM] * used), *[pl.BlockSpec(memory_space=pl.ANY)] * len(after)],
        out_specs=[IN_VMEM] * len(outs),
        scratch_shapes=list(scratch),
        out_shape=outs,
        compiler_params=pltpu.CompilerParams(vmem_limit_bytes=mib * MIB),
        cost_estimate=cost(flops, size),
        name=name,
    )(*args, *after)


IN_VMEM = pl.BlockSpec(memory_space=pltpu.VMEM)
IN_HBM = pl.BlockSpec(memory_space=pltpu.HBM)


def swapped(shard, axis, by):
    devices = lax.axis_size(axis)
    return lax.ppermute(shard, axis, [(i, i ^ by) for i in range(devices)])


def fast(
    tokens, proj_x, proj_z, proj_bc, proj_dt, dt_bias, decay_rate, skip_gain,
    conv_x, conv_bc, norm_gain, proj_out,
):
    toks, depth = tokens.shape
    heads = proj_dt.shape[1]
    head_dim = proj_x.shape[1] // heads
    lanes = proj_bc.shape[1]
    state_dim = lanes // 2
    taps = conv_bc.shape[1]
    local_heads = heads // 2
    half = local_heads * head_dim
    chunks = 2
    width = half // chunks
    blocks = width // lanes
    chunk_heads = local_heads // chunks
    out_cols = proj_out.shape[1]
    ctx_size = lax.axis_size("ctx")
    conv_x_t, conv_bc_t, proj_dt_t = conv_x.T, conv_bc.T, proj_dt.T
    bias, decay, skip, gain = (v[None] for v in (dt_bias, decay_rate, skip_gain, norm_gain))

    kb = depth // 8
    parts = depth // kb
    edge_rows = (1 + chunks * blocks) * HALO
    msg_first, edge_first = call(
        functools.partial(first_kernel, chunks=chunks, kb=kb),
        (tokens, proj_x, proj_bc, proj_dt_t),
        [IN_HBM] * 4,
        [sds(toks + heads + blocks * toks, lanes), sds((1 + blocks) * HALO, lanes)],
        [
            pltpu.VMEM((toks, depth), bf16),
            pltpu.VMEM((depth, width), bf16),
            pltpu.VMEM((depth, lanes), bf16),
            pltpu.VMEM((heads, depth), bf16),
            pltpu.VMEM((toks, width), f32),
            pltpu.VMEM((toks, lanes), f32),
            pltpu.VMEM((heads, toks), f32),
            pltpu.SemaphoreType.DMA((4 * parts,)),
        ],
        flops=2 * toks * depth * (width + lanes + heads),
        size=2 * depth * (toks + width + lanes + heads),
        name="first",
        mib=53,
    )
    first_got = swapped(msg_first, "row", 1)
    msg_second, x_mine, edge_other, edge_own = call(
        functools.partial(second_kernel, chunks=chunks, kb=kb),
        (tokens, proj_x, edge_first),
        [IN_HBM] * 3,
        [sds(blocks * toks, lanes), sds(chunks * blocks * toks, lanes), *[sds(edge_rows, lanes)] * 2],
        [
            pltpu.VMEM(edge_first.shape, bf16),
            pltpu.VMEM((toks, depth), bf16),
            pltpu.VMEM((depth, width + half), bf16),
            pltpu.VMEM((toks, width + half), f32),
            pltpu.SemaphoreType.DMA((3 * parts + 1,)),
        ],
        flops=2 * toks * depth * (width + half),
        size=2 * depth * (toks + width + half),
        name="second",
        mib=52,
    )
    second_got = swapped(msg_second, "row", 1)
    down = [(i, (i + 1) % ctx_size) for i in range(ctx_size)]
    edge_a = lax.ppermute(
        edge_other, ("ctx", "row"), [(2 * i + s, 2 * j + 1 - s) for i, j in down for s in range(2)]
    )
    edge_b = lax.ppermute(edge_own, "ctx", down)
    z_send, tok_held = call(
        functools.partial(gate_product_kernel, kb=kb),
        (tokens, proj_z),
        [IN_HBM] * 2,
        [sds(chunks * blocks * toks, lanes), sds(toks, depth)],
        [
            pltpu.VMEM((depth, half), bf16),
            pltpu.VMEM((toks, half), f32),
            pltpu.SemaphoreType.DMA((2 * parts,)),
        ],
        flops=2 * toks * depth * half,
        size=2 * depth * (toks + half),
        name="z_other",
        mib=50,
        after=(edge_own,),
    )

    rows = state_dim + HALO
    sizes = dict(head_dim=head_dim, state_dim=state_dim, lanes=lanes)
    states, scans = [], []
    bc_now = scores = None
    for c in range(chunks):
        args = [] if c == 0 else [bc_now]
        args += [
            msg_first, first_got, x_mine, first_got if c == 0 else second_got, edge_a, edge_b,
            conv_x_t, conv_bc_t, bias, decay,
        ]
        outs = [sds(toks, lanes), sds(toks, toks, dtype=f32)] if c == 0 else []
        outs += [
            sds(blocks * rows, lanes),
            sds(toks, width),
            sds(toks, width),
            sds(chunk_heads, toks, dtype=f32),
            sds(toks, chunk_heads, dtype=f32),
        ]
        got = call(
            functools.partial(
                state_kernel, first=c == 0, chunk=c, chunks=chunks, toks=toks, **sizes
            ),
            args,
            None,
            outs,
            [pltpu.VMEM((HALO + toks, lanes), f32)],
            flops=2 * toks * width * (state_dim + 64),
            size=2 * toks * width * 6,
            name="state",
            after=(z_send,),
        )
        if c == 0:
            bc_now, scores, *got = got
        states.append(got[0])
        scans.append(got[1:])

    z_send, _ = lax.optimization_barrier((z_send, states))
    z_got = swapped(z_send, "row", 1)
    messages, sent = [], []
    for c in range(chunks):
        heard = [states[c]]
        send = states[c]
        by = 1
        while by < ctx_size:
            if by > 1:
                (send,) = call(
                    functools.partial(combine_kernel, state_dim=state_dim, lanes=lanes),
                    heard, None, [sds(*send.shape)],
                    flops=send.size * 6, size=send.size * 6, name="combine",
                )
            heard.append(swapped(send, "ctx", by))
            by *= 2
        messages.append(heard)
        sent.append(send)

    args = (scores, skip, proj_out, *[a for scan in scans for a in scan])
    *inners, w_own = call(
        functools.partial(inner_kernel, chunks=chunks, head_dim=head_dim, lanes=lanes),
        args,
        [IN_VMEM, IN_VMEM, IN_HBM, *[IN_VMEM] * (len(args) - 3)],
        [*[sds(toks, width, dtype=f32)] * chunks, sds(half, out_cols)],
        [pltpu.SemaphoreType.DMA((half // lanes,))],
        flops=4 * toks * toks * half,
        size=4 * toks * half * 3 + 2 * half * out_cols,
        name="inner",
        mib=42,
    )
    early = half // 2
    z_mine, w_early = call(
        functools.partial(own_gate_kernel, kb=kb),
        (tok_held, proj_z, proj_out),
        [IN_VMEM, IN_HBM, IN_HBM],
        [sds(chunks * blocks * toks, lanes), sds(early, out_cols)],
        [
            pltpu.VMEM((depth, half), bf16),
            pltpu.VMEM((toks, half), f32),
            pltpu.SemaphoreType.DMA((parts + early // lanes,)),
        ],
        flops=2 * toks * half * depth,
        size=2 * depth * half + 2 * early * out_cols,
        name="z_own",
        mib=34,
        after=(sent[-1], inners[-1]),
    )

    normed, normed_got = [], []
    cut = toks * 8 // 16
    bounds = ((0, cut), (cut, toks))
    for c in range(chunks):
        now = call(
            functools.partial(
                gate_kernel, messages=len(messages[c]), bounds=bounds, chunk=c, chunks=chunks, **sizes
            ),
            (inners[c], bc_now, scans[c][2], z_mine, z_got, gain, *messages[c]),
            None,
            [sds(blocks * (end - start), lanes) for start, end in bounds],
            flops=2 * toks * width * (state_dim + 4 * head_dim),
            size=2 * toks * width * 6,
            name="gate",
        )
        normed.append(now)
        normed_got.append([swapped(part, "row", 1) for part in now])

    piece = out_cols // lax.axis_size("col")
    partial, w_late = call(
        functools.partial(own_kernel, bounds=bounds),
        (proj_out, w_own, *[part for now in normed for part in now]),
        [IN_HBM, *[IN_VMEM] * (1 + len(bounds) * chunks)],
        [sds(toks, out_cols, dtype=f32), sds(half - early, out_cols)],
        [pltpu.VMEM((toks, half), bf16), pltpu.SemaphoreType.DMA(((half - early) // lanes,))],
        flops=2 * toks * half * out_cols,
        size=2 * (2 * half - early) * out_cols,
        name="out_own",
        mib=26,
    )

    def out_rest(jobs, name, after=()):
        args = (partial, w_early, w_late, *[now[part] for now in normed_got for part, *_ in jobs])
        jobs = tuple((*bounds[part], far, crossed) for part, far, crossed in jobs)
        return call(
            functools.partial(rest_kernel, jobs=jobs),
            args,
            None,
            [sds(sum(end - start for start, end, *_ in jobs), piece)] * 2,
            name=name,
            after=after,
        )

    def added(a, b):
        return (a.astype(f32) + b.astype(f32)).astype(bf16)

    got_far, near, order = [], [], ()
    for part in range(len(bounds)):
        send, keep = out_rest(((part, True, 0),), "out_far", order)
        far = added(keep, swapped(send, "col", 1))
        got_far.append(swapped(far, "col", 2))
        order = (keep,) if part == 0 else (far,)
        send, keep = out_rest(((part, False, 0),), "out_near", order)
        near.append(keep.astype(f32) + swapped(send, "col", 1).astype(f32))
        order = (keep,)
    return (jnp.concatenate(near) + jnp.concatenate(got_far).astype(f32)).astype(bf16)


def shifted(shard, axis, by):
    devices = lax.axis_size(axis)
    pairs = [(i, i + by) for i in range(devices) if 0 <= i + by < devices]
    return lax.ppermute(shard, axis, pairs)


def general(
    tokens,
    proj_x,
    proj_z,
    proj_bc,
    proj_dt,
    dt_bias,
    decay_rate,
    skip_gain,
    conv_x,
    conv_bc,
    norm_gain,
    proj_out,
):
    tok_count = tokens.shape[0]
    col_heads = proj_dt.shape[1]
    head_dim = proj_x.shape[1] // col_heads
    state_dim = proj_bc.shape[1] // 2
    tap_count = conv_bc.shape[1]
    group_count = tok_count // Q
    bc_term = jnp.einsum("dc,td->ct", proj_bc, tokens, preferred_element_type=jnp.float32)
    local_heads = col_heads // lax.axis_size("row")
    first_head = lax.axis_index("row") * local_heads
    x_part = jnp.einsum("dc,td->ct", proj_x, tokens, preferred_element_type=jnp.float32).reshape(
        local_heads * lax.axis_size("row"), head_dim, tok_count
    )
    z_part = jnp.einsum("dc,td->ct", proj_z, tokens, preferred_element_type=jnp.float32).reshape(
        local_heads * lax.axis_size("row"), head_dim, tok_count
    )
    dt_part = jnp.einsum("dc,td->ct", proj_dt, tokens, preferred_element_type=jnp.float32).reshape(
        local_heads * lax.axis_size("row"), 1, tok_count
    )
    head_sum = lax.psum_scatter(
        jnp.concatenate([x_part, z_part, dt_part], axis=1).astype(jnp.bfloat16),
        "row",
        scatter_dimension=0,
        tiled=True,
    )
    bc_sum = lax.psum(bc_term.astype(jnp.bfloat16), "row")
    channels = local_heads * head_dim
    z_in = head_sum[:, head_dim : 2 * head_dim]
    dt_in = head_sum[:, 2 * head_dim]
    flat_in = jnp.concatenate([head_sum[:, :head_dim].reshape(channels, tok_count), bc_sum], axis=0)
    prior = shifted(flat_in[:, tok_count - tap_count + 1 :], "ctx", 1)
    padded = jnp.concatenate([prior, flat_in], axis=1).astype(jnp.float32)
    kernel = jnp.concatenate(
        [lax.dynamic_slice_in_dim(conv_x, first_head * head_dim, channels, 0), conv_bc], axis=0
    )
    running = jnp.zeros(flat_in.shape, jnp.float32)
    for tap_index in range(tap_count):
        running = (
            running
            + kernel[:, tap_index : tap_index + 1] * padded[:, tap_index : tap_index + tok_count]
        )
    conv_out = jax.nn.silu(running)
    x_conv = conv_out[:channels].reshape(local_heads, head_dim, tok_count)
    b_blocks = conv_out[channels : channels + state_dim].reshape(state_dim, group_count, Q)
    c_blocks = conv_out[channels + state_dim :].reshape(state_dim, group_count, Q)
    bias_now = lax.dynamic_slice_in_dim(dt_bias, first_head, local_heads, 0)
    decay_now = lax.dynamic_slice_in_dim(decay_rate, first_head, local_heads, 0)
    skip_now = lax.dynamic_slice_in_dim(skip_gain, first_head, local_heads, 0)
    gain_now = lax.dynamic_slice_in_dim(norm_gain, first_head * head_dim, channels, 0).reshape(
        local_heads, head_dim, 1
    )
    dt_full = jax.nn.softplus(dt_in.astype(jnp.float32) + bias_now[:, None])
    log_decay = -decay_now[:, None] * dt_full
    x_scaled = x_conv * dt_full[:, None, :]
    cum_decay = jnp.cumsum(log_decay.reshape(local_heads, group_count, Q), axis=2)
    x_blocks = x_scaled.reshape(local_heads, head_dim, group_count, Q)
    scores = jnp.einsum("nci,ncj->cij", c_blocks, b_blocks, precision=highest_mode)
    lower_mask = jnp.arange(Q)[:, None] >= jnp.arange(Q)[None, :]
    log_gap = cum_decay[:, :, :, None] - cum_decay[:, :, None, :]
    weights = jnp.where(lower_mask, jnp.exp(jnp.where(lower_mask, log_gap, 0.0)), 0.0)
    inner_out = jnp.einsum(
        "hcij,hpcj->hpci", scores[None] * weights, x_blocks, precision=highest_mode
    )
    tail_weight = jnp.exp(cum_decay[:, :, -1:] - cum_decay)
    group_states = jnp.einsum(
        "hcj,hpcj,ncj->chpn", tail_weight, x_blocks, b_blocks, precision=highest_mode
    )
    group_logs = cum_decay[:, :, -1].T

    def group_step(carried, step_inputs):
        group_log, group_state = step_inputs
        return (jnp.exp(group_log)[:, None, None] * carried + group_state, carried)

    start_state = jnp.zeros((local_heads, head_dim, state_dim), jnp.float32)
    final_state, local_enter = lax.scan(group_step, start_state, (group_logs, group_states))
    device_log = jnp.sum(group_logs, axis=0)
    before_logs = jnp.cumsum(group_logs, axis=0) - group_logs
    log_all, state_all = (
        lax.all_gather(device_log[None].astype(jnp.bfloat16), "ctx", axis=0, tiled=True).astype(
            jnp.float32
        ),
        lax.all_gather(final_state[None].astype(jnp.bfloat16), "ctx", axis=0, tiled=True).astype(
            jnp.float32
        ),
    )
    my_index = lax.axis_index("ctx")
    earlier_mask = (jnp.arange(log_all.shape[0], dtype=jnp.int32) < my_index)[:, None]
    log_prefix = jnp.cumsum(log_all, axis=0)
    up_to_me = jnp.sum(jnp.where(earlier_mask, log_all, 0.0), axis=0)
    reach_weight = jnp.where(
        earlier_mask, jnp.exp(jnp.where(earlier_mask, up_to_me - log_prefix, 0.0)), 0.0
    )
    device_state = jnp.einsum("jh,jhpn->hpn", reach_weight, state_all, precision=highest_mode)
    enter_state = jnp.exp(before_logs)[:, :, None, None] * device_state[None] + local_enter
    outer_out = jnp.exp(cum_decay)[:, None] * jnp.einsum(
        "nci,chpn->hpci", c_blocks, enter_state, precision=highest_mode
    )
    ssm_out = (inner_out + outer_out).reshape(local_heads, head_dim, tok_count) + skip_now[
        :, None, None
    ] * x_conv
    gated = ssm_out * jax.nn.silu(z_in.astype(jnp.float32))
    inv_rms = lax.rsqrt(jnp.mean(gated * gated, axis=1, keepdims=True) + 1e-05)
    normed = (gated * inv_rms * gain_now).astype(jnp.bfloat16)
    out_cols = proj_out.shape[1]
    piece = lax.all_gather(normed, "row", axis=0, tiled=True)
    piece_heads = piece.shape[0]
    rows_now = proj_out.reshape(piece_heads, head_dim, out_cols)
    col_partial = jnp.einsum("hpt,hpd->td", piece, rows_now, preferred_element_type=jnp.float32)
    return lax.psum_scatter(
        col_partial.astype(jnp.bfloat16), "col", scatter_dimension=1, tiled=True
    )


def local(*args):
    tokens, proj_x, _, proj_bc, proj_dt = args[:5]
    toks, heads, lanes = tokens.shape[0], proj_dt.shape[1], proj_bc.shape[1]
    ctx_size = lax.axis_size("ctx")
    fits = (
        lax.axis_size("row") == 2
        and lax.axis_size("col") == 4
        and ctx_size & (ctx_size - 1) == 0
        and toks == Q
        and lanes == toks
        and heads % 32 == 0
        and toks % heads == 0
        and proj_x.shape[1] % (4 * lanes) == 0
        and lanes % (2 * proj_x.shape[1] // heads) == 0
    )
    return fast(*args) if fits else general(*args)


def solution(mesh):
    in_specs = (
        P("ctx", "row"),
        P("row", "col"),
        P("row", "col"),
        P("row", None),
        P("row", "col"),
        P("col"),
        P("col"),
        P("col"),
        P("col", None),
        P(),
        P("col"),
        P("col", "row"),
    )
    out_specs = P("ctx", ("row", "col"))
    return jax.shard_map(local, mesh=mesh, in_specs=in_specs, out_specs=out_specs, check_vma=False)
```

```python
import functools

import jax
import jax.numpy as jnp
from jax import lax
from jax.experimental import pallas as pl
from jax.experimental.pallas import tpu as pltpu
from jax.sharding import PartitionSpec as P

Q = 256
EPS = 1e-05
HALO = 16
MIB = 1024 * 1024
f32 = jnp.float32
bf16 = jnp.bfloat16
highest_mode = lax.Precision.HIGHEST


def mm(a, b):
    return jnp.dot(a, b, preferred_element_type=f32)


def mm_tn(a, b):
    return lax.dot_general(a, b, (((0,), (0,)), ((), ())), preferred_element_type=f32)


def mm_nt(a, b):
    return lax.dot_general(a, b, (((1,), (1,)), ((), ())), preferred_element_type=f32)


def silu(v):
    return v / (1.0 + jnp.exp(-v))


def softplus(v):
    return jnp.maximum(v, 0.0) + jnp.log(1.0 + jnp.exp(-jnp.abs(v)))


def total(mine, theirs):
    return (mine.astype(f32) + theirs.astype(f32)).astype(bf16).astype(f32)


def spread(per_head, head_dim):
    heads = per_head.shape[0]
    high = per_head.astype(bf16)
    low = (per_head - high.astype(f32)).astype(bf16)
    parts = jnp.concatenate([high.astype(f32), low.astype(f32)], axis=0).astype(bf16)
    shape = (2 * heads, heads * head_dim)
    row = lax.broadcasted_iota(jnp.int32, shape, 0) % heads
    col = lax.broadcasted_iota(jnp.int32, shape, 1) // head_dim
    return mm_tn(parts, jnp.where(row == col, 1.0, 0.0).astype(bf16))


def pick(row_vector, first, count):
    shape = (count, row_vector.shape[1])
    lane = lax.broadcasted_iota(jnp.int32, shape, 1)
    sub = lax.broadcasted_iota(jnp.int32, shape, 0)
    return jnp.sum(jnp.where(lane == sub + first, row_vector, 0.0), axis=1, keepdims=True)


def conv(ext_ref, taps, toks):
    count = taps.shape[0]
    running = None
    for tap in range(count):
        term = taps[tap : tap + 1, :] * ext_ref[pl.ds(HALO - count + 1 + tap, toks), :]
        running = term if running is None else running + term
    return running


def prefix(messages, here, state_dim):
    def parts(message):
        return message[:state_dim].astype(f32), message[state_dim : state_dim + 1].astype(f32)

    state, decay = parts(messages[0])
    enter = jnp.zeros_like(state)
    reach = jnp.ones_like(decay)
    for step, message in enumerate(messages[1:]):
        their_state, their_decay = parts(message)
        later = ((here >> step) & 1) == 1
        enter = jnp.where(later, enter + reach * their_state, enter)
        reach = jnp.where(later, reach * their_decay, reach)
        state = jnp.where(later, decay * their_state + state, their_decay * state + their_state)
        decay = decay * their_decay
    return enter, state, decay


def copies(pairs, sems):
    started = []
    for i, (source, target) in enumerate(pairs):
        now = pltpu.make_async_copy(source, target, sems.at[i])
        now.start()
        started.append(now)
    return started


def product(tok, held, waits, acc, kb):
    for i in range(tok.shape[1] // kb):
        for wait in waits[i]:
            wait.wait()
        deep = slice(i * kb, (i + 1) * kb)
        for low in range(0, acc.shape[1], 256):
            cols = slice(low, min(low + 256, acc.shape[1]))
            part = mm(tok[:, deep], held[deep, cols])
            if i == 0:
                acc[:, cols] = part
            else:
                acc[:, cols] += part


def place():
    return lax.axis_index("row"), lax.axis_index("col"), lax.axis_index("ctx")


def first_kernel(tok, w_x, w_bc, w_dt, msg, edge, held_tok, held_x, held_bc, held_dt, acc_x, acc_bc, acc_dt, sems, *, chunks, kb):
    toks, lanes = acc_bc.shape
    width = acc_x.shape[1]
    low = pl.multiple_of((1 - place()[0]) * chunks * width, width)
    parts = tok.shape[1] // kb
    pairs = []
    for i in range(parts):
        deep = pl.ds(i * kb, kb)
        pairs += [
            (tok.at[:, deep], held_tok.at[:, deep]),
            (w_x.at[deep, pl.ds(low, width)], held_x.at[deep, :]),
            (w_bc.at[deep, :], held_bc.at[deep, :]),
            (w_dt.at[:, deep], held_dt.at[:, deep]),
        ]
    started = copies(pairs, sems)
    for i in range(parts):
        for wait in started[4 * i : 4 * i + 4]:
            wait.wait()
        deep = slice(i * kb, (i + 1) * kb)
        now = held_tok[:, deep]
        for acc, part in (
            (acc_x, mm(now, held_x[deep, :])),
            (acc_bc, mm(now, held_bc[deep, :])),
            (acc_dt, mm_nt(held_dt[:, deep], now)),
        ):
            if i == 0:
                acc[...] = part
            else:
                acc[...] += part
    heads = acc_dt.shape[0]
    msg[:toks, :] = acc_bc[...].astype(bf16)
    msg[toks : toks + heads, :] = acc_dt[...].astype(bf16)
    edge[:HALO, :] = acc_bc[toks - HALO :, :].astype(bf16)
    for j in range(width // lanes):
        low = toks + heads + j * toks
        cols = slice(j * lanes, (j + 1) * lanes)
        msg[low : low + toks, :] = acc_x[:, cols].astype(bf16)
        edge[(1 + j) * HALO : (2 + j) * HALO, :] = acc_x[toks - HALO :, cols].astype(bf16)


def second_kernel(tok, w_x, edge_first, msg, mine, edge_other, edge_own, edge_in, held_tok, held, acc, sems, *, chunks, kb):
    toks, width = acc.shape
    lanes = msg.shape[1]
    row = place()[0]
    half = chunks * (msg.shape[0] // toks) * lanes
    first = width - half
    low_other = pl.multiple_of((2 - row) * half - first, lanes)
    low_own = pl.multiple_of(row * half, lanes)
    parts = tok.shape[1] // kb
    pairs = []
    for i in range(parts):
        deep = pl.ds(i * kb, kb)
        pairs += [
            (tok.at[:, deep], held_tok.at[:, deep]),
            (w_x.at[deep, pl.ds(low_other, first)], held.at[deep, pl.ds(0, first)]),
            (w_x.at[deep, pl.ds(low_own, half)], held.at[deep, pl.ds(first, half)]),
        ]
    started = copies([*pairs, (edge_first, edge_in)], sems)
    product(held_tok, held, [started[3 * i : 3 * i + 3] for i in range(parts)], acc, kb)
    started[-1].wait()
    per = msg.shape[0] // toks
    base = edge_in.shape[0]
    edge_other[:base, :] = edge_in[...]
    edge_own[:HALO, :] = edge_in[:HALO, :]
    for j in range(width // lanes):
        now = acc[:, j * lanes : (j + 1) * lanes].astype(bf16)
        if j < per:
            msg[j * toks : (j + 1) * toks, :] = now
            edge_other[base + j * HALO : base + (j + 1) * HALO, :] = now[toks - HALO :, :]
        else:
            i = j - per
            mine[i * toks : (i + 1) * toks, :] = now
            edge_own[(i + 1) * HALO : (i + 2) * HALO, :] = now[toks - HALO :, :]


def gate_product_kernel(tok, weight, *refs, kb):
    *outs, tok_out, held, acc, sems = refs
    toks, width = acc.shape
    lanes = outs[0].shape[1]
    low = pl.multiple_of((1 - place()[0]) * width, width)
    parts = tok.shape[1] // kb
    pairs = []
    for i in range(parts):
        deep = pl.ds(i * kb, kb)
        pairs += [
            (tok.at[:, deep], tok_out.at[:, deep]),
            (weight.at[deep, pl.ds(low, width)], held.at[deep, :]),
        ]
    started = copies(pairs, sems)
    product(tok_out, held, [started[2 * i : 2 * i + 2] for i in range(parts)], acc, kb)
    per = width // lanes // len(outs)
    for j in range(width // lanes):
        at_row = j % per * toks
        outs[j // per][at_row : at_row + toks, :] = acc[:, j * lanes : (j + 1) * lanes].astype(bf16)


def rows_of(weight, target, low, lanes):
    return [
        (weight.at[pl.ds(low + i * lanes, lanes), :], target.at[pl.ds(i * lanes, lanes), :])
        for i in range(target.shape[0] // lanes)
    ]


def rows_of(weight, target, low, lanes):
    return [
        (weight.at[pl.ds(low + i * lanes, lanes), :], target.at[pl.ds(i * lanes, lanes), :])
        for i in range(target.shape[0] // lanes)
    ]


def inner_kernel(scores, skip, scaled, conv_out, cum, cum_t, out, *, chunk, chunks, head_dim):
    heads = scaled.shape[1] // head_dim
    within(
        place(), scores, scaled, conv_out, cum, cum_t, skip, out,
        head_dim=head_dim, first_of=chunk * heads, local_heads=chunks * heads,
    )


def own_gate_kernel(tok, weight, w_out, mine, w_own, held, acc, sems, *, kb):
    toks, width = acc.shape
    lanes = mine.shape[1]
    row = place()[0]
    low = pl.multiple_of(row * width, width)
    parts = tok.shape[1] // kb
    pairs = [
        (weight.at[pl.ds(i * kb, kb), pl.ds(low, width)], held.at[pl.ds(i * kb, kb), :])
        for i in range(parts)
    ]
    pairs += rows_of(w_out, w_own, pl.multiple_of(row * width, lanes), lanes)
    started = copies(pairs, sems)
    product(tok, held, [[now] for now in started[:parts]], acc, kb)
    for j in range(width // lanes):
        mine[j * toks : (j + 1) * toks, :] = acc[:, j * lanes : (j + 1) * lanes].astype(bf16)
    for now in started[parts:]:
        now.wait()


def state_kernel(
    *refs, first, chunk, chunks, head_dim, state_dim, toks, lanes
):
    refs = list(refs)
    if not first:
        bc_in = refs.pop(0)
    mine, theirs, x_mine, x_theirs, edge_a, edge_b, taps_x, taps_bc, bias, decay = refs[:10]
    refs = refs[10:]
    if first:
        bc_out, scores = refs.pop(0), refs.pop(0)
    msg, scaled, conv_out, cum_out, cum_t_out, ext = refs
    row, _, here = place()
    blocks = x_mine.shape[0] // toks // chunks
    heads = blocks * lanes // head_dim
    local_heads = heads * chunks
    inside = jnp.where(here > 0, 1.0, 0.0)

    def halo(block):
        low = block * HALO
        return total(edge_a[low : low + HALO, :], edge_b[low : low + HALO, :]) * inside

    if first:
        ext[:HALO, :] = halo(0)
        ext[HALO:, :] = total(mine[:toks, :], theirs[:toks, :])
        bc_now = silu(conv(ext, taps_bc[...], toks)).astype(bf16)
        bc_out[...] = bc_now
        b_now = bc_now[:, :state_dim]
        products = mm_nt(bc_now[:, state_dim:], b_now)
        shape = (toks, toks)
        lower = lax.broadcasted_iota(jnp.int32, shape, 0) >= lax.broadcasted_iota(jnp.int32, shape, 1)
        scores[...] = jnp.where(lower, products, 0.0)
    else:
        b_now = bc_in[:, :state_dim]

    low = pl.multiple_of(toks + row * local_heads, local_heads)
    dt_sum = total(mine[pl.ds(low, local_heads), :], theirs[pl.ds(low, local_heads), :])
    dt_sum = dt_sum[chunk * heads : (chunk + 1) * heads]
    first_head = row * local_heads + chunk * heads
    dt_now = softplus(dt_sum + pick(bias[...], first_head, heads))
    log_decay = -pick(decay[...], first_head, heads) * dt_now
    shape = (toks, toks)
    upper = lax.broadcasted_iota(jnp.int32, shape, 0) <= lax.broadcasted_iota(jnp.int32, shape, 1)
    cum = lax.dot_general(
        log_decay,
        jnp.where(upper, 1.0, 0.0),
        (((1,), (0,)), ((), ())),
        precision=highest_mode,
        preferred_element_type=f32,
    )
    last = cum[:, toks - 1 : toks]
    cum_out[...] = cum
    cum_t_out[...] = cum.T
    dt_wide = spread(dt_now, head_dim)
    tail_wide = spread(dt_now * jnp.exp(last - cum), head_dim)
    through = spread(jnp.exp(jnp.broadcast_to(last, (heads, HALO))), head_dim)
    rows = state_dim + HALO
    x_low = x_theirs.shape[0] - blocks * toks
    taps_low = (row * chunks + chunk) * blocks * lanes
    for j in range(blocks):
        ext[:HALO, :] = halo(1 + chunk * blocks + j)
        ext[HALO:, :] = total(
            x_mine[(chunk * blocks + j) * toks : (chunk * blocks + j + 1) * toks, :],
            x_theirs[x_low + j * toks : x_low + (j + 1) * toks, :],
        )
        cols = slice(j * lanes, (j + 1) * lanes)
        x_now = silu(conv(ext, taps_x[:, pl.ds(pl.multiple_of(taps_low + j * lanes, lanes), lanes)], toks))
        conv_out[:, cols] = x_now.astype(bf16)
        scaled[:, cols] = (x_now * dt_wide[:, cols]).astype(bf16)
        state = mm_tn(b_now, (x_now * tail_wide[:, cols]).astype(bf16))
        msg[j * rows : j * rows + state_dim, :] = state.astype(bf16)
        msg[j * rows + state_dim : (j + 1) * rows, :] = through[:, cols].astype(bf16)


def combine_kernel(*refs, state_dim, lanes):
    *messages, out = refs
    rows = state_dim + HALO
    for j in range(out.shape[0] // rows):
        now = [m[j * rows : (j + 1) * rows, :] for m in messages]
        _, state, decay = prefix(now, place()[2], state_dim)
        out[j * rows : j * rows + state_dim, :] = state.astype(bf16)
        out[j * rows + state_dim : (j + 1) * rows, :] = jnp.broadcast_to(decay, (HALO, lanes)).astype(bf16)


def within(where, scores, scaled, conv_out, cum, cum_t, skip, out, *, head_dim, first_of, local_heads):
    toks, channels = scaled.shape
    pair = 2 * head_dim
    half = toks // 2
    heads = channels // head_dim
    skip_now = pick(skip[...], where[0] * local_heads + first_of, heads)
    skip_wide = spread(jnp.broadcast_to(skip_now, (heads, HALO)), head_dim)[:1, :]
    left = lax.broadcasted_iota(jnp.int32, (toks, pair), 1) < head_dim
    zero = jnp.zeros((toks, pair), bf16)
    for p in range(heads // 2):
        cols = slice(p * pair, (p + 1) * pair)
        x_pair = scaled[:, cols]
        top = None
        for side in range(2):
            h = 2 * p + side
            x_now = jnp.where(left, x_pair, zero) if side == 0 else jnp.where(left, zero, x_pair)
            gap_top = jnp.minimum(cum_t[:half, h : h + 1] - cum[h : h + 1, :half], 0.0)
            gap_low = jnp.minimum(cum_t[half:, h : h + 1] - cum[h : h + 1, :], 0.0)
            w_top = (jnp.exp(gap_top) * scores[:half, :half]).astype(bf16)
            w_low = (jnp.exp(gap_low) * scores[half:, :]).astype(bf16)
            part_top = mm(w_top, x_now[:half])
            part_low = mm(w_low, x_now)
            top = part_top if top is None else top + part_top
            low = part_low if side == 0 else low + part_low
        skips = skip_wide[:, cols]
        out[:half, cols] = top + skips * conv_out[:half, cols].astype(f32)
        out[half:, cols] = low + skips * conv_out[half:, cols].astype(f32)


def gate_kernel(inner, bc, cum, z_mine, z_theirs, gain, *refs, messages, bounds, chunk, chunks, head_dim, state_dim, lanes):
    messages, outs = refs[:messages], refs[messages:]
    toks = inner.shape[0]
    row, _, here = place()
    gain_low = (row * chunks + chunk) * inner.shape[1]
    rows = state_dim + HALO
    grown = spread(jnp.exp(cum[...]), head_dim)
    c_now = bc[:, state_dim:]
    wide = 2 * head_dim
    shape = (wide, wide)
    same = (lax.broadcasted_iota(jnp.int32, shape, 0) // head_dim) == (
        lax.broadcasted_iota(jnp.int32, shape, 1) // head_dim
    )
    mean_of = jnp.where(same, 1.0 / head_dim, 0.0).astype(bf16)
    for j in range(inner.shape[1] // lanes):
        now = [m[j * rows : (j + 1) * rows, :] for m in messages]
        enter, _, _ = prefix(now, here, state_dim)
        cols = slice(j * lanes, (j + 1) * lanes)
        scanned = inner[:, cols] + grown[:, cols] * mm(c_now, enter.astype(bf16))
        z_low = (chunk * inner.shape[1] // lanes + j) * toks
        z_now = total(z_mine[z_low : z_low + toks, :], z_theirs[j * toks : (j + 1) * toks, :])
        gated = scanned * silu(z_now)
        square = gated * gated
        for i in range(lanes // wide):
            part = square[:, i * wide : (i + 1) * wide]
            high = part.astype(bf16)
            rest = (part - high.astype(f32)).astype(bf16)
            mean = mm(high, mean_of) + mm(rest, mean_of)
            low = j * lanes + i * wide
            done = (
                gated[:, i * wide : (i + 1) * wide]
                * lax.rsqrt(mean + EPS)
                * gain[:, pl.ds(pl.multiple_of(gain_low + low, wide), wide)]
            ).astype(bf16)
            for (start, end), out in zip(bounds, outs):
                size = end - start
                out[j * size : (j + 1) * size, i * wide : (i + 1) * wide] = done[start:end]


def own_kernel(weight, w_first, *refs, cuts):
    *normed, partial, rest, w_last, whole, sems = refs
    lanes = normed[0].shape[1]
    half = rest.shape[0]
    row = place()[0]
    first = w_first.shape[0]
    pairs = rows_of(weight, w_last, pl.multiple_of(row * half + first, lanes), lanes)
    needed = len(pairs)
    pairs += rows_of(weight, rest, pl.multiple_of((1 - row) * half, lanes), lanes)
    started = copies(pairs, sems)
    for now in started[:needed]:
        now.wait()

    @pl.when(row >= 0)
    def _():
        own_product(w_first, w_last, normed, partial, whole, cuts)

    for now in started[needed:]:
        now.wait()


def own_product(w_first, w_last, normed, partial, whole, cuts):
    cut_row = w_first.shape[0]
    width = partial.shape[1]
    lanes = normed[0].shape[1]
    low = whole.shape[1]
    for cut in cuts[::-1]:
        parts, normed = normed[: len(cut)], normed[len(cut) :]
        blocks = parts[0].shape[0] // (cut[0][1] - cut[0][0])
        low -= blocks * lanes
        for j in range(blocks):
            for (start, end), part in zip(cut, parts):
                size = end - start
                whole[start:end, low + j * lanes : low + (j + 1) * lanes] = part[j * size : (j + 1) * size, :]
    for low in range(0, width, 512):
        cols = slice(low, min(low + 512, width))
        partial[:, cols] = mm(whole[:, :cut_row], w_first[:, cols]) + mm(whole[:, cut_row:], w_last[:, cols])


def rest_kernel(partial, rest, *refs, start, end, far):
    *normed, send, keep = refs
    lanes = normed[0].shape[1]
    piece = send.shape[1]
    size = end - start
    step = min(512, piece)
    blocks = rest.shape[0] // lanes // len(normed)
    _, col, _ = place()
    pair = 1 - col // 2 if far else col // 2
    for target, core in ((send, 1 - col % 2), (keep, col % 2)):
        base = (pair * 2 + core) * piece
        for low in range(0, piece, step):
            cols = pl.ds(pl.multiple_of(base + low, step), step)
            acc = partial[start:end, cols]
            row = 0
            for chunk in normed[::-1]:
                held_toks = chunk.shape[0] // blocks
                first = start if held_toks > size else 0
                for j in range(blocks):
                    now = chunk[j * held_toks + first : j * held_toks + first + size, :]
                    acc = acc + mm(now, rest[row : row + lanes, cols])
                    row += lanes
            target[:, low : low + step] = acc.astype(bf16)


def final_kernel(*refs, bounds):
    *parts, out = refs
    for i, (start, end) in enumerate(bounds):
        far, keep, got = parts[3 * i : 3 * i + 3]
        total_now = far[...].astype(f32) + keep[...].astype(f32) + got[...].astype(f32)
        out[start:end, :] = total_now.astype(bf16)


def sds(*shape, dtype=bf16):
    return jax.ShapeDtypeStruct(shape, dtype)


def call(kernel, args, specs, outs, scratch=(), name=None, mib=16, after=()):
    used = len(args)

    def body(*refs):
        kernel(*refs[:used], *refs[used + len(after) :])

    return pl.pallas_call(
        body,
        in_specs=[*(specs or [IN_VMEM] * used), *[pl.BlockSpec(memory_space=pl.ANY)] * len(after)],
        out_specs=[IN_VMEM] * len(outs),
        scratch_shapes=list(scratch),
        out_shape=outs,
        compiler_params=pltpu.CompilerParams(vmem_limit_bytes=int(mib * MIB)),
        cost_estimate=pl.CostEstimate(flops=0, bytes_accessed=0, transcendentals=0),
        name=name,
    )(*args, *after)


IN_VMEM = pl.BlockSpec(memory_space=pltpu.VMEM)
IN_HBM = pl.BlockSpec(memory_space=pltpu.HBM)


def swapped(shard, axis, by):
    devices = lax.axis_size(axis)
    return lax.ppermute(shard, axis, [(i, i ^ by) for i in range(devices)])


def fast(
    tokens, proj_x, proj_z, proj_bc, proj_dt, dt_bias, decay_rate, skip_gain,
    conv_x, conv_bc, norm_gain, proj_out,
):
    toks, depth = tokens.shape
    heads = proj_dt.shape[1]
    head_dim = proj_x.shape[1] // heads
    lanes = proj_bc.shape[1]
    state_dim = lanes // 2
    taps = conv_bc.shape[1]
    local_heads = heads // 2
    half = local_heads * head_dim
    chunks = 2
    width = half // chunks
    blocks = width // lanes
    chunk_heads = local_heads // chunks
    out_cols = proj_out.shape[1]
    ctx_size = lax.axis_size("ctx")
    conv_x_t, conv_bc_t, proj_dt_t = conv_x.T, conv_bc.T, proj_dt.T
    bias, decay, skip, gain = (v[None] for v in (dt_bias, decay_rate, skip_gain, norm_gain))

    kb = depth // 8
    parts = depth // kb
    edge_rows = (1 + chunks * blocks) * HALO
    msg_first, edge_first = call(
        functools.partial(first_kernel, chunks=chunks, kb=kb),
        (tokens, proj_x, proj_bc, proj_dt_t),
        [IN_HBM] * 4,
        [sds(toks + heads + blocks * toks, lanes), sds((1 + blocks) * HALO, lanes)],
        [
            pltpu.VMEM((toks, depth), bf16),
            pltpu.VMEM((depth, width), bf16),
            pltpu.VMEM((depth, lanes), bf16),
            pltpu.VMEM((heads, depth), bf16),
            pltpu.VMEM((toks, width), f32),
            pltpu.VMEM((toks, lanes), f32),
            pltpu.VMEM((heads, toks), f32),
            pltpu.SemaphoreType.DMA((4 * parts,)),
        ],
        name="first",
        mib=53.9,
    )
    first_got = swapped(msg_first, "row", 1)
    msg_second, x_mine, edge_other, edge_own = call(
        functools.partial(second_kernel, chunks=chunks, kb=kb),
        (tokens, proj_x, edge_first),
        [IN_HBM] * 3,
        [sds(blocks * toks, lanes), sds(chunks * blocks * toks, lanes), *[sds(edge_rows, lanes)] * 2],
        [
            pltpu.VMEM(edge_first.shape, bf16),
            pltpu.VMEM((toks, depth), bf16),
            pltpu.VMEM((depth, width + half), bf16),
            pltpu.VMEM((toks, width + half), f32),
            pltpu.SemaphoreType.DMA((3 * parts + 1,)),
        ],
        name="second",
        mib=52,
    )
    second_got = swapped(msg_second, "row", 1)
    down = [(i, (i + 1) % ctx_size) for i in range(ctx_size)]
    edge_a = lax.ppermute(
        edge_other, ("ctx", "row"), [(2 * i + s, 2 * j + 1 - s) for i, j in down for s in range(2)]
    )
    edge_b = lax.ppermute(edge_own, "ctx", down)
    *z_send, tok_held = call(
        functools.partial(gate_product_kernel, kb=kb),
        (tokens, proj_z),
        [IN_HBM] * 2,
        [*[sds(blocks * toks, lanes)] * chunks, sds(toks, depth)],
        [
            pltpu.VMEM((depth, half), bf16),
            pltpu.VMEM((toks, half), f32),
            pltpu.SemaphoreType.DMA((2 * parts,)),
        ],
        name="z_other",
        mib=50,
        after=(edge_own,),
    )

    rows = state_dim + HALO
    sizes = dict(head_dim=head_dim, state_dim=state_dim, lanes=lanes)
    states, scans = [], []
    bc_now = scores = None
    for c in range(chunks):
        args = [] if c == 0 else [bc_now]
        args += [
            msg_first, first_got, x_mine, first_got if c == 0 else second_got, edge_a, edge_b,
            conv_x_t, conv_bc_t, bias, decay,
        ]
        outs = [sds(toks, lanes), sds(toks, toks, dtype=f32)] if c == 0 else []
        outs += [
            sds(blocks * rows, lanes),
            sds(toks, width),
            sds(toks, width),
            sds(chunk_heads, toks, dtype=f32),
            sds(toks, chunk_heads, dtype=f32),
        ]
        got = call(
            functools.partial(
                state_kernel, first=c == 0, chunk=c, chunks=chunks, toks=toks, **sizes
            ),
            args,
            None,
            outs,
            [pltpu.VMEM((HALO + toks, lanes), f32)],
            name="state",
            after=(z_send[0],),
        )
        if c == 0:
            bc_now, scores, *got = got
        states.append(got[0])
        scans.append(got[1:])

    z_send, _ = lax.optimization_barrier((z_send, states))
    z_got = [swapped(z, "row", 1) for z in z_send]
    def inner_call(c):
        (inner,) = call(
            functools.partial(inner_kernel, chunk=c, chunks=chunks, head_dim=head_dim),
            (scores, skip, *scans[c]),
            None,
            [sds(toks, width, dtype=f32)],
            name="inner",
            after=sent[:1],
        )
        return inner

    messages, sent, inners = [], [], []
    for c in range(chunks):
        if c == 1:
            inners = [inner_call(i) for i in range(chunks)]
        heard = [states[c]]
        send = states[c]
        by = 1
        while by < ctx_size:
            if by > 1:
                (send,) = call(
                    functools.partial(combine_kernel, state_dim=state_dim, lanes=lanes),
                    heard, None, [sds(*send.shape)], name="combine", after=(*sent, *inners),
                )
            heard.append(swapped(send, "ctx", by))
            by *= 2
        messages.append(heard)
        sent.append(send)
    early = half // 2
    z_mine, w_first = call(
        functools.partial(own_gate_kernel, kb=kb),
        (tok_held, proj_z, proj_out),
        [IN_VMEM, IN_HBM, IN_HBM],
        [sds(chunks * blocks * toks, lanes), sds(early, out_cols)],
        [
            pltpu.VMEM((depth, half), bf16),
            pltpu.VMEM((toks, half), f32),
            pltpu.SemaphoreType.DMA((parts + early // lanes,)),
        ],
        name="z_own",
        mib=38,
        after=(*sent, *inners),
    )

    normed, normed_got = [], []
    bounds = ((0, toks // 2), (toks // 2, toks))
    cuts = [((0, toks),)] * (chunks - 1) + [bounds]
    for c in range(chunks):
        now = call(
            functools.partial(
                gate_kernel, messages=len(messages[c]), bounds=cuts[c], chunk=c, chunks=chunks, **sizes
            ),
            (inners[c], bc_now, scans[c][2], z_mine, z_got[c], gain, *messages[c]),
            None,
            [sds(blocks * (end - start), lanes) for start, end in cuts[c]],
            name="gate",
        )
        normed.append(now)
        normed_got.append([swapped(part, "row", 1) for part in now])

    piece = out_cols // lax.axis_size("col")
    partial, rest = call(
        functools.partial(own_kernel, cuts=cuts),
        (proj_out, w_first, *[part for now in normed[::-1] for part in now]),
        [IN_HBM, *[IN_VMEM] * (1 + sum(len(cut) for cut in cuts))],
        [sds(toks, out_cols, dtype=f32), sds(half, out_cols)],
        [
            pltpu.VMEM((half - early, out_cols), bf16),
            pltpu.VMEM((toks, half), bf16),
            pltpu.SemaphoreType.DMA(((2 * half - early) // lanes,)),
        ],
        name="out_own",
        mib=34,
    )

    def out_rest(part, far, after):
        start, end = bounds[part]
        args = (partial, rest, *[now[min(part, len(now) - 1)] for now in normed_got[::-1]])
        return call(
            functools.partial(rest_kernel, start=start, end=end, far=far),
            args,
            None,
            [sds(end - start, piece)] * 2,
            name="out_far" if far else "out_near",
            after=after,
        )

    def added(a, b):
        return (a.astype(f32) + b.astype(f32)).astype(bf16)

    sends, sums, keep = [], [], None
    for part in range(len(bounds)):
        send, far_keep = out_rest(part, True, () if keep is None else (keep,))
        sums.append(added(far_keep, swapped(send, "col", 1)))
        send, keep = out_rest(part, False, (far_keep,))
        sends.append((send, keep))
    args = []
    for far, (send, keep) in zip(sums, sends):
        args += [swapped(far, "col", 2), keep, swapped(send, "col", 1)]
    (out,) = call(
        functools.partial(final_kernel, bounds=bounds), args, None, [sds(toks, piece)], name="final"
    )
    return out


def shifted(shard, axis, by):
    devices = lax.axis_size(axis)
    pairs = [(i, i + by) for i in range(devices) if 0 <= i + by < devices]
    return lax.ppermute(shard, axis, pairs)


def general(
    tokens,
    proj_x,
    proj_z,
    proj_bc,
    proj_dt,
    dt_bias,
    decay_rate,
    skip_gain,
    conv_x,
    conv_bc,
    norm_gain,
    proj_out,
):
    tok_count = tokens.shape[0]
    col_heads = proj_dt.shape[1]
    head_dim = proj_x.shape[1] // col_heads
    state_dim = proj_bc.shape[1] // 2
    tap_count = conv_bc.shape[1]
    group_count = tok_count // Q
    bc_term = jnp.einsum("dc,td->ct", proj_bc, tokens, preferred_element_type=jnp.float32)
    local_heads = col_heads // lax.axis_size("row")
    first_head = lax.axis_index("row") * local_heads
    x_part = jnp.einsum("dc,td->ct", proj_x, tokens, preferred_element_type=jnp.float32).reshape(
        local_heads * lax.axis_size("row"), head_dim, tok_count
    )
    z_part = jnp.einsum("dc,td->ct", proj_z, tokens, preferred_element_type=jnp.float32).reshape(
        local_heads * lax.axis_size("row"), head_dim, tok_count
    )
    dt_part = jnp.einsum("dc,td->ct", proj_dt, tokens, preferred_element_type=jnp.float32).reshape(
        local_heads * lax.axis_size("row"), 1, tok_count
    )
    head_sum = lax.psum_scatter(
        jnp.concatenate([x_part, z_part, dt_part], axis=1).astype(jnp.bfloat16),
        "row",
        scatter_dimension=0,
        tiled=True,
    )
    bc_sum = lax.psum(bc_term.astype(jnp.bfloat16), "row")
    channels = local_heads * head_dim
    z_in = head_sum[:, head_dim : 2 * head_dim]
    dt_in = head_sum[:, 2 * head_dim]
    flat_in = jnp.concatenate([head_sum[:, :head_dim].reshape(channels, tok_count), bc_sum], axis=0)
    prior = shifted(flat_in[:, tok_count - tap_count + 1 :], "ctx", 1)
    padded = jnp.concatenate([prior, flat_in], axis=1).astype(jnp.float32)
    kernel = jnp.concatenate(
        [lax.dynamic_slice_in_dim(conv_x, first_head * head_dim, channels, 0), conv_bc], axis=0
    )
    running = jnp.zeros(flat_in.shape, jnp.float32)
    for tap_index in range(tap_count):
        running = (
            running
            + kernel[:, tap_index : tap_index + 1] * padded[:, tap_index : tap_index + tok_count]
        )
    conv_out = jax.nn.silu(running)
    x_conv = conv_out[:channels].reshape(local_heads, head_dim, tok_count)
    b_blocks = conv_out[channels : channels + state_dim].reshape(state_dim, group_count, Q)
    c_blocks = conv_out[channels + state_dim :].reshape(state_dim, group_count, Q)
    bias_now = lax.dynamic_slice_in_dim(dt_bias, first_head, local_heads, 0)
    decay_now = lax.dynamic_slice_in_dim(decay_rate, first_head, local_heads, 0)
    skip_now = lax.dynamic_slice_in_dim(skip_gain, first_head, local_heads, 0)
    gain_now = lax.dynamic_slice_in_dim(norm_gain, first_head * head_dim, channels, 0).reshape(
        local_heads, head_dim, 1
    )
    dt_full = jax.nn.softplus(dt_in.astype(jnp.float32) + bias_now[:, None])
    log_decay = -decay_now[:, None] * dt_full
    x_scaled = x_conv * dt_full[:, None, :]
    cum_decay = jnp.cumsum(log_decay.reshape(local_heads, group_count, Q), axis=2)
    x_blocks = x_scaled.reshape(local_heads, head_dim, group_count, Q)
    scores = jnp.einsum("nci,ncj->cij", c_blocks, b_blocks, precision=highest_mode)
    lower_mask = jnp.arange(Q)[:, None] >= jnp.arange(Q)[None, :]
    log_gap = cum_decay[:, :, :, None] - cum_decay[:, :, None, :]
    weights = jnp.where(lower_mask, jnp.exp(jnp.where(lower_mask, log_gap, 0.0)), 0.0)
    inner_out = jnp.einsum(
        "hcij,hpcj->hpci", scores[None] * weights, x_blocks, precision=highest_mode
    )
    tail_weight = jnp.exp(cum_decay[:, :, -1:] - cum_decay)
    group_states = jnp.einsum(
        "hcj,hpcj,ncj->chpn", tail_weight, x_blocks, b_blocks, precision=highest_mode
    )
    group_logs = cum_decay[:, :, -1].T

    def group_step(carried, step_inputs):
        group_log, group_state = step_inputs
        return (jnp.exp(group_log)[:, None, None] * carried + group_state, carried)

    start_state = jnp.zeros((local_heads, head_dim, state_dim), jnp.float32)
    final_state, local_enter = lax.scan(group_step, start_state, (group_logs, group_states))
    device_log = jnp.sum(group_logs, axis=0)
    before_logs = jnp.cumsum(group_logs, axis=0) - group_logs
    log_all, state_all = (
        lax.all_gather(device_log[None].astype(jnp.bfloat16), "ctx", axis=0, tiled=True).astype(
            jnp.float32
        ),
        lax.all_gather(final_state[None].astype(jnp.bfloat16), "ctx", axis=0, tiled=True).astype(
            jnp.float32
        ),
    )
    my_index = lax.axis_index("ctx")
    earlier_mask = (jnp.arange(log_all.shape[0], dtype=jnp.int32) < my_index)[:, None]
    log_prefix = jnp.cumsum(log_all, axis=0)
    up_to_me = jnp.sum(jnp.where(earlier_mask, log_all, 0.0), axis=0)
    reach_weight = jnp.where(
        earlier_mask, jnp.exp(jnp.where(earlier_mask, up_to_me - log_prefix, 0.0)), 0.0
    )
    device_state = jnp.einsum("jh,jhpn->hpn", reach_weight, state_all, precision=highest_mode)
    enter_state = jnp.exp(before_logs)[:, :, None, None] * device_state[None] + local_enter
    outer_out = jnp.exp(cum_decay)[:, None] * jnp.einsum(
        "nci,chpn->hpci", c_blocks, enter_state, precision=highest_mode
    )
    ssm_out = (inner_out + outer_out).reshape(local_heads, head_dim, tok_count) + skip_now[
        :, None, None
    ] * x_conv
    gated = ssm_out * jax.nn.silu(z_in.astype(jnp.float32))
    inv_rms = lax.rsqrt(jnp.mean(gated * gated, axis=1, keepdims=True) + 1e-05)
    normed = (gated * inv_rms * gain_now).astype(jnp.bfloat16)
    out_cols = proj_out.shape[1]
    piece = lax.all_gather(normed, "row", axis=0, tiled=True)
    piece_heads = piece.shape[0]
    rows_now = proj_out.reshape(piece_heads, head_dim, out_cols)
    col_partial = jnp.einsum("hpt,hpd->td", piece, rows_now, preferred_element_type=jnp.float32)
    return lax.psum_scatter(
        col_partial.astype(jnp.bfloat16), "col", scatter_dimension=1, tiled=True
    )


def local(*args):
    tokens, proj_x, _, proj_bc, proj_dt = args[:5]
    toks, heads, lanes = tokens.shape[0], proj_dt.shape[1], proj_bc.shape[1]
    ctx_size = lax.axis_size("ctx")
    fits = (
        lax.axis_size("row") == 2
        and lax.axis_size("col") == 4
        and ctx_size & (ctx_size - 1) == 0
        and toks == Q
        and lanes == toks
        and heads % 32 == 0
        and toks % heads == 0
        and proj_x.shape[1] % (4 * lanes) == 0
        and lanes % (2 * proj_x.shape[1] // heads) == 0
    )
    return fast(*args) if fits else general(*args)


def solution(mesh):
    in_specs = (
        P("ctx", "row"),
        P("row", "col"),
        P("row", "col"),
        P("row", None),
        P("row", "col"),
        P("col"),
        P("col"),
        P("col"),
        P("col", None),
        P(),
        P("col"),
        P("col", "row"),
    )
    out_specs = P("ctx", ("row", "col"))
    return jax.shard_map(local, mesh=mesh, in_specs=in_specs, out_specs=out_specs, check_vma=False)
```

```python
import functools

import jax
import jax.numpy as jnp
from jax import lax
from jax.experimental import pallas as pl
from jax.experimental.pallas import tpu as pltpu
from jax.sharding import PartitionSpec as P

Q = 256
EPS = 1e-05
HALO = 16
MIB = 1024 * 1024
f32 = jnp.float32
bf16 = jnp.bfloat16
highest_mode = lax.Precision.HIGHEST


def mm(a, b):
    return jnp.dot(a, b, preferred_element_type=f32)


def mm_tn(a, b):
    return lax.dot_general(a, b, (((0,), (0,)), ((), ())), preferred_element_type=f32)


def mm_nt(a, b):
    return lax.dot_general(a, b, (((1,), (1,)), ((), ())), preferred_element_type=f32)


def silu(v):
    return v / (1.0 + jnp.exp(-v))


def softplus(v):
    return jnp.maximum(v, 0.0) + jnp.log(1.0 + jnp.exp(-jnp.abs(v)))


def total(mine, theirs):
    return (mine.astype(f32) + theirs.astype(f32)).astype(bf16).astype(f32)


def spread(per_head, head_dim):
    heads = per_head.shape[0]
    high = per_head.astype(bf16)
    low = (per_head - high.astype(f32)).astype(bf16)
    parts = jnp.concatenate([high.astype(f32), low.astype(f32)], axis=0).astype(bf16)
    shape = (2 * heads, heads * head_dim)
    row = lax.broadcasted_iota(jnp.int32, shape, 0) % heads
    col = lax.broadcasted_iota(jnp.int32, shape, 1) // head_dim
    return mm_tn(parts, jnp.where(row == col, 1.0, 0.0).astype(bf16))


def pick(row_vector, first, count):
    shape = (count, row_vector.shape[1])
    lane = lax.broadcasted_iota(jnp.int32, shape, 1)
    sub = lax.broadcasted_iota(jnp.int32, shape, 0)
    return jnp.sum(jnp.where(lane == sub + first, row_vector, 0.0), axis=1, keepdims=True)


def conv(ext_ref, taps, toks):
    count = taps.shape[0]
    running = None
    for tap in range(count):
        term = taps[tap : tap + 1, :] * ext_ref[pl.ds(HALO - count + 1 + tap, toks), :]
        running = term if running is None else running + term
    return running


def block_of(message, block, blocks, state_dim):
    decays = message[blocks * state_dim :, :].astype(f32)
    state = message[block * state_dim : (block + 1) * state_dim, :].astype(f32)
    return state, decays[block : block + 1]


def decay_rows(decays):
    row = lax.broadcasted_iota(jnp.int32, (HALO, decays[0].shape[1]), 0)
    rows = jnp.zeros((HALO, decays[0].shape[1]), f32)
    for j, decay in enumerate(decays):
        rows = jnp.where(row == j, decay, rows)
    return rows.astype(bf16)


def prefix(messages, here):
    state, decay = messages[0]
    enter = jnp.zeros_like(state)
    reach = jnp.ones_like(decay)
    for step, (their_state, their_decay) in enumerate(messages[1:]):
        later = ((here >> step) & 1) == 1
        enter = jnp.where(later, enter + reach * their_state, enter)
        reach = jnp.where(later, reach * their_decay, reach)
        state = jnp.where(later, decay * their_state + state, their_decay * state + their_state)
        decay = decay * their_decay
    return enter, state, decay


def copies(pairs, sems):
    started = []
    for i, (source, target) in enumerate(pairs):
        now = pltpu.make_async_copy(source, target, sems.at[i])
        now.start()
        started.append(now)
    return started


def product(tok, held, waits, acc, kb):
    for i in range(tok.shape[1] // kb):
        for wait in waits[i]:
            wait.wait()
        deep = slice(i * kb, (i + 1) * kb)
        for low in range(0, acc.shape[1], 256):
            cols = slice(low, min(low + 256, acc.shape[1]))
            part = mm(tok[:, deep], held[deep, cols])
            if i == 0:
                acc[:, cols] = part
            else:
                acc[:, cols] += part


def place():
    return lax.axis_index("row"), lax.axis_index("col"), lax.axis_index("ctx")


def first_kernel(tok, w_x, w_bc, w_dt, msg, edge, held_tok, held_x, held_bc, held_dt, acc_x, acc_bc, acc_dt, sems, *, chunks, kb):
    toks, lanes = acc_bc.shape
    width = acc_x.shape[1]
    low = pl.multiple_of((1 - place()[0]) * chunks * width, width)
    parts = tok.shape[1] // kb
    pairs = []
    for i in range(parts):
        deep = pl.ds(i * kb, kb)
        pairs += [
            (tok.at[:, deep], held_tok.at[:, deep]),
            (w_x.at[deep, pl.ds(low, width)], held_x.at[deep, :]),
            (w_bc.at[deep, :], held_bc.at[deep, :]),
            (w_dt.at[:, deep], held_dt.at[:, deep]),
        ]
    started = copies(pairs, sems)
    for i in range(parts):
        for wait in started[4 * i : 4 * i + 4]:
            wait.wait()
        deep = slice(i * kb, (i + 1) * kb)
        now = held_tok[:, deep]
        for acc, part in (
            (acc_x, mm(now, held_x[deep, :])),
            (acc_bc, mm(now, held_bc[deep, :])),
            (acc_dt, mm_nt(held_dt[:, deep], now)),
        ):
            if i == 0:
                acc[...] = part
            else:
                acc[...] += part
    heads = acc_dt.shape[0]
    msg[:toks, :] = acc_bc[...].astype(bf16)
    msg[toks : toks + heads, :] = acc_dt[...].astype(bf16)
    edge[:HALO, :] = acc_bc[toks - HALO :, :].astype(bf16)
    for j in range(width // lanes):
        low = toks + heads + j * toks
        cols = slice(j * lanes, (j + 1) * lanes)
        msg[low : low + toks, :] = acc_x[:, cols].astype(bf16)
        edge[(1 + j) * HALO : (2 + j) * HALO, :] = acc_x[toks - HALO :, cols].astype(bf16)


def second_kernel(tok, w_x, edge_first, msg, mine, edge_other, edge_own, edge_in, held_tok, held, acc, sems, *, chunks, kb):
    toks, width = acc.shape
    lanes = msg.shape[1]
    row = place()[0]
    half = chunks * (msg.shape[0] // toks) * lanes
    first = width - half
    low_other = pl.multiple_of((2 - row) * half - first, lanes)
    low_own = pl.multiple_of(row * half, lanes)
    parts = tok.shape[1] // kb
    pairs = []
    for i in range(parts):
        deep = pl.ds(i * kb, kb)
        pairs += [
            (tok.at[:, deep], held_tok.at[:, deep]),
            (w_x.at[deep, pl.ds(low_other, first)], held.at[deep, pl.ds(0, first)]),
            (w_x.at[deep, pl.ds(low_own, half)], held.at[deep, pl.ds(first, half)]),
        ]
    started = copies([*pairs, (edge_first, edge_in)], sems)
    product(held_tok, held, [started[3 * i : 3 * i + 3] for i in range(parts)], acc, kb)
    started[-1].wait()
    per = msg.shape[0] // toks
    base = edge_in.shape[0]
    edge_other[:base, :] = edge_in[...]
    edge_own[:HALO, :] = edge_in[:HALO, :]
    for j in range(width // lanes):
        now = acc[:, j * lanes : (j + 1) * lanes].astype(bf16)
        if j < per:
            msg[j * toks : (j + 1) * toks, :] = now
            edge_other[base + j * HALO : base + (j + 1) * HALO, :] = now[toks - HALO :, :]
        else:
            i = j - per
            mine[i * toks : (i + 1) * toks, :] = now
            edge_own[(i + 1) * HALO : (i + 2) * HALO, :] = now[toks - HALO :, :]


def gate_product_kernel(tok, weight, *refs, kb):
    *outs, tok_out, held, acc, sems = refs
    toks, width = acc.shape
    lanes = outs[0].shape[1]
    low = pl.multiple_of((1 - place()[0]) * width, width)
    parts = tok.shape[1] // kb
    pairs = []
    for i in range(parts):
        deep = pl.ds(i * kb, kb)
        pairs += [
            (tok.at[:, deep], tok_out.at[:, deep]),
            (weight.at[deep, pl.ds(low, width)], held.at[deep, :]),
        ]
    started = copies(pairs, sems)
    product(tok_out, held, [started[2 * i : 2 * i + 2] for i in range(parts)], acc, kb)
    per = width // lanes // len(outs)
    for j in range(width // lanes):
        at_row = j % per * toks
        outs[j // per][at_row : at_row + toks, :] = acc[:, j * lanes : (j + 1) * lanes].astype(bf16)


def rows_of(weight, target, low, lanes):
    return [
        (weight.at[pl.ds(low + i * lanes, lanes), :], target.at[pl.ds(i * lanes, lanes), :])
        for i in range(target.shape[0] // lanes)
    ]


def rows_of(weight, target, low, lanes):
    return [
        (weight.at[pl.ds(low + i * lanes, lanes), :], target.at[pl.ds(i * lanes, lanes), :])
        for i in range(target.shape[0] // lanes)
    ]


def inner_kernel(scores, skip, scaled, conv_out, cum, cum_t, out, *, chunk, chunks, head_dim):
    heads = scaled.shape[1] // head_dim
    within(
        place(), scores, scaled, conv_out, cum, cum_t, skip, out,
        head_dim=head_dim, first_of=chunk * heads, local_heads=chunks * heads,
    )


def own_gate_kernel(tok, weight, w_out, mine, w_own, held, acc, sems, *, kb):
    toks, width = acc.shape
    lanes = mine.shape[1]
    row = place()[0]
    low = pl.multiple_of(row * width, width)
    parts = tok.shape[1] // kb
    pairs = [
        (weight.at[pl.ds(i * kb, kb), pl.ds(low, width)], held.at[pl.ds(i * kb, kb), :])
        for i in range(parts)
    ]
    pairs += rows_of(w_out, w_own, pl.multiple_of(row * width, lanes), lanes)
    started = copies(pairs, sems)
    product(tok, held, [[now] for now in started[:parts]], acc, kb)
    for j in range(width // lanes):
        mine[j * toks : (j + 1) * toks, :] = acc[:, j * lanes : (j + 1) * lanes].astype(bf16)
    for now in started[parts:]:
        now.wait()


def state_kernel(
    *refs, first, chunk, chunks, head_dim, state_dim, toks, lanes
):
    refs = list(refs)
    if not first:
        bc_in = refs.pop(0)
    mine, theirs, x_mine, x_theirs, edge_a, edge_b, taps_x, taps_bc, bias, decay = refs[:10]
    refs = refs[10:]
    if first:
        bc_out, scores = refs.pop(0), refs.pop(0)
    msg, scaled, conv_out, cum_out, cum_t_out, ext = refs
    row, _, here = place()
    blocks = x_mine.shape[0] // toks // chunks
    heads = blocks * lanes // head_dim
    local_heads = heads * chunks
    inside = jnp.where(here > 0, 1.0, 0.0)

    def halo(block):
        low = block * HALO
        return total(edge_a[low : low + HALO, :], edge_b[low : low + HALO, :]) * inside

    if first:
        ext[:HALO, :] = halo(0)
        ext[HALO:, :] = total(mine[:toks, :], theirs[:toks, :])
        bc_now = silu(conv(ext, taps_bc[...], toks)).astype(bf16)
        bc_out[...] = bc_now
        b_now = bc_now[:, :state_dim]
        products = mm_nt(bc_now[:, state_dim:], b_now)
        shape = (toks, toks)
        lower = lax.broadcasted_iota(jnp.int32, shape, 0) >= lax.broadcasted_iota(jnp.int32, shape, 1)
        scores[...] = jnp.where(lower, products, 0.0)
    else:
        b_now = bc_in[:, :state_dim]

    low = pl.multiple_of(toks + row * local_heads, local_heads)
    dt_sum = total(mine[pl.ds(low, local_heads), :], theirs[pl.ds(low, local_heads), :])
    dt_sum = dt_sum[chunk * heads : (chunk + 1) * heads]
    first_head = row * local_heads + chunk * heads
    dt_now = softplus(dt_sum + pick(bias[...], first_head, heads))
    log_decay = -pick(decay[...], first_head, heads) * dt_now
    shape = (toks, toks)
    upper = lax.broadcasted_iota(jnp.int32, shape, 0) <= lax.broadcasted_iota(jnp.int32, shape, 1)
    cum = lax.dot_general(
        log_decay,
        jnp.where(upper, 1.0, 0.0),
        (((1,), (0,)), ((), ())),
        precision=highest_mode,
        preferred_element_type=f32,
    )
    last = cum[:, toks - 1 : toks]
    cum_out[...] = cum
    cum_t_out[...] = cum.T
    dt_wide = spread(dt_now, head_dim)
    tail_wide = spread(dt_now * jnp.exp(last - cum), head_dim)
    through = spread(jnp.exp(jnp.broadcast_to(last, (heads, HALO))), head_dim)
    x_low = x_theirs.shape[0] - blocks * toks
    taps_low = (row * chunks + chunk) * blocks * lanes
    for j in range(blocks):
        ext[:HALO, :] = halo(1 + chunk * blocks + j)
        ext[HALO:, :] = total(
            x_mine[(chunk * blocks + j) * toks : (chunk * blocks + j + 1) * toks, :],
            x_theirs[x_low + j * toks : x_low + (j + 1) * toks, :],
        )
        cols = slice(j * lanes, (j + 1) * lanes)
        x_now = silu(conv(ext, taps_x[:, pl.ds(pl.multiple_of(taps_low + j * lanes, lanes), lanes)], toks))
        conv_out[:, cols] = x_now.astype(bf16)
        scaled[:, cols] = (x_now * dt_wide[:, cols]).astype(bf16)
        state = mm_tn(b_now, (x_now * tail_wide[:, cols]).astype(bf16))
        msg[j * state_dim : (j + 1) * state_dim, :] = state.astype(bf16)
    msg[blocks * state_dim :, :] = decay_rows(
        [through[:1, j * lanes : (j + 1) * lanes] for j in range(blocks)]
    )


def combine_kernel(*refs, state_dim):
    *messages, out = refs
    here = place()[2]
    blocks = out.shape[0] // state_dim
    decays = []
    for j in range(blocks):
        now = [block_of(m, j, blocks, state_dim) for m in messages]
        _, state, decay = prefix(now, here)
        out[j * state_dim : (j + 1) * state_dim, :] = state.astype(bf16)
        decays.append(decay)
    out[blocks * state_dim :, :] = decay_rows(decays)


def within(where, scores, scaled, conv_out, cum, cum_t, skip, out, *, head_dim, first_of, local_heads):
    toks, channels = scaled.shape
    pair = 2 * head_dim
    half = toks // 2
    heads = channels // head_dim
    skip_now = pick(skip[...], where[0] * local_heads + first_of, heads)
    skip_wide = spread(jnp.broadcast_to(skip_now, (heads, HALO)), head_dim)[:1, :]
    left = lax.broadcasted_iota(jnp.int32, (toks, pair), 1) < head_dim
    zero = jnp.zeros((toks, pair), bf16)
    for p in range(heads // 2):
        cols = slice(p * pair, (p + 1) * pair)
        x_pair = scaled[:, cols]
        top = None
        for side in range(2):
            h = 2 * p + side
            x_now = jnp.where(left, x_pair, zero) if side == 0 else jnp.where(left, zero, x_pair)
            gap_top = jnp.minimum(cum_t[:half, h : h + 1] - cum[h : h + 1, :half], 0.0)
            gap_low = jnp.minimum(cum_t[half:, h : h + 1] - cum[h : h + 1, :], 0.0)
            w_top = (jnp.exp(gap_top) * scores[:half, :half]).astype(bf16)
            w_low = (jnp.exp(gap_low) * scores[half:, :]).astype(bf16)
            part_top = mm(w_top, x_now[:half])
            part_low = mm(w_low, x_now)
            top = part_top if top is None else top + part_top
            low = part_low if side == 0 else low + part_low
        skips = skip_wide[:, cols]
        out[:half, cols] = top + skips * conv_out[:half, cols].astype(f32)
        out[half:, cols] = low + skips * conv_out[half:, cols].astype(f32)


def gate_kernel(inner, bc, cum, z_mine, z_theirs, gain, *refs, messages, bounds, chunk, chunks, head_dim, state_dim, lanes):
    messages, outs = refs[:messages], refs[messages:]
    toks = inner.shape[0]
    row, _, here = place()
    gain_low = (row * chunks + chunk) * inner.shape[1]
    blocks = inner.shape[1] // lanes
    grown = spread(jnp.exp(cum[...]), head_dim)
    c_now = bc[:, state_dim:]
    wide = 2 * head_dim
    shape = (wide, wide)
    same = (lax.broadcasted_iota(jnp.int32, shape, 0) // head_dim) == (
        lax.broadcasted_iota(jnp.int32, shape, 1) // head_dim
    )
    mean_of = jnp.where(same, 1.0 / head_dim, 0.0).astype(bf16)
    for j in range(blocks):
        enter, _, _ = prefix([block_of(m, j, blocks, state_dim) for m in messages], here)
        cols = slice(j * lanes, (j + 1) * lanes)
        scanned = inner[:, cols] + grown[:, cols] * mm(c_now, enter.astype(bf16))
        z_low = (chunk * inner.shape[1] // lanes + j) * toks
        z_now = total(z_mine[z_low : z_low + toks, :], z_theirs[j * toks : (j + 1) * toks, :])
        gated = scanned * silu(z_now)
        square = gated * gated
        for i in range(lanes // wide):
            part = square[:, i * wide : (i + 1) * wide]
            high = part.astype(bf16)
            rest = (part - high.astype(f32)).astype(bf16)
            mean = mm(high, mean_of) + mm(rest, mean_of)
            low = j * lanes + i * wide
            done = (
                gated[:, i * wide : (i + 1) * wide]
                * lax.rsqrt(mean + EPS)
                * gain[:, pl.ds(pl.multiple_of(gain_low + low, wide), wide)]
            ).astype(bf16)
            for (start, end), out in zip(bounds, outs):
                size = end - start
                out[j * size : (j + 1) * size, i * wide : (i + 1) * wide] = done[start:end]


def own_kernel(weight, w_first, *refs, cuts):
    *normed, partial, rest, w_last, whole, sems = refs
    lanes = normed[0].shape[1]
    half = rest.shape[0]
    row = place()[0]
    first = w_first.shape[0]
    pairs = rows_of(weight, w_last, pl.multiple_of(row * half + first, lanes), lanes)
    needed = len(pairs)
    pairs += rows_of(weight, rest, pl.multiple_of((1 - row) * half, lanes), lanes)
    started = copies(pairs, sems)
    for now in started[:needed]:
        now.wait()

    @pl.when(row >= 0)
    def _():
        own_product(w_first, w_last, normed, partial, whole, cuts)

    for now in started[needed:]:
        now.wait()


def own_product(w_first, w_last, normed, partial, whole, cuts):
    cut_row = w_first.shape[0]
    width = partial.shape[1]
    lanes = normed[0].shape[1]
    low = whole.shape[1]
    for cut in cuts[::-1]:
        parts, normed = normed[: len(cut)], normed[len(cut) :]
        blocks = parts[0].shape[0] // (cut[0][1] - cut[0][0])
        low -= blocks * lanes
        for j in range(blocks):
            for (start, end), part in zip(cut, parts):
                size = end - start
                whole[start:end, low + j * lanes : low + (j + 1) * lanes] = part[j * size : (j + 1) * size, :]
    for low in range(0, width, 512):
        cols = slice(low, min(low + 512, width))
        partial[:, cols] = mm(whole[:, :cut_row], w_first[:, cols]) + mm(whole[:, cut_row:], w_last[:, cols])


def rest_kernel(partial, rest, *refs, start, end, far):
    *normed, send, keep = refs
    lanes = normed[0].shape[1]
    piece = send.shape[1]
    size = end - start
    step = min(512, piece)
    blocks = rest.shape[0] // lanes // len(normed)
    _, col, _ = place()
    pair = 1 - col // 2 if far else col // 2
    for target, core in ((send, 1 - col % 2), (keep, col % 2)):
        base = (pair * 2 + core) * piece
        for low in range(0, piece, step):
            cols = pl.ds(pl.multiple_of(base + low, step), step)
            acc = partial[start:end, cols]
            row = 0
            for chunk in normed[::-1]:
                held_toks = chunk.shape[0] // blocks
                first = start if held_toks > size else 0
                for j in range(blocks):
                    now = chunk[j * held_toks + first : j * held_toks + first + size, :]
                    acc = acc + mm(now, rest[row : row + lanes, cols])
                    row += lanes
            target[:, low : low + step] = acc.astype(bf16)


def final_kernel(*refs, bounds):
    *parts, out = refs
    for i, (start, end) in enumerate(bounds):
        far, keep, got = parts[3 * i : 3 * i + 3]
        total_now = far[...].astype(f32) + keep[...].astype(f32) + got[...].astype(f32)
        out[start:end, :] = total_now.astype(bf16)


def sds(*shape, dtype=bf16):
    return jax.ShapeDtypeStruct(shape, dtype)


def call(kernel, args, specs, outs, scratch=(), name=None, mib=16, after=()):
    used = len(args)

    def body(*refs):
        kernel(*refs[:used], *refs[used + len(after) :])

    return pl.pallas_call(
        body,
        in_specs=[*(specs or [IN_VMEM] * used), *[pl.BlockSpec(memory_space=pl.ANY)] * len(after)],
        out_specs=[IN_VMEM] * len(outs),
        scratch_shapes=list(scratch),
        out_shape=outs,
        compiler_params=pltpu.CompilerParams(vmem_limit_bytes=int(mib * MIB)),
        cost_estimate=pl.CostEstimate(flops=0, bytes_accessed=0, transcendentals=0),
        name=name,
    )(*args, *after)


IN_VMEM = pl.BlockSpec(memory_space=pltpu.VMEM)
IN_HBM = pl.BlockSpec(memory_space=pltpu.HBM)


def swapped(shard, axis, by):
    devices = lax.axis_size(axis)
    return lax.ppermute(shard, axis, [(i, i ^ by) for i in range(devices)])


def fast(
    tokens, proj_x, proj_z, proj_bc, proj_dt, dt_bias, decay_rate, skip_gain,
    conv_x, conv_bc, norm_gain, proj_out,
):
    toks, depth = tokens.shape
    heads = proj_dt.shape[1]
    head_dim = proj_x.shape[1] // heads
    lanes = proj_bc.shape[1]
    state_dim = lanes // 2
    taps = conv_bc.shape[1]
    local_heads = heads // 2
    half = local_heads * head_dim
    chunks = 2
    width = half // chunks
    blocks = width // lanes
    chunk_heads = local_heads // chunks
    out_cols = proj_out.shape[1]
    ctx_size = lax.axis_size("ctx")
    conv_x_t, conv_bc_t, proj_dt_t = conv_x.T, conv_bc.T, proj_dt.T
    bias, decay, skip, gain = (v[None] for v in (dt_bias, decay_rate, skip_gain, norm_gain))

    kb = depth // 8
    parts = depth // kb
    edge_rows = (1 + chunks * blocks) * HALO
    msg_first, edge_first = call(
        functools.partial(first_kernel, chunks=chunks, kb=kb),
        (tokens, proj_x, proj_bc, proj_dt_t),
        [IN_HBM] * 4,
        [sds(toks + heads + blocks * toks, lanes), sds((1 + blocks) * HALO, lanes)],
        [
            pltpu.VMEM((toks, depth), bf16),
            pltpu.VMEM((depth, width), bf16),
            pltpu.VMEM((depth, lanes), bf16),
            pltpu.VMEM((heads, depth), bf16),
            pltpu.VMEM((toks, width), f32),
            pltpu.VMEM((toks, lanes), f32),
            pltpu.VMEM((heads, toks), f32),
            pltpu.SemaphoreType.DMA((4 * parts,)),
        ],
        name="first",
        mib=53.9,
    )
    first_got = swapped(msg_first, "row", 1)
    msg_second, x_mine, edge_other, edge_own = call(
        functools.partial(second_kernel, chunks=chunks, kb=kb),
        (tokens, proj_x, edge_first),
        [IN_HBM] * 3,
        [sds(blocks * toks, lanes), sds(chunks * blocks * toks, lanes), *[sds(edge_rows, lanes)] * 2],
        [
            pltpu.VMEM(edge_first.shape, bf16),
            pltpu.VMEM((toks, depth), bf16),
            pltpu.VMEM((depth, width + half), bf16),
            pltpu.VMEM((toks, width + half), f32),
            pltpu.SemaphoreType.DMA((3 * parts + 1,)),
        ],
        name="second",
        mib=52,
    )
    second_got = swapped(msg_second, "row", 1)
    down = [(i, (i + 1) % ctx_size) for i in range(ctx_size)]
    edge_a = lax.ppermute(
        edge_other, ("ctx", "row"), [(2 * i + s, 2 * j + 1 - s) for i, j in down for s in range(2)]
    )
    edge_b = lax.ppermute(edge_own, "ctx", down)
    *z_send, tok_held = call(
        functools.partial(gate_product_kernel, kb=kb),
        (tokens, proj_z),
        [IN_HBM] * 2,
        [*[sds(blocks * toks, lanes)] * chunks, sds(toks, depth)],
        [
            pltpu.VMEM((depth, half), bf16),
            pltpu.VMEM((toks, half), f32),
            pltpu.SemaphoreType.DMA((2 * parts,)),
        ],
        name="z_other",
        mib=50,
        after=(edge_own,),
    )

    sizes = dict(head_dim=head_dim, state_dim=state_dim, lanes=lanes)
    states, scans = [], []
    bc_now = scores = None
    for c in range(chunks):
        args = [] if c == 0 else [bc_now]
        args += [
            msg_first, first_got, x_mine, first_got if c == 0 else second_got, edge_a, edge_b,
            conv_x_t, conv_bc_t, bias, decay,
        ]
        outs = [sds(toks, lanes), sds(toks, toks, dtype=f32)] if c == 0 else []
        outs += [
            sds(blocks * state_dim + HALO, lanes),
            sds(toks, width),
            sds(toks, width),
            sds(chunk_heads, toks, dtype=f32),
            sds(toks, chunk_heads, dtype=f32),
        ]
        got = call(
            functools.partial(
                state_kernel, first=c == 0, chunk=c, chunks=chunks, toks=toks, **sizes
            ),
            args,
            None,
            outs,
            [pltpu.VMEM((HALO + toks, lanes), f32)],
            name="state",
            after=(z_send[0],),
        )
        if c == 0:
            bc_now, scores, *got = got
        states.append(got[0])
        scans.append(got[1:])

    z_send, _ = lax.optimization_barrier((z_send, states))
    z_got = [swapped(z, "row", 1) for z in z_send]
    def inner_call(c):
        (inner,) = call(
            functools.partial(inner_kernel, chunk=c, chunks=chunks, head_dim=head_dim),
            (scores, skip, *scans[c]),
            None,
            [sds(toks, width, dtype=f32)],
            name="inner",
            after=sent[:1],
        )
        return inner

    messages, sent, inners = [], [], []
    for c in range(chunks):
        if c == 1:
            inners = [inner_call(i) for i in range(chunks)]
        heard = [states[c]]
        send = states[c]
        by = 1
        while by < ctx_size:
            if by > 1:
                (send,) = call(
                    functools.partial(combine_kernel, state_dim=state_dim),
                    heard, None, [sds(*send.shape)], name="combine", after=(*sent, *inners),
                )
            heard.append(swapped(send, "ctx", by))
            by *= 2
        messages.append(heard)
        sent.append(send)
    early = half // 2
    z_mine, w_first = call(
        functools.partial(own_gate_kernel, kb=kb),
        (tok_held, proj_z, proj_out),
        [IN_VMEM, IN_HBM, IN_HBM],
        [sds(chunks * blocks * toks, lanes), sds(early, out_cols)],
        [
            pltpu.VMEM((depth, half), bf16),
            pltpu.VMEM((toks, half), f32),
            pltpu.SemaphoreType.DMA((parts + early // lanes,)),
        ],
        name="z_own",
        mib=38,
        after=(*sent, *inners),
    )

    normed, normed_got = [], []
    bounds = ((0, toks // 2), (toks // 2, toks))
    cuts = [((0, toks),)] * (chunks - 1) + [bounds]
    for c in range(chunks):
        now = call(
            functools.partial(
                gate_kernel, messages=len(messages[c]), bounds=cuts[c], chunk=c, chunks=chunks, **sizes
            ),
            (inners[c], bc_now, scans[c][2], z_mine, z_got[c], gain, *messages[c]),
            None,
            [sds(blocks * (end - start), lanes) for start, end in cuts[c]],
            name="gate",
        )
        normed.append(now)
        normed_got.append([swapped(part, "row", 1) for part in now])

    piece = out_cols // lax.axis_size("col")
    partial, rest = call(
        functools.partial(own_kernel, cuts=cuts),
        (proj_out, w_first, *[part for now in normed[::-1] for part in now]),
        [IN_HBM, *[IN_VMEM] * (1 + sum(len(cut) for cut in cuts))],
        [sds(toks, out_cols, dtype=f32), sds(half, out_cols)],
        [
            pltpu.VMEM((half - early, out_cols), bf16),
            pltpu.VMEM((toks, half), bf16),
            pltpu.SemaphoreType.DMA(((2 * half - early) // lanes,)),
        ],
        name="out_own",
        mib=34,
    )

    def out_rest(part, far, after):
        start, end = bounds[part]
        args = (partial, rest, *[now[min(part, len(now) - 1)] for now in normed_got[::-1]])
        return call(
            functools.partial(rest_kernel, start=start, end=end, far=far),
            args,
            None,
            [sds(end - start, piece)] * 2,
            name="out_far" if far else "out_near",
            after=after,
        )

    def added(a, b):
        return (a.astype(f32) + b.astype(f32)).astype(bf16)

    sends, sums, keep = [], [], None
    for part in range(len(bounds)):
        send, far_keep = out_rest(part, True, () if keep is None else (keep,))
        sums.append(added(far_keep, swapped(send, "col", 1)))
        send, keep = out_rest(part, False, (far_keep,))
        sends.append((send, keep))
    args = []
    for far, (send, keep) in zip(sums, sends):
        args += [swapped(far, "col", 2), keep, swapped(send, "col", 1)]
    (out,) = call(
        functools.partial(final_kernel, bounds=bounds), args, None, [sds(toks, piece)], name="final"
    )
    return out


def shifted(shard, axis, by):
    devices = lax.axis_size(axis)
    pairs = [(i, i + by) for i in range(devices) if 0 <= i + by < devices]
    return lax.ppermute(shard, axis, pairs)


def general(
    tokens,
    proj_x,
    proj_z,
    proj_bc,
    proj_dt,
    dt_bias,
    decay_rate,
    skip_gain,
    conv_x,
    conv_bc,
    norm_gain,
    proj_out,
):
    tok_count = tokens.shape[0]
    col_heads = proj_dt.shape[1]
    head_dim = proj_x.shape[1] // col_heads
    state_dim = proj_bc.shape[1] // 2
    tap_count = conv_bc.shape[1]
    group_count = tok_count // Q
    bc_term = jnp.einsum("dc,td->ct", proj_bc, tokens, preferred_element_type=jnp.float32)
    local_heads = col_heads // lax.axis_size("row")
    first_head = lax.axis_index("row") * local_heads
    x_part = jnp.einsum("dc,td->ct", proj_x, tokens, preferred_element_type=jnp.float32).reshape(
        local_heads * lax.axis_size("row"), head_dim, tok_count
    )
    z_part = jnp.einsum("dc,td->ct", proj_z, tokens, preferred_element_type=jnp.float32).reshape(
        local_heads * lax.axis_size("row"), head_dim, tok_count
    )
    dt_part = jnp.einsum("dc,td->ct", proj_dt, tokens, preferred_element_type=jnp.float32).reshape(
        local_heads * lax.axis_size("row"), 1, tok_count
    )
    head_sum = lax.psum_scatter(
        jnp.concatenate([x_part, z_part, dt_part], axis=1).astype(jnp.bfloat16),
        "row",
        scatter_dimension=0,
        tiled=True,
    )
    bc_sum = lax.psum(bc_term.astype(jnp.bfloat16), "row")
    channels = local_heads * head_dim
    z_in = head_sum[:, head_dim : 2 * head_dim]
    dt_in = head_sum[:, 2 * head_dim]
    flat_in = jnp.concatenate([head_sum[:, :head_dim].reshape(channels, tok_count), bc_sum], axis=0)
    prior = shifted(flat_in[:, tok_count - tap_count + 1 :], "ctx", 1)
    padded = jnp.concatenate([prior, flat_in], axis=1).astype(jnp.float32)
    kernel = jnp.concatenate(
        [lax.dynamic_slice_in_dim(conv_x, first_head * head_dim, channels, 0), conv_bc], axis=0
    )
    running = jnp.zeros(flat_in.shape, jnp.float32)
    for tap_index in range(tap_count):
        running = (
            running
            + kernel[:, tap_index : tap_index + 1] * padded[:, tap_index : tap_index + tok_count]
        )
    conv_out = jax.nn.silu(running)
    x_conv = conv_out[:channels].reshape(local_heads, head_dim, tok_count)
    b_blocks = conv_out[channels : channels + state_dim].reshape(state_dim, group_count, Q)
    c_blocks = conv_out[channels + state_dim :].reshape(state_dim, group_count, Q)
    bias_now = lax.dynamic_slice_in_dim(dt_bias, first_head, local_heads, 0)
    decay_now = lax.dynamic_slice_in_dim(decay_rate, first_head, local_heads, 0)
    skip_now = lax.dynamic_slice_in_dim(skip_gain, first_head, local_heads, 0)
    gain_now = lax.dynamic_slice_in_dim(norm_gain, first_head * head_dim, channels, 0).reshape(
        local_heads, head_dim, 1
    )
    dt_full = jax.nn.softplus(dt_in.astype(jnp.float32) + bias_now[:, None])
    log_decay = -decay_now[:, None] * dt_full
    x_scaled = x_conv * dt_full[:, None, :]
    cum_decay = jnp.cumsum(log_decay.reshape(local_heads, group_count, Q), axis=2)
    x_blocks = x_scaled.reshape(local_heads, head_dim, group_count, Q)
    scores = jnp.einsum("nci,ncj->cij", c_blocks, b_blocks, precision=highest_mode)
    lower_mask = jnp.arange(Q)[:, None] >= jnp.arange(Q)[None, :]
    log_gap = cum_decay[:, :, :, None] - cum_decay[:, :, None, :]
    weights = jnp.where(lower_mask, jnp.exp(jnp.where(lower_mask, log_gap, 0.0)), 0.0)
    inner_out = jnp.einsum(
        "hcij,hpcj->hpci", scores[None] * weights, x_blocks, precision=highest_mode
    )
    tail_weight = jnp.exp(cum_decay[:, :, -1:] - cum_decay)
    group_states = jnp.einsum(
        "hcj,hpcj,ncj->chpn", tail_weight, x_blocks, b_blocks, precision=highest_mode
    )
    group_logs = cum_decay[:, :, -1].T

    def group_step(carried, step_inputs):
        group_log, group_state = step_inputs
        return (jnp.exp(group_log)[:, None, None] * carried + group_state, carried)

    start_state = jnp.zeros((local_heads, head_dim, state_dim), jnp.float32)
    final_state, local_enter = lax.scan(group_step, start_state, (group_logs, group_states))
    device_log = jnp.sum(group_logs, axis=0)
    before_logs = jnp.cumsum(group_logs, axis=0) - group_logs
    log_all, state_all = (
        lax.all_gather(device_log[None].astype(jnp.bfloat16), "ctx", axis=0, tiled=True).astype(
            jnp.float32
        ),
        lax.all_gather(final_state[None].astype(jnp.bfloat16), "ctx", axis=0, tiled=True).astype(
            jnp.float32
        ),
    )
    my_index = lax.axis_index("ctx")
    earlier_mask = (jnp.arange(log_all.shape[0], dtype=jnp.int32) < my_index)[:, None]
    log_prefix = jnp.cumsum(log_all, axis=0)
    up_to_me = jnp.sum(jnp.where(earlier_mask, log_all, 0.0), axis=0)
    reach_weight = jnp.where(
        earlier_mask, jnp.exp(jnp.where(earlier_mask, up_to_me - log_prefix, 0.0)), 0.0
    )
    device_state = jnp.einsum("jh,jhpn->hpn", reach_weight, state_all, precision=highest_mode)
    enter_state = jnp.exp(before_logs)[:, :, None, None] * device_state[None] + local_enter
    outer_out = jnp.exp(cum_decay)[:, None] * jnp.einsum(
        "nci,chpn->hpci", c_blocks, enter_state, precision=highest_mode
    )
    ssm_out = (inner_out + outer_out).reshape(local_heads, head_dim, tok_count) + skip_now[
        :, None, None
    ] * x_conv
    gated = ssm_out * jax.nn.silu(z_in.astype(jnp.float32))
    inv_rms = lax.rsqrt(jnp.mean(gated * gated, axis=1, keepdims=True) + 1e-05)
    normed = (gated * inv_rms * gain_now).astype(jnp.bfloat16)
    out_cols = proj_out.shape[1]
    piece = lax.all_gather(normed, "row", axis=0, tiled=True)
    piece_heads = piece.shape[0]
    rows_now = proj_out.reshape(piece_heads, head_dim, out_cols)
    col_partial = jnp.einsum("hpt,hpd->td", piece, rows_now, preferred_element_type=jnp.float32)
    return lax.psum_scatter(
        col_partial.astype(jnp.bfloat16), "col", scatter_dimension=1, tiled=True
    )


def local(*args):
    tokens, proj_x, _, proj_bc, proj_dt = args[:5]
    toks, heads, lanes = tokens.shape[0], proj_dt.shape[1], proj_bc.shape[1]
    ctx_size = lax.axis_size("ctx")
    fits = (
        lax.axis_size("row") == 2
        and lax.axis_size("col") == 4
        and ctx_size & (ctx_size - 1) == 0
        and toks == Q
        and lanes == toks
        and heads % 32 == 0
        and toks % heads == 0
        and proj_x.shape[1] % (4 * lanes) == 0
        and lanes % (2 * proj_x.shape[1] // heads) == 0
    )
    return fast(*args) if fits else general(*args)


def solution(mesh):
    in_specs = (
        P("ctx", "row"),
        P("row", "col"),
        P("row", "col"),
        P("row", None),
        P("row", "col"),
        P("col"),
        P("col"),
        P("col"),
        P("col", None),
        P(),
        P("col"),
        P("col", "row"),
    )
    out_specs = P("ctx", ("row", "col"))
    return jax.shard_map(local, mesh=mesh, in_specs=in_specs, out_specs=out_specs, check_vma=False)
```

```python
import functools

import jax
import jax.numpy as jnp
from jax import lax
from jax.experimental import pallas as pl
from jax.experimental.pallas import tpu as pltpu
from jax.sharding import PartitionSpec as P

Q = 256
EPS = 1e-05
HALO = 16
MIB = 1024 * 1024
f32 = jnp.float32
bf16 = jnp.bfloat16
highest_mode = lax.Precision.HIGHEST


def mm(a, b):
    return jnp.dot(a, b, preferred_element_type=f32)


def mm_tn(a, b):
    return lax.dot_general(a, b, (((0,), (0,)), ((), ())), preferred_element_type=f32)


def mm_nt(a, b):
    return lax.dot_general(a, b, (((1,), (1,)), ((), ())), preferred_element_type=f32)


def silu(v):
    return v / (1.0 + jnp.exp(-v))


def softplus(v):
    return jnp.maximum(v, 0.0) + jnp.log(1.0 + jnp.exp(-jnp.abs(v)))


def total(mine, theirs):
    return (mine.astype(f32) + theirs.astype(f32)).astype(bf16).astype(f32)


def spread(per_head, head_dim):
    heads = per_head.shape[0]
    high = per_head.astype(bf16)
    low = (per_head - high.astype(f32)).astype(bf16)
    parts = jnp.concatenate([high.astype(f32), low.astype(f32)], axis=0).astype(bf16)
    shape = (2 * heads, heads * head_dim)
    row = lax.broadcasted_iota(jnp.int32, shape, 0) % heads
    col = lax.broadcasted_iota(jnp.int32, shape, 1) // head_dim
    return mm_tn(parts, jnp.where(row == col, 1.0, 0.0).astype(bf16))


def pick(row_vector, first, count):
    shape = (count, row_vector.shape[1])
    lane = lax.broadcasted_iota(jnp.int32, shape, 1)
    sub = lax.broadcasted_iota(jnp.int32, shape, 0)
    return jnp.sum(jnp.where(lane == sub + first, row_vector, 0.0), axis=1, keepdims=True)


def conv(ext_ref, taps, toks):
    count = taps.shape[0]
    running = None
    for tap in range(count):
        term = taps[tap : tap + 1, :] * ext_ref[pl.ds(HALO - count + 1 + tap, toks), :]
        running = term if running is None else running + term
    return running


def block_of(message, block, blocks, state_dim):
    decays = message[blocks * state_dim :, :].astype(f32)
    state = message[block * state_dim : (block + 1) * state_dim, :].astype(f32)
    return state, decays[block : block + 1]


def decay_rows(decays):
    row = lax.broadcasted_iota(jnp.int32, (HALO, decays[0].shape[1]), 0)
    rows = jnp.zeros((HALO, decays[0].shape[1]), f32)
    for j, decay in enumerate(decays):
        rows = jnp.where(row == j, decay, rows)
    return rows.astype(bf16)


def prefix(messages, here):
    state, decay = messages[0]
    enter = jnp.zeros_like(state)
    reach = jnp.ones_like(decay)
    for step, (their_state, their_decay) in enumerate(messages[1:]):
        later = ((here >> step) & 1) == 1
        enter = jnp.where(later, enter + reach * their_state, enter)
        reach = jnp.where(later, reach * their_decay, reach)
        state = jnp.where(later, decay * their_state + state, their_decay * state + their_state)
        decay = decay * their_decay
    return enter, state, decay


def copies(pairs, sems):
    started = []
    for i, (source, target) in enumerate(pairs):
        now = pltpu.make_async_copy(source, target, sems.at[i])
        now.start()
        started.append(now)
    return started


def product(tok, held, waits, acc, kb):
    for i in range(tok.shape[1] // kb):
        for wait in waits[i]:
            wait.wait()
        deep = slice(i * kb, (i + 1) * kb)
        for low in range(0, acc.shape[1], 256):
            cols = slice(low, min(low + 256, acc.shape[1]))
            part = mm(tok[:, deep], held[deep, cols])
            if i == 0:
                acc[:, cols] = part
            else:
                acc[:, cols] += part


def place():
    return lax.axis_index("row"), lax.axis_index("col"), lax.axis_index("ctx")


def first_kernel(tok, w_x, w_bc, w_dt, msg, edge, held_tok, held_x, held_bc, held_dt, acc_x, acc_bc, acc_dt, sems, *, chunks, kb):
    toks, lanes = acc_bc.shape
    width = acc_x.shape[1]
    low = pl.multiple_of((1 - place()[0]) * chunks * width, width)
    parts = tok.shape[1] // kb
    pairs = []
    for i in range(parts):
        deep = pl.ds(i * kb, kb)
        pairs += [
            (tok.at[:, deep], held_tok.at[:, deep]),
            (w_x.at[deep, pl.ds(low, width)], held_x.at[deep, :]),
            (w_bc.at[deep, :], held_bc.at[deep, :]),
            (w_dt.at[:, deep], held_dt.at[:, deep]),
        ]
    started = copies(pairs, sems)
    for i in range(parts):
        for wait in started[4 * i : 4 * i + 4]:
            wait.wait()
        deep = slice(i * kb, (i + 1) * kb)
        now = held_tok[:, deep]
        for acc, part in (
            (acc_x, mm(now, held_x[deep, :])),
            (acc_bc, mm(now, held_bc[deep, :])),
            (acc_dt, mm_nt(held_dt[:, deep], now)),
        ):
            if i == 0:
                acc[...] = part
            else:
                acc[...] += part
    heads = acc_dt.shape[0]
    msg[:toks, :] = acc_bc[...].astype(bf16)
    msg[toks : toks + heads, :] = acc_dt[...].astype(bf16)
    edge[:HALO, :] = acc_bc[toks - HALO :, :].astype(bf16)
    for j in range(width // lanes):
        low = toks + heads + j * toks
        cols = slice(j * lanes, (j + 1) * lanes)
        msg[low : low + toks, :] = acc_x[:, cols].astype(bf16)
        edge[(1 + j) * HALO : (2 + j) * HALO, :] = acc_x[toks - HALO :, cols].astype(bf16)


def second_kernel(tok, w_x, edge_first, msg, mine, edge_other, edge_own, edge_in, held_tok, held, acc, sems, *, chunks, kb):
    toks, width = acc.shape
    lanes = msg.shape[1]
    row = place()[0]
    half = chunks * (msg.shape[0] // toks) * lanes
    first = width - half
    low_other = pl.multiple_of((2 - row) * half - first, lanes)
    low_own = pl.multiple_of(row * half, lanes)
    parts = tok.shape[1] // kb
    pairs = []
    for i in range(parts):
        deep = pl.ds(i * kb, kb)
        pairs += [
            (tok.at[:, deep], held_tok.at[:, deep]),
            (w_x.at[deep, pl.ds(low_other, first)], held.at[deep, pl.ds(0, first)]),
            (w_x.at[deep, pl.ds(low_own, half)], held.at[deep, pl.ds(first, half)]),
        ]
    started = copies([*pairs, (edge_first, edge_in)], sems)
    product(held_tok, held, [started[3 * i : 3 * i + 3] for i in range(parts)], acc, kb)
    started[-1].wait()
    per = msg.shape[0] // toks
    base = edge_in.shape[0]
    edge_other[:base, :] = edge_in[...]
    edge_own[:HALO, :] = edge_in[:HALO, :]
    for j in range(width // lanes):
        now = acc[:, j * lanes : (j + 1) * lanes].astype(bf16)
        if j < per:
            msg[j * toks : (j + 1) * toks, :] = now
            edge_other[base + j * HALO : base + (j + 1) * HALO, :] = now[toks - HALO :, :]
        else:
            i = j - per
            mine[i * toks : (i + 1) * toks, :] = now
            edge_own[(i + 1) * HALO : (i + 2) * HALO, :] = now[toks - HALO :, :]


def gate_product_kernel(tok, weight, *refs, kb):
    *outs, tok_out, held, acc, sems = refs
    toks, width = acc.shape
    lanes = outs[0].shape[1]
    low = pl.multiple_of((1 - place()[0]) * width, width)
    parts = tok.shape[1] // kb
    pairs = []
    for i in range(parts):
        deep = pl.ds(i * kb, kb)
        pairs += [
            (tok.at[:, deep], tok_out.at[:, deep]),
            (weight.at[deep, pl.ds(low, width)], held.at[deep, :]),
        ]
    started = copies(pairs, sems)
    product(tok_out, held, [started[2 * i : 2 * i + 2] for i in range(parts)], acc, kb)
    per = width // lanes // len(outs)
    for j in range(width // lanes):
        at_row = j % per * toks
        outs[j // per][at_row : at_row + toks, :] = acc[:, j * lanes : (j + 1) * lanes].astype(bf16)


def rows_of(weight, target, low, lanes):
    return [
        (weight.at[pl.ds(low + i * lanes, lanes), :], target.at[pl.ds(i * lanes, lanes), :])
        for i in range(target.shape[0] // lanes)
    ]


def rows_of(weight, target, low, lanes):
    return [
        (weight.at[pl.ds(low + i * lanes, lanes), :], target.at[pl.ds(i * lanes, lanes), :])
        for i in range(target.shape[0] // lanes)
    ]


def inner_kernel(bc, skip, dt, conv_out, cum, cum_t, out, *, chunk, chunks, head_dim):
    heads = conv_out.shape[1] // head_dim
    within(
        place(), bc, dt, conv_out, cum, cum_t, skip, out,
        head_dim=head_dim, first_of=chunk * heads, local_heads=chunks * heads,
    )


def own_gate_kernel(tok, weight, w_out, mine, w_own, held, acc, sems, *, kb):
    toks, width = acc.shape
    lanes = mine.shape[1]
    row = place()[0]
    low = pl.multiple_of(row * width, width)
    parts = tok.shape[1] // kb
    pairs = [
        (weight.at[pl.ds(i * kb, kb), pl.ds(low, width)], held.at[pl.ds(i * kb, kb), :])
        for i in range(parts)
    ]
    pairs += rows_of(w_out, w_own, pl.multiple_of(row * width, lanes), lanes)
    started = copies(pairs, sems)
    product(tok, held, [[now] for now in started[:parts]], acc, kb)
    for j in range(width // lanes):
        mine[j * toks : (j + 1) * toks, :] = acc[:, j * lanes : (j + 1) * lanes].astype(bf16)
    for now in started[parts:]:
        now.wait()


def state_kernel(
    *refs, first, chunk, chunks, head_dim, state_dim, toks, lanes
):
    refs = list(refs)
    if not first:
        bc_in = refs.pop(0)
    mine, theirs, x_mine, x_theirs, edge_b, edge_a, taps_x, taps_bc, bias, decay = refs[:10]
    refs = refs[10:]
    if first:
        bc_out = refs.pop(0)
    msg, dt_out, conv_out, cum_out, cum_t_out, ext = refs
    row, _, here = place()
    blocks = x_mine.shape[0] // toks // chunks
    heads = blocks * lanes // head_dim
    local_heads = heads * chunks
    inside = jnp.where(here > 0, 1.0, 0.0)

    def halo(block):
        low = block * HALO
        return total(edge_a[low : low + HALO, :], edge_b[low : low + HALO, :]) * inside

    if first:
        ext[:HALO, :] = halo(0)
        ext[HALO:, :] = total(mine[:toks, :], theirs[:toks, :])
        bc_now = silu(conv(ext, taps_bc[...], toks)).astype(bf16)
        bc_out[...] = bc_now
        b_now = bc_now[:, :state_dim]
    else:
        b_now = bc_in[:, :state_dim]

    low = pl.multiple_of(toks + row * local_heads, local_heads)
    dt_sum = total(mine[pl.ds(low, local_heads), :], theirs[pl.ds(low, local_heads), :])
    dt_sum = dt_sum[chunk * heads : (chunk + 1) * heads]
    first_head = row * local_heads + chunk * heads
    dt_now = softplus(dt_sum + pick(bias[...], first_head, heads))
    log_decay = -pick(decay[...], first_head, heads) * dt_now
    shape = (toks, toks)
    upper = lax.broadcasted_iota(jnp.int32, shape, 0) <= lax.broadcasted_iota(jnp.int32, shape, 1)
    cum = lax.dot_general(
        log_decay,
        jnp.where(upper, 1.0, 0.0),
        (((1,), (0,)), ((), ())),
        precision=highest_mode,
        preferred_element_type=f32,
    )
    last = cum[:, toks - 1 : toks]
    cum_out[...] = cum
    cum_t_out[...] = cum.T
    dt_out[...] = dt_now
    tail_wide = spread(dt_now * jnp.exp(last - cum), head_dim)
    through = spread(jnp.exp(jnp.broadcast_to(last, (heads, HALO))), head_dim)
    x_low = x_theirs.shape[0] - blocks * toks
    taps_low = (row * chunks + chunk) * blocks * lanes
    for j in range(blocks):
        ext[:HALO, :] = halo(1 + chunk * blocks + j)
        ext[HALO:, :] = total(
            x_mine[(chunk * blocks + j) * toks : (chunk * blocks + j + 1) * toks, :],
            x_theirs[x_low + j * toks : x_low + (j + 1) * toks, :],
        )
        cols = slice(j * lanes, (j + 1) * lanes)
        x_now = silu(conv(ext, taps_x[:, pl.ds(pl.multiple_of(taps_low + j * lanes, lanes), lanes)], toks))
        conv_out[:, cols] = x_now.astype(bf16)
        state = mm_tn(b_now, (x_now * tail_wide[:, cols]).astype(bf16))
        msg[j * state_dim : (j + 1) * state_dim, :] = state.astype(bf16)
    msg[blocks * state_dim :, :] = decay_rows(
        [through[:1, j * lanes : (j + 1) * lanes] for j in range(blocks)]
    )


def combine_kernel(*refs, state_dim):
    *messages, out = refs
    here = place()[2]
    blocks = out.shape[0] // state_dim
    decays = []
    for j in range(blocks):
        now = [block_of(m, j, blocks, state_dim) for m in messages]
        _, state, decay = prefix(now, here)
        out[j * state_dim : (j + 1) * state_dim, :] = state.astype(bf16)
        decays.append(decay)
    out[blocks * state_dim :, :] = decay_rows(decays)


def within(where, bc, dt, conv_out, cum, cum_t, skip, out, *, head_dim, first_of, local_heads):
    toks, channels = conv_out.shape
    state_dim = bc.shape[1] // 2
    shape = (toks, toks)
    lower = lax.broadcasted_iota(jnp.int32, shape, 0) >= lax.broadcasted_iota(jnp.int32, shape, 1)
    scores = jnp.where(lower, mm_nt(bc[:, state_dim:], bc[:, :state_dim]), 0.0)
    dt_wide = spread(dt[...], head_dim)
    pair = 2 * head_dim
    half = toks // 2
    heads = channels // head_dim
    skip_now = pick(skip[...], where[0] * local_heads + first_of, heads)
    skip_wide = spread(jnp.broadcast_to(skip_now, (heads, HALO)), head_dim)[:1, :]
    left = lax.broadcasted_iota(jnp.int32, (toks, pair), 1) < head_dim
    zero = jnp.zeros((toks, pair), bf16)
    for p in range(heads // 2):
        cols = slice(p * pair, (p + 1) * pair)
        x_pair = (conv_out[:, cols].astype(f32) * dt_wide[:, cols]).astype(bf16)
        top = None
        for side in range(2):
            h = 2 * p + side
            x_now = jnp.where(left, x_pair, zero) if side == 0 else jnp.where(left, zero, x_pair)
            gap_top = jnp.minimum(cum_t[:half, h : h + 1] - cum[h : h + 1, :half], 0.0)
            gap_low = jnp.minimum(cum_t[half:, h : h + 1] - cum[h : h + 1, :], 0.0)
            w_top = (jnp.exp(gap_top) * scores[:half, :half]).astype(bf16)
            w_low = (jnp.exp(gap_low) * scores[half:, :]).astype(bf16)
            part_top = mm(w_top, x_now[:half])
            part_low = mm(w_low, x_now)
            top = part_top if top is None else top + part_top
            low = part_low if side == 0 else low + part_low
        skips = skip_wide[:, cols]
        out[:half, cols] = top + skips * conv_out[:half, cols].astype(f32)
        out[half:, cols] = low + skips * conv_out[half:, cols].astype(f32)


def gate_kernel(inner, bc, cum, z_mine, z_theirs, gain, *refs, messages, bounds, chunk, chunks, head_dim, state_dim, lanes):
    messages, outs = refs[:messages], refs[messages:]
    toks = inner.shape[0]
    row, _, here = place()
    gain_low = (row * chunks + chunk) * inner.shape[1]
    blocks = inner.shape[1] // lanes
    grown = spread(jnp.exp(cum[...]), head_dim)
    c_now = bc[:, state_dim:]
    wide = 2 * head_dim
    shape = (wide, wide)
    same = (lax.broadcasted_iota(jnp.int32, shape, 0) // head_dim) == (
        lax.broadcasted_iota(jnp.int32, shape, 1) // head_dim
    )
    mean_of = jnp.where(same, 1.0 / head_dim, 0.0).astype(bf16)
    for j in range(blocks):
        enter, _, _ = prefix([block_of(m, j, blocks, state_dim) for m in messages], here)
        cols = slice(j * lanes, (j + 1) * lanes)
        scanned = inner[:, cols] + grown[:, cols] * mm(c_now, enter.astype(bf16))
        z_low = (chunk * inner.shape[1] // lanes + j) * toks
        z_now = total(z_mine[z_low : z_low + toks, :], z_theirs[j * toks : (j + 1) * toks, :])
        gated = scanned * silu(z_now)
        square = gated * gated
        for i in range(lanes // wide):
            part = square[:, i * wide : (i + 1) * wide]
            high = part.astype(bf16)
            rest = (part - high.astype(f32)).astype(bf16)
            mean = mm(high, mean_of) + mm(rest, mean_of)
            low = j * lanes + i * wide
            done = (
                gated[:, i * wide : (i + 1) * wide]
                * lax.rsqrt(mean + EPS)
                * gain[:, pl.ds(pl.multiple_of(gain_low + low, wide), wide)]
            ).astype(bf16)
            for (start, end), out in zip(bounds, outs):
                size = end - start
                out[j * size : (j + 1) * size, i * wide : (i + 1) * wide] = done[start:end]


def own_kernel(weight, w_first, *refs, cuts):
    *normed, partial, rest, w_last, whole, sems = refs
    lanes = normed[0].shape[1]
    half = rest.shape[0]
    row = place()[0]
    first = w_first.shape[0]
    pairs = rows_of(weight, w_last, pl.multiple_of(row * half + first, lanes), lanes)
    needed = len(pairs)
    pairs += rows_of(weight, rest, pl.multiple_of((1 - row) * half, lanes), lanes)
    started = copies(pairs, sems)
    for now in started[:needed]:
        now.wait()

    @pl.when(row >= 0)
    def _():
        own_product(w_first, w_last, normed, partial, whole, cuts)

    for now in started[needed:]:
        now.wait()


def own_product(w_first, w_last, normed, partial, whole, cuts):
    cut_row = w_first.shape[0]
    width = partial.shape[1]
    lanes = normed[0].shape[1]
    low = whole.shape[1]
    for cut in cuts[::-1]:
        parts, normed = normed[: len(cut)], normed[len(cut) :]
        blocks = parts[0].shape[0] // (cut[0][1] - cut[0][0])
        low -= blocks * lanes
        for j in range(blocks):
            for (start, end), part in zip(cut, parts):
                size = end - start
                whole[start:end, low + j * lanes : low + (j + 1) * lanes] = part[j * size : (j + 1) * size, :]
    for low in range(0, width, 512):
        cols = slice(low, min(low + 512, width))
        partial[:, cols] = mm(whole[:, :cut_row], w_first[:, cols]) + mm(whole[:, cut_row:], w_last[:, cols])


def rest_kernel(partial, rest, *refs, start, end, far):
    *normed, send, keep = refs
    lanes = normed[0].shape[1]
    piece = send.shape[1]
    size = end - start
    step = min(512, piece)
    blocks = rest.shape[0] // lanes // len(normed)
    _, col, _ = place()
    pair = 1 - col // 2 if far else col // 2
    for target, core in ((send, 1 - col % 2), (keep, col % 2)):
        base = (pair * 2 + core) * piece
        for low in range(0, piece, step):
            cols = pl.ds(pl.multiple_of(base + low, step), step)
            acc = partial[start:end, cols]
            row = 0
            for chunk in normed[::-1]:
                held_toks = chunk.shape[0] // blocks
                first = start if held_toks > size else 0
                for j in range(blocks):
                    now = chunk[j * held_toks + first : j * held_toks + first + size, :]
                    acc = acc + mm(now, rest[row : row + lanes, cols])
                    row += lanes
            target[:, low : low + step] = acc.astype(bf16)


def final_kernel(*refs, bounds):
    *parts, out = refs
    for i, (start, end) in enumerate(bounds):
        far, keep, got = parts[3 * i : 3 * i + 3]
        total_now = far[...].astype(f32) + keep[...].astype(f32) + got[...].astype(f32)
        out[start:end, :] = total_now.astype(bf16)


def sds(*shape, dtype=bf16):
    return jax.ShapeDtypeStruct(shape, dtype)


def call(kernel, args, specs, outs, scratch=(), name=None, mib=16, after=()):
    used = len(args)

    def body(*refs):
        kernel(*refs[:used], *refs[used + len(after) :])

    return pl.pallas_call(
        body,
        in_specs=[*(specs or [IN_VMEM] * used), *[pl.BlockSpec(memory_space=pl.ANY)] * len(after)],
        out_specs=[IN_VMEM] * len(outs),
        scratch_shapes=list(scratch),
        out_shape=outs,
        compiler_params=pltpu.CompilerParams(vmem_limit_bytes=int(mib * MIB)),
        cost_estimate=pl.CostEstimate(flops=0, bytes_accessed=0, transcendentals=0),
        name=name,
    )(*args, *after)


IN_VMEM = pl.BlockSpec(memory_space=pltpu.VMEM)
IN_HBM = pl.BlockSpec(memory_space=pltpu.HBM)


def swapped(shard, axis, by):
    devices = lax.axis_size(axis)
    return lax.ppermute(shard, axis, [(i, i ^ by) for i in range(devices)])


def fast(
    tokens, proj_x, proj_z, proj_bc, proj_dt, dt_bias, decay_rate, skip_gain,
    conv_x, conv_bc, norm_gain, proj_out,
):
    toks, depth = tokens.shape
    heads = proj_dt.shape[1]
    head_dim = proj_x.shape[1] // heads
    lanes = proj_bc.shape[1]
    state_dim = lanes // 2
    taps = conv_bc.shape[1]
    local_heads = heads // 2
    half = local_heads * head_dim
    chunks = 2
    width = half // chunks
    blocks = width // lanes
    chunk_heads = local_heads // chunks
    out_cols = proj_out.shape[1]
    ctx_size = lax.axis_size("ctx")
    conv_x_t, conv_bc_t, proj_dt_t = conv_x.T, conv_bc.T, proj_dt.T
    bias, decay, skip, gain = (v[None] for v in (dt_bias, decay_rate, skip_gain, norm_gain))

    kb = depth // 8
    parts = depth // kb
    edge_rows = (1 + chunks * blocks) * HALO
    msg_first, edge_first = call(
        functools.partial(first_kernel, chunks=chunks, kb=kb),
        (tokens, proj_x, proj_bc, proj_dt_t),
        [IN_HBM] * 4,
        [sds(toks + heads + blocks * toks, lanes), sds((1 + blocks) * HALO, lanes)],
        [
            pltpu.VMEM((toks, depth), bf16),
            pltpu.VMEM((depth, width), bf16),
            pltpu.VMEM((depth, lanes), bf16),
            pltpu.VMEM((heads, depth), bf16),
            pltpu.VMEM((toks, width), f32),
            pltpu.VMEM((toks, lanes), f32),
            pltpu.VMEM((heads, toks), f32),
            pltpu.SemaphoreType.DMA((4 * parts,)),
        ],
        name="first",
        mib=53.9,
    )
    first_got = swapped(msg_first, "row", 1)
    msg_second, x_mine, edge_other, edge_own = call(
        functools.partial(second_kernel, chunks=chunks, kb=kb),
        (tokens, proj_x, edge_first),
        [IN_HBM] * 3,
        [sds(blocks * toks, lanes), sds(chunks * blocks * toks, lanes), *[sds(edge_rows, lanes)] * 2],
        [
            pltpu.VMEM(edge_first.shape, bf16),
            pltpu.VMEM((toks, depth), bf16),
            pltpu.VMEM((depth, width + half), bf16),
            pltpu.VMEM((toks, width + half), f32),
            pltpu.SemaphoreType.DMA((3 * parts + 1,)),
        ],
        name="second",
        mib=52,
    )
    second_got = swapped(msg_second, "row", 1)
    down = [(i, (i + 1) % ctx_size) for i in range(ctx_size)]
    edge_a = lax.ppermute(
        edge_other, ("ctx", "row"), [(2 * i + s, 2 * j + 1 - s) for i, j in down for s in range(2)]
    )
    edge_b = lax.ppermute(edge_own, "ctx", down)
    *z_send, tok_held = call(
        functools.partial(gate_product_kernel, kb=kb),
        (tokens, proj_z),
        [IN_HBM] * 2,
        [*[sds(blocks * toks, lanes)] * chunks, sds(toks, depth)],
        [
            pltpu.VMEM((depth, half), bf16),
            pltpu.VMEM((toks, half), f32),
            pltpu.SemaphoreType.DMA((2 * parts,)),
        ],
        name="z_other",
        mib=50,
        after=(edge_own,),
    )

    sizes = dict(head_dim=head_dim, state_dim=state_dim, lanes=lanes)
    states, scans = [], []
    bc_now = None
    for c in range(chunks):
        args = [] if c == 0 else [bc_now]
        args += [
            msg_first, first_got, x_mine, first_got if c == 0 else second_got, edge_b, edge_a,
            conv_x_t, conv_bc_t, bias, decay,
        ]
        outs = [sds(toks, lanes)] if c == 0 else []
        outs += [
            sds(blocks * state_dim + HALO, lanes),
            sds(chunk_heads, toks, dtype=f32),
            sds(toks, width),
            sds(chunk_heads, toks, dtype=f32),
            sds(toks, chunk_heads, dtype=f32),
        ]
        got = call(
            functools.partial(
                state_kernel, first=c == 0, chunk=c, chunks=chunks, toks=toks, **sizes
            ),
            args,
            None,
            outs,
            [pltpu.VMEM((HALO + toks, lanes), f32)],
            name="state",
            after=(z_send[0],),
        )
        if c == 0:
            bc_now, *got = got
        states.append(got[0])
        scans.append(got[1:])

    z_send, _ = lax.optimization_barrier((z_send, states))
    z_got = [swapped(z, "row", 1) for z in z_send]
    def inner_call(c):
        (inner,) = call(
            functools.partial(inner_kernel, chunk=c, chunks=chunks, head_dim=head_dim),
            (bc_now, skip, *scans[c]),
            None,
            [sds(toks, width, dtype=f32)],
            name="inner",
            after=sent[:1],
        )
        return inner

    messages, sent, inners = [], [], []
    for c in range(chunks):
        if c == 1:
            inners = [inner_call(i) for i in range(chunks)]
        heard = [states[c]]
        send = states[c]
        by = 1
        while by < ctx_size:
            if by > 1:
                (send,) = call(
                    functools.partial(combine_kernel, state_dim=state_dim),
                    heard, None, [sds(*send.shape)], name="combine", after=(*sent, *inners),
                )
            heard.append(swapped(send, "ctx", by))
            by *= 2
        messages.append(heard)
        sent.append(send)
    early = half // 4
    z_mine, w_first = call(
        functools.partial(own_gate_kernel, kb=kb),
        (tok_held, proj_z, proj_out),
        [IN_VMEM, IN_HBM, IN_HBM],
        [sds(chunks * blocks * toks, lanes), sds(early, out_cols)],
        [
            pltpu.VMEM((depth, half), bf16),
            pltpu.VMEM((toks, half), f32),
            pltpu.SemaphoreType.DMA((parts + early // lanes,)),
        ],
        name="z_own",
        mib=38,
        after=(*sent, *inners),
    )

    normed, normed_got = [], []
    bounds = ((0, toks // 2), (toks // 2, toks))
    cuts = [((0, toks),)] * (chunks - 1) + [bounds]
    for c in range(chunks):
        now = call(
            functools.partial(
                gate_kernel, messages=len(messages[c]), bounds=cuts[c], chunk=c, chunks=chunks, **sizes
            ),
            (inners[c], bc_now, scans[c][2], z_mine, z_got[c], gain, *messages[c]),
            None,
            [sds(blocks * (end - start), lanes) for start, end in cuts[c]],
            name="gate",
        )
        normed.append(now)
        normed_got.append([swapped(part, "row", 1) for part in now])

    piece = out_cols // lax.axis_size("col")
    partial, rest = call(
        functools.partial(own_kernel, cuts=cuts),
        (proj_out, w_first, *[part for now in normed[::-1] for part in now]),
        [IN_HBM, *[IN_VMEM] * (1 + sum(len(cut) for cut in cuts))],
        [sds(toks, out_cols, dtype=f32), sds(half, out_cols)],
        [
            pltpu.VMEM((half - early, out_cols), bf16),
            pltpu.VMEM((toks, half), bf16),
            pltpu.SemaphoreType.DMA(((2 * half - early) // lanes,)),
        ],
        name="out_own",
        mib=34,
    )

    def out_rest(part, far, after):
        start, end = bounds[part]
        args = (partial, rest, *[now[min(part, len(now) - 1)] for now in normed_got[::-1]])
        return call(
            functools.partial(rest_kernel, start=start, end=end, far=far),
            args,
            None,
            [sds(end - start, piece)] * 2,
            name="out_far" if far else "out_near",
            after=after,
        )

    def added(a, b):
        return (a.astype(f32) + b.astype(f32)).astype(bf16)

    sends, sums, keep = [], [], None
    for part in range(len(bounds)):
        send, far_keep = out_rest(part, True, () if keep is None else (keep,))
        sums.append(added(far_keep, swapped(send, "col", 1)))
        send, keep = out_rest(part, False, (far_keep,))
        sends.append((send, keep))
    args = []
    for far, (send, keep) in zip(sums, sends):
        args += [swapped(far, "col", 2), keep, swapped(send, "col", 1)]
    (out,) = call(
        functools.partial(final_kernel, bounds=bounds), args, None, [sds(toks, piece)], name="final"
    )
    return out


def shifted(shard, axis, by):
    devices = lax.axis_size(axis)
    pairs = [(i, i + by) for i in range(devices) if 0 <= i + by < devices]
    return lax.ppermute(shard, axis, pairs)


def general(
    tokens,
    proj_x,
    proj_z,
    proj_bc,
    proj_dt,
    dt_bias,
    decay_rate,
    skip_gain,
    conv_x,
    conv_bc,
    norm_gain,
    proj_out,
):
    tok_count = tokens.shape[0]
    col_heads = proj_dt.shape[1]
    head_dim = proj_x.shape[1] // col_heads
    state_dim = proj_bc.shape[1] // 2
    tap_count = conv_bc.shape[1]
    group_count = tok_count // Q
    bc_term = jnp.einsum("dc,td->ct", proj_bc, tokens, preferred_element_type=jnp.float32)
    local_heads = col_heads // lax.axis_size("row")
    first_head = lax.axis_index("row") * local_heads
    x_part = jnp.einsum("dc,td->ct", proj_x, tokens, preferred_element_type=jnp.float32).reshape(
        local_heads * lax.axis_size("row"), head_dim, tok_count
    )
    z_part = jnp.einsum("dc,td->ct", proj_z, tokens, preferred_element_type=jnp.float32).reshape(
        local_heads * lax.axis_size("row"), head_dim, tok_count
    )
    dt_part = jnp.einsum("dc,td->ct", proj_dt, tokens, preferred_element_type=jnp.float32).reshape(
        local_heads * lax.axis_size("row"), 1, tok_count
    )
    head_sum = lax.psum_scatter(
        jnp.concatenate([x_part, z_part, dt_part], axis=1).astype(jnp.bfloat16),
        "row",
        scatter_dimension=0,
        tiled=True,
    )
    bc_sum = lax.psum(bc_term.astype(jnp.bfloat16), "row")
    channels = local_heads * head_dim
    z_in = head_sum[:, head_dim : 2 * head_dim]
    dt_in = head_sum[:, 2 * head_dim]
    flat_in = jnp.concatenate([head_sum[:, :head_dim].reshape(channels, tok_count), bc_sum], axis=0)
    prior = shifted(flat_in[:, tok_count - tap_count + 1 :], "ctx", 1)
    padded = jnp.concatenate([prior, flat_in], axis=1).astype(jnp.float32)
    kernel = jnp.concatenate(
        [lax.dynamic_slice_in_dim(conv_x, first_head * head_dim, channels, 0), conv_bc], axis=0
    )
    running = jnp.zeros(flat_in.shape, jnp.float32)
    for tap_index in range(tap_count):
        running = (
            running
            + kernel[:, tap_index : tap_index + 1] * padded[:, tap_index : tap_index + tok_count]
        )
    conv_out = jax.nn.silu(running)
    x_conv = conv_out[:channels].reshape(local_heads, head_dim, tok_count)
    b_blocks = conv_out[channels : channels + state_dim].reshape(state_dim, group_count, Q)
    c_blocks = conv_out[channels + state_dim :].reshape(state_dim, group_count, Q)
    bias_now = lax.dynamic_slice_in_dim(dt_bias, first_head, local_heads, 0)
    decay_now = lax.dynamic_slice_in_dim(decay_rate, first_head, local_heads, 0)
    skip_now = lax.dynamic_slice_in_dim(skip_gain, first_head, local_heads, 0)
    gain_now = lax.dynamic_slice_in_dim(norm_gain, first_head * head_dim, channels, 0).reshape(
        local_heads, head_dim, 1
    )
    dt_full = jax.nn.softplus(dt_in.astype(jnp.float32) + bias_now[:, None])
    log_decay = -decay_now[:, None] * dt_full
    x_scaled = x_conv * dt_full[:, None, :]
    cum_decay = jnp.cumsum(log_decay.reshape(local_heads, group_count, Q), axis=2)
    x_blocks = x_scaled.reshape(local_heads, head_dim, group_count, Q)
    scores = jnp.einsum("nci,ncj->cij", c_blocks, b_blocks, precision=highest_mode)
    lower_mask = jnp.arange(Q)[:, None] >= jnp.arange(Q)[None, :]
    log_gap = cum_decay[:, :, :, None] - cum_decay[:, :, None, :]
    weights = jnp.where(lower_mask, jnp.exp(jnp.where(lower_mask, log_gap, 0.0)), 0.0)
    inner_out = jnp.einsum(
        "hcij,hpcj->hpci", scores[None] * weights, x_blocks, precision=highest_mode
    )
    tail_weight = jnp.exp(cum_decay[:, :, -1:] - cum_decay)
    group_states = jnp.einsum(
        "hcj,hpcj,ncj->chpn", tail_weight, x_blocks, b_blocks, precision=highest_mode
    )
    group_logs = cum_decay[:, :, -1].T

    def group_step(carried, step_inputs):
        group_log, group_state = step_inputs
        return (jnp.exp(group_log)[:, None, None] * carried + group_state, carried)

    start_state = jnp.zeros((local_heads, head_dim, state_dim), jnp.float32)
    final_state, local_enter = lax.scan(group_step, start_state, (group_logs, group_states))
    device_log = jnp.sum(group_logs, axis=0)
    before_logs = jnp.cumsum(group_logs, axis=0) - group_logs
    log_all, state_all = (
        lax.all_gather(device_log[None].astype(jnp.bfloat16), "ctx", axis=0, tiled=True).astype(
            jnp.float32
        ),
        lax.all_gather(final_state[None].astype(jnp.bfloat16), "ctx", axis=0, tiled=True).astype(
            jnp.float32
        ),
    )
    my_index = lax.axis_index("ctx")
    earlier_mask = (jnp.arange(log_all.shape[0], dtype=jnp.int32) < my_index)[:, None]
    log_prefix = jnp.cumsum(log_all, axis=0)
    up_to_me = jnp.sum(jnp.where(earlier_mask, log_all, 0.0), axis=0)
    reach_weight = jnp.where(
        earlier_mask, jnp.exp(jnp.where(earlier_mask, up_to_me - log_prefix, 0.0)), 0.0
    )
    device_state = jnp.einsum("jh,jhpn->hpn", reach_weight, state_all, precision=highest_mode)
    enter_state = jnp.exp(before_logs)[:, :, None, None] * device_state[None] + local_enter
    outer_out = jnp.exp(cum_decay)[:, None] * jnp.einsum(
        "nci,chpn->hpci", c_blocks, enter_state, precision=highest_mode
    )
    ssm_out = (inner_out + outer_out).reshape(local_heads, head_dim, tok_count) + skip_now[
        :, None, None
    ] * x_conv
    gated = ssm_out * jax.nn.silu(z_in.astype(jnp.float32))
    inv_rms = lax.rsqrt(jnp.mean(gated * gated, axis=1, keepdims=True) + 1e-05)
    normed = (gated * inv_rms * gain_now).astype(jnp.bfloat16)
    out_cols = proj_out.shape[1]
    piece = lax.all_gather(normed, "row", axis=0, tiled=True)
    piece_heads = piece.shape[0]
    rows_now = proj_out.reshape(piece_heads, head_dim, out_cols)
    col_partial = jnp.einsum("hpt,hpd->td", piece, rows_now, preferred_element_type=jnp.float32)
    return lax.psum_scatter(
        col_partial.astype(jnp.bfloat16), "col", scatter_dimension=1, tiled=True
    )


def local(*args):
    tokens, proj_x, _, proj_bc, proj_dt = args[:5]
    toks, heads, lanes = tokens.shape[0], proj_dt.shape[1], proj_bc.shape[1]
    ctx_size = lax.axis_size("ctx")
    fits = (
        lax.axis_size("row") == 2
        and lax.axis_size("col") == 4
        and ctx_size & (ctx_size - 1) == 0
        and toks == Q
        and lanes == toks
        and heads % 32 == 0
        and toks % heads == 0
        and proj_x.shape[1] % (4 * lanes) == 0
        and lanes % (2 * proj_x.shape[1] // heads) == 0
    )
    return fast(*args) if fits else general(*args)


def solution(mesh):
    in_specs = (
        P("ctx", "row"),
        P("row", "col"),
        P("row", "col"),
        P("row", None),
        P("row", "col"),
        P("col"),
        P("col"),
        P("col"),
        P("col", None),
        P(),
        P("col"),
        P("col", "row"),
    )
    out_specs = P("ctx", ("row", "col"))
    return jax.shard_map(local, mesh=mesh, in_specs=in_specs, out_specs=out_specs, check_vma=False)
```
